32 devices in a mesh: dp: 16 (over z, y, core), ctx: 2 (over x).
Axes of the slice: x: 2, y: 2, z: 4, core: 2. Of those that a mesh axis runs over, the one named last changes fastest.
Arguments:
- patch_in: bfloat16 [32, 1024, 1024], P('dp', 'ctx'), may hold values from -6 to 6
- cls_in: bfloat16 [32, 1024], P('dp'), may hold values from -6 to 6
- d_patch: bfloat16 [32, 1024, 1024], P('dp', 'ctx'), may hold values from -6 to 6
- d_cls: bfloat16 [32, 1024], P('dp'), may hold values from -6 to 6
- image_valid: int32 [32], P('dp'), may hold values 0 or 1
- patch_coords: int32 [1024, 2], P('ctx'), may hold values from 0 to 31
- w_query: bfloat16 [1024, 1024], P(('dp', 'ctx')), may hold values from -0.1875 to 0.1875
- w_key: bfloat16 [1024, 1024], P(('dp', 'ctx')), may hold values from -0.1875 to 0.1875
- w_value: bfloat16 [1024, 1024], P(('dp', 'ctx')), may hold values from -0.1875 to 0.1875
- w_gate: bfloat16 [1024, 2730], P(('dp', 'ctx')), may hold values from -0.1875 to 0.1875
- w_up: bfloat16 [1024, 2730], P(('dp', 'ctx')), may hold values from -0.1875 to 0.1875
- w_out: bfloat16 [1024, 1024], P(None, ('dp', 'ctx')), may hold values from -1 to 1
- w_down: bfloat16 [2730, 1024], P(None, ('dp', 'ctx')), may hold values from -0.109375 to 0.109375
- layer_vectors: bfloat16 [8, 1024], P(None, ('dp', 'ctx')), may hold values from -1.25 to 1.25
- ffn_vectors: bfloat16 [4, 2730], replicated, may hold values from -2 to 2
Outputs:
- patch_out: bfloat16 [32, 1024, 1024], P('dp', 'ctx')
- cls_out: bfloat16 [32, 1024], P('dp')
- patch_grad: bfloat16 [32, 1024, 1024], P('dp', 'ctx')
- cls_grad: bfloat16 [32, 1024], P('dp')
- grad_w_query: float32 [1024, 1024], P(('dp', 'ctx'))
- grad_w_key: float32 [1024, 1024], P(('dp', 'ctx'))
- grad_w_value: float32 [1024, 1024], P(('dp', 'ctx'))
- grad_w_gate: float32 [1024, 2730], P(('dp', 'ctx'))
- grad_w_up: float32 [1024, 2730], P(('dp', 'ctx'))
- grad_w_out: float32 [1024, 1024], P(None, ('dp', 'ctx'))
- grad_w_down: float32 [2730, 1024], P(None, ('dp', 'ctx'))
- grad_layer_vectors: float32 [8, 1024], P(None, ('dp', 'ctx'))
- grad_ffn_vectors: float32 [4, 2730], replicated
The draws below stay inside these ranges and needn't reach their ends.
All inputs are finite; a program needn't handle non-finite values. No bound on the sum of `image_valid` on one device may be relied on, other than what follows from the above.
Results may differ from the reference program's by a relative error of at most 0.015.
Values may be sent and summed in bfloat16 or wider, within the bound.
No kernel may reach another device: no remote copies, remote signals or barrier semaphores. Data moves between devices by JAX's collectives and lax.ppermute only.
A program may use at most 256 MiB of HBM per device.

```python
import jax
import jax.numpy as jnp
from jax import lax

D = 1024
H = 16
HD = 64
FF = 2730
PATCHES = 1024
IMAGES = 32


def draw_layer_vectors(key, part):
    key = jax.random.fold_in(key, 11)
    first_key, second_key = jax.random.split(key)
    spread = jax.random.uniform(first_key, (8, D), jnp.float32, -1.0, 1.0)
    normal = jnp.clip(jax.random.normal(second_key, (8, D), jnp.float32), -4.0, 4.0)
    gain_rows = jnp.logical_or(jnp.arange(8) == 0, jnp.arange(8) == 5)
    return jnp.where(gain_rows[:, None], 1.0 + 0.15 * spread, 0.3 * normal).astype(jnp.bfloat16)


def draw_ffn_vectors(key, part):
    key = jax.random.fold_in(key, 23)
    first_key, second_key = jax.random.split(key)
    spread = jax.random.uniform(first_key, (4, FF), jnp.float32, -1.0, 1.0)
    normal = jnp.clip(jax.random.normal(second_key, (4, FF), jnp.float32), -4.0, 4.0)
    scales = jnp.array([0.5, 0.3, 0.0, 0.3], jnp.float32)
    gain_row = jnp.arange(4) == 2
    return jnp.where(gain_row[:, None], 1.0 + 0.3 * spread, scales[:, None] * normal).astype(jnp.bfloat16)


def place_ends(drawn, rng, low, high):
    longest = drawn.shape.index(max(drawn.shape))
    spots = []
    for shift in (0, 1):
        where = [jax.random.randint(jax.random.fold_in(rng, axis), (), 0, length) for axis, length in enumerate(drawn.shape)]
        where[longest] = (where[longest] + shift) % drawn.shape[longest]
        spots.append(tuple(where))
    return drawn.at[spots[0]].set(low).at[spots[1]].set(high)


def steps_of(rng, shape, pieces, least, high):
    factor_of = 1.0
    for position, shards_of in pieces:
        steps = jax.random.uniform(jax.random.fold_in(jax.random.fold_in(rng, 6), position), (shards_of,), jnp.float32, least / len(pieces), high / len(pieces))
        factor_of = factor_of * jnp.repeat(jnp.exp(steps), shape[position] // shards_of).reshape((-1,) + (1,) * (len(shape) - 1 - position))
    return factor_of


def noise(key, shape, scale, limit, pieces=(), held_as=jnp.bfloat16):
    level = steps_of(key, shape, pieces, -0.22, 0.18) if pieces else 1.0
    entries = jax.random.normal(key, shape, jnp.float32) * scale * level
    return jnp.minimum(jnp.maximum(entries, -limit), limit).astype(held_as)


def setup_inputs(seed: int = 0) -> dict:
    key_list = jax.random.split(jax.random.key(seed), 16)
    return {
        "patch_in": noise(key_list[0], (IMAGES, PATCHES, D), 1.0, 6.0, ((0, 16), (1, 2))),
        "cls_in": noise(key_list[1], (IMAGES, D), 1.0, 6.0, ((0, 16),)),
        "d_patch": noise(key_list[2], (IMAGES, PATCHES, D), 1.0, 6.0, ((0, 16), (1, 2))),
        "d_cls": noise(key_list[3], (IMAGES, D), 1.0, 6.0, ((0, 16),)),
        "image_valid": place_ends((jax.random.randint(key_list[4], (IMAGES,), 0, 8) < 7).astype(jnp.int32), jax.random.fold_in(key_list[4], 1), 0, 1),
        "patch_coords": place_ends(jax.random.randint(key_list[5], (PATCHES, 2), 0, 32), jax.random.fold_in(key_list[5], 1), 0, 31).astype(jnp.int32),
        "w_query": noise(key_list[6], (D, D), D ** -0.5, 0.1875, ((0, 32),)),
        "w_key": noise(key_list[7], (D, D), D ** -0.5, 0.1875, ((0, 32),)),
        "w_value": noise(key_list[8], (D, D), D ** -0.5, 0.1875, ((0, 32),)),
        "w_gate": noise(key_list[9], (D, FF), D ** -0.5, 0.1875, ((0, 32),)),
        "w_up": noise(key_list[10], (D, FF), D ** -0.5, 0.1875, ((0, 32),)),
        "w_out": noise(key_list[11], (D, D), (max(1, D // 32)) ** -0.5, 1.0, ((1, 32),)),
        "w_down": noise(key_list[12], (FF, D), FF ** -0.5, 0.109375, ((1, 32),)),
        "layer_vectors": draw_layer_vectors(jax.random.fold_in(key_list[15], 71), 0),
        "ffn_vectors": draw_ffn_vectors(jax.random.fold_in(key_list[15], 71), 0),
    }


@jax.custom_vjp
def low(v):
    return lax.optimization_barrier(v.astype(jnp.bfloat16)).astype(jnp.float32)

@jax.custom_vjp
def low_back(v):
    return v

def low_keep(v):
    return (low(v), None)

def low_pass(kept, grad):
    return (grad,)

def back_keep(v):
    return (v, None)

def back_low(kept, grad):
    return (low(grad),)
low.defvjp(low_keep, low_pass)
low_back.defvjp(back_keep, back_low)
epsilon = 1e-06

def matmul_high(left, right):
    return jnp.dot(left, right, precision=lax.Precision.HIGHEST, preferred_element_type=jnp.float32)

def layer_norm(values, gain, shift):
    centred = values - lax.optimization_barrier(jnp.mean(values, axis=-1, keepdims=True))
    spread = lax.optimization_barrier(jnp.mean(centred * centred, axis=-1, keepdims=True))
    return centred * lax.rsqrt(spread + epsilon) * gain + shift

def rotary_tables(coords):
    freqs = 10000.0 ** (-jnp.arange(16).astype(jnp.float32) / 16.0)
    along_rows = coords[:, 0:1].astype(jnp.float32) * freqs[None, :]
    along_cols = coords[:, 1:2].astype(jnp.float32) * freqs[None, :]
    angles = jnp.concatenate([along_rows, along_rows, along_cols, along_cols], axis=1)
    cosines = jnp.concatenate([jnp.ones((1, 64), jnp.float32), jnp.cos(angles)], axis=0)
    sines = jnp.concatenate([jnp.zeros((1, 64), jnp.float32), jnp.sin(angles)], axis=0)
    return (cosines, sines)

def rotate(values, cosines, sines):
    swapped = jnp.concatenate([-values[..., 16:32], values[..., 0:16], -values[..., 48:64], values[..., 32:48]], axis=-1)
    return values * cosines[:, None, :] + swapped * sines[:, None, :]

def layer_block(tokens, params, cosines, sines):
    w_query, w_key, w_value, w_gate, w_up, w_out, w_down, vectors, ffn_vec = params
    length = tokens.shape[0]
    normed = low(layer_norm(tokens, vectors[0], vectors[1]))
    queries = low_back(matmul_high(normed, w_query) + vectors[2])
    keys_raw = low_back(matmul_high(normed, w_key))
    values = low_back(low(matmul_high(normed, w_value) + vectors[3]))
    q_rot = low(rotate(queries.reshape(length, H, HD), cosines, sines) * HD ** (-0.5))
    k_rot = low(rotate(keys_raw.reshape(length, H, HD), cosines, sines))
    logit_scores = low_back(jnp.einsum('qhd,khd->hqk', q_rot, k_rot, precision=lax.Precision.HIGHEST))
    shifted = jnp.exp(logit_scores - lax.optimization_barrier(jnp.max(logit_scores, axis=-1, keepdims=True)))
    attn_probs = low(shifted / lax.optimization_barrier(jnp.sum(shifted, axis=-1, keepdims=True)))
    blended_values = jnp.einsum('hqk,khd->qhd', attn_probs, values.reshape(length, H, HD), precision=lax.Precision.HIGHEST)
    attended = low_back(low(blended_values.reshape(length, H * HD)))
    middle = tokens + low_back(matmul_high(attended, w_out) + vectors[4])
    normed_two = low(layer_norm(middle, vectors[5], vectors[6]))
    gate_proj = low_back(matmul_high(normed_two, w_gate) + ffn_vec[0])
    up_proj = low_back(matmul_high(normed_two, w_up) + ffn_vec[1])
    inner_act = low(layer_norm(jax.nn.silu(gate_proj) * up_proj, ffn_vec[2], ffn_vec[3]))
    return middle + low_back(matmul_high(inner_act, w_down) + vectors[7])

def reference(patch_in, cls_in, d_patch, d_cls, image_valid, patch_coords, w_query, w_key, w_value, w_gate, w_up, w_out, w_down, layer_vectors, ffn_vectors):
    params = tuple((weight.astype(jnp.float32) for weight in (w_query, w_key, w_value, w_gate, w_up, w_out, w_down, layer_vectors, ffn_vectors)))
    cosines, sines = rotary_tables(patch_coords)
    keep_mask = image_valid.astype(jnp.float32)
    tokens = jnp.concatenate([cls_in[:, None, :], patch_in], axis=1).astype(jnp.float32)
    cotangent = jnp.concatenate([d_cls[:, None, :], d_patch], axis=1).astype(jnp.float32) * keep_mask[:, None, None]

    def image_step(totals, item):
        image_rows, image_cot, image_keep = item
        result, pullback = jax.vjp(lambda rows, weights: layer_block(rows, weights, cosines, sines), image_rows, params)
        row_grad, weight_grads = pullback(image_cot)
        totals = jax.tree.map(lambda first, second: first + second, totals, weight_grads)
        return (totals, (result * image_keep, row_grad))
    totals, (results, row_grads) = lax.scan(image_step, jax.tree.map(jnp.zeros_like, params), (tokens, cotangent, keep_mask))
    return (results[:, 1:].astype(jnp.bfloat16), results[:, 0].astype(jnp.bfloat16), row_grads[:, 1:].astype(jnp.bfloat16), row_grads[:, 0].astype(jnp.bfloat16), totals[0], totals[1], totals[2], totals[3], totals[4], totals[5], totals[6], totals[7], totals[8])
```

```python
import functools
import math

import jax
import jax.numpy as jnp
from jax import lax
from jax.experimental import pallas as pl
from jax.experimental.pallas import tpu as pltpu
from jax.sharding import PartitionSpec as P

HD = 64
MICRO = 2


epsilon = 1e-06


def layer_norm(values, gain, shift):
    centred = values - jnp.mean(values, axis=-1, keepdims=True)
    inv_std = lax.rsqrt(jnp.mean(centred * centred, axis=-1, keepdims=True) + epsilon)
    unit_rows = centred * inv_std
    return (unit_rows * gain + shift, unit_rows, inv_std)


def norm_back(grad_out, gain, unit_rows, inv_std, row_mask):
    scaled = grad_out * gain
    grad_in = inv_std * (
        scaled
        - jnp.mean(scaled, axis=-1, keepdims=True)
        - unit_rows * jnp.mean(scaled * unit_rows, axis=-1, keepdims=True)
    )
    weighted = grad_out * row_mask
    return (grad_in, jnp.sum(weighted * unit_rows, axis=(0, 1)), jnp.sum(weighted, axis=(0, 1)))


def rotary_tables(coords):
    freqs = 10000.0 ** (-jnp.arange(16).astype(jnp.float32) / 16.0)
    along_rows = coords[:, 0:1].astype(jnp.float32) * freqs[None, :]
    along_cols = coords[:, 1:2].astype(jnp.float32) * freqs[None, :]
    angles = jnp.concatenate([along_rows, along_rows, along_cols, along_cols], axis=1)
    cosines = jnp.concatenate([jnp.ones((1, 64), jnp.float32), jnp.cos(angles)], axis=0)
    sines = jnp.concatenate([jnp.zeros((1, 64), jnp.float32), jnp.sin(angles)], axis=0)
    return (cosines, sines)


def rotate(values, cosines, sines):
    swapped = jnp.concatenate(
        [-values[..., 16:32], values[..., 0:16], -values[..., 48:64], values[..., 32:48]], axis=-1
    )
    return values * cosines[:, None, :] + swapped * sines[:, None, :]


def unrotate(grads, cosines, sines):
    with_sin = grads * sines[:, None, :]
    moved = jnp.concatenate(
        [with_sin[..., 16:32], -with_sin[..., 0:16], with_sin[..., 48:64], -with_sin[..., 32:48]],
        axis=-1,
    )
    return grads * cosines[:, None, :] + moved


def project(rows_in, weight):
    return jnp.einsum("brd,de->bre", rows_in, weight, preferred_element_type=jnp.float32)


def project_back(grads, weight):
    return jnp.einsum("bre,de->brd", grads, weight, preferred_element_type=jnp.float32)


def weight_grad(rows_in, grads):
    return jnp.einsum("brd,bre->de", rows_in, grads, preferred_element_type=jnp.float32)


def fetch_forward(w_query, w_key, w_value, w_gate, w_up, w_out, w_down, layer_vectors):
    first_group = (
        lax.all_gather(w_query, ("dp", "ctx"), axis=0, tiled=True),
        lax.all_gather(w_key, ("dp", "ctx"), axis=0, tiled=True),
        lax.all_gather(w_value, ("dp", "ctx"), axis=0, tiled=True),
        lax.all_gather(w_gate, ("dp", "ctx"), axis=0, tiled=True),
        lax.all_gather(w_up, ("dp", "ctx"), axis=0, tiled=True),
    )
    second_group = (
        lax.all_gather(w_out, ("dp", "ctx"), axis=1, tiled=True),
        lax.all_gather(w_down, ("dp", "ctx"), axis=1, tiled=True),
        lax.all_gather(layer_vectors, ("dp", "ctx"), axis=1, tiled=True),
    )
    return tuple(first_group) + tuple(second_group)


def fetch_backward(w_query, w_key, w_value, w_gate, w_up, w_out, w_down, layer_vectors):
    first_group = (
        lax.all_gather(w_query, ("dp", "ctx"), axis=0, tiled=True),
        lax.all_gather(w_key, ("dp", "ctx"), axis=0, tiled=True),
        lax.all_gather(w_value, ("dp", "ctx"), axis=0, tiled=True),
        lax.all_gather(w_gate, ("dp", "ctx"), axis=0, tiled=True),
        lax.all_gather(w_up, ("dp", "ctx"), axis=0, tiled=True),
    )
    second_group = (
        lax.all_gather(w_out, ("dp", "ctx"), axis=1, tiled=True),
        lax.all_gather(w_down, ("dp", "ctx"), axis=1, tiled=True),
        lax.all_gather(layer_vectors, ("dp", "ctx"), axis=1, tiled=True),
    )
    return tuple(first_group) + tuple(second_group)


def head_forward(item):
    block_of_queries, block_of_keys, block_of_values = item
    logit_scores = jnp.einsum(
        "wey,wmy->wem", block_of_queries, block_of_keys, preferred_element_type=jnp.float32
    )
    row_peak = jnp.max(logit_scores, axis=-1, keepdims=True)
    shifted = jnp.exp(logit_scores - row_peak)
    denominator = jnp.sum(shifted, axis=-1, keepdims=True)
    reduced_probabilities = (shifted / denominator).astype(jnp.bfloat16)
    blended_values = jnp.einsum(
        "sce,sem->scm", reduced_probabilities, block_of_values, preferred_element_type=jnp.float32
    )
    return (blended_values, (row_peak + jnp.log(denominator))[..., 0])


def forward_pass(tokens, weights, ffn_vec, cosines, sines):
    w_query, w_key, w_value, w_gate, w_up, w_out, w_down, vectors_low = weights
    vectors = vectors_low.astype(jnp.float32)
    batch, row_count, model_width = tokens.shape
    heads = model_width // HD
    normed, unit_one, std_one = layer_norm(tokens, vectors[0], vectors[1])
    normed_low = normed.astype(jnp.bfloat16)
    queries = project(normed_low, w_query) + vectors[2]
    keys_raw = project(normed_low, w_key)
    values_low = (project(normed_low, w_value) + vectors[3]).astype(jnp.bfloat16)
    q_rot = (
        rotate(queries.reshape(batch, row_count, heads, HD), cosines, sines) * HD ** (-0.5)
    ).astype(jnp.bfloat16)
    k_flat = (
        rotate(keys_raw.reshape(batch, row_count, heads, HD), cosines, sines)
        .astype(jnp.bfloat16)
        .reshape(batch, row_count, model_width)
    )
    far_keys, far_values = (
        lax.all_gather(k_flat[:, 1:], "ctx", axis=1, tiled=True),
        lax.all_gather(values_low[:, 1:], "ctx", axis=1, tiled=True),
    )
    all_keys = jnp.concatenate([k_flat[:, :1], far_keys], axis=1)
    all_values = jnp.concatenate([values_low[:, :1], far_values], axis=1)
    length = all_keys.shape[1]
    head_queries = q_rot.transpose(2, 0, 1, 3)
    head_keys = all_keys.reshape(batch, length, heads, HD).transpose(2, 0, 1, 3)
    head_values = all_values.reshape(batch, length, heads, HD).transpose(2, 0, 1, 3)
    head_out, log_sums = lax.map(head_forward, (head_queries, head_keys, head_values))
    attended = (
        head_out.transpose(1, 2, 0, 3).reshape(batch, row_count, model_width).astype(jnp.bfloat16)
    )
    middle = tokens + (project(attended, w_out) + vectors[4])
    normed_two, unit_two, std_two = layer_norm(middle, vectors[5], vectors[6])
    normed_two_low = normed_two.astype(jnp.bfloat16)
    gate_proj = project(normed_two_low, w_gate) + ffn_vec[0]
    up_proj = project(normed_two_low, w_up) + ffn_vec[1]
    activated = jax.nn.silu(gate_proj)
    inner_act, unit_three, std_three = layer_norm(activated * up_proj, ffn_vec[2], ffn_vec[3])
    inner_low = inner_act.astype(jnp.bfloat16)
    result = middle + (project(inner_low, w_down) + vectors[7])
    saved = (
        normed_low,
        unit_one,
        std_one,
        head_queries,
        head_keys,
        head_values,
        log_sums,
        attended,
        unit_two,
        std_two,
        normed_two_low,
        gate_proj,
        up_proj,
        activated,
        unit_three,
        std_three,
        inner_low,
    )
    return (result, saved)


def backward_pass(grad_rows, weights, ffn_vec, cosines, sines, saved, row_mask):
    w_query, w_key, w_value, w_gate, w_up, w_out, w_down, vectors_low = weights
    vectors = vectors_low.astype(jnp.float32)
    (
        normed_low,
        unit_one,
        std_one,
        head_queries,
        head_keys,
        head_values,
        log_sums,
        attended,
        unit_two,
        std_two,
        normed_two_low,
        gate_proj,
        up_proj,
        activated,
        unit_three,
        std_three,
        inner_low,
    ) = saved
    batch, row_count, model_width = grad_rows.shape
    heads = model_width // HD
    reduced_mask = row_mask.astype(jnp.bfloat16)
    branch_low = grad_rows.astype(jnp.bfloat16)
    grad_down = weight_grad(inner_low, branch_low * reduced_mask)
    grad_inner = project_back(branch_low, w_down)
    grad_mix, gain_three, shift_three = norm_back(
        grad_inner, ffn_vec[2], unit_three, std_three, row_mask
    )
    sigmoid_gate = jax.nn.sigmoid(gate_proj)
    gate_low = (
        grad_mix * up_proj * sigmoid_gate * (1.0 + gate_proj * (1.0 - sigmoid_gate))
    ).astype(jnp.bfloat16)
    up_low = (grad_mix * activated).astype(jnp.bfloat16)
    grad_gate_w = weight_grad(normed_two_low * reduced_mask, gate_low)
    grad_up_w = weight_grad(normed_two_low * reduced_mask, up_low)
    grad_normed_two = project_back(gate_low, w_gate) + project_back(up_low, w_up)
    grad_mid_norm, gain_two, shift_two = norm_back(
        grad_normed_two, vectors[5], unit_two, std_two, row_mask
    )
    grad_middle = grad_rows + grad_mid_norm
    out_low = grad_middle.astype(jnp.bfloat16)
    grad_out_w = weight_grad(attended * reduced_mask, out_low)
    attended_grad = project_back(out_low, w_out).astype(jnp.bfloat16)
    head_grads = attended_grad.reshape(batch, row_count, heads, HD).transpose(2, 0, 1, 3)

    def head_backward(item):
        block_of_queries, block_of_keys, block_of_values, block_gradient, log_block = item
        logit_scores = jnp.einsum(
            "wey,wmy->wem", block_of_queries, block_of_keys, preferred_element_type=jnp.float32
        )
        attn_probs = jnp.exp(logit_scores - log_block[..., None])
        grad_probs = jnp.einsum(
            "wey,wmy->wem", block_gradient, block_of_values, preferred_element_type=jnp.float32
        )
        inner_sum = jnp.sum(attn_probs * grad_probs, axis=-1, keepdims=True)
        score_gradients = (attn_probs * (grad_probs - inner_sum)).astype(jnp.bfloat16)
        grad_query = jnp.einsum(
            "sce,sem->scm", score_gradients, block_of_keys, preferred_element_type=jnp.float32
        )
        grad_key = jnp.einsum(
            "ipz,iph->izh",
            score_gradients * reduced_mask,
            block_of_queries,
            preferred_element_type=jnp.float32,
        )
        grad_value = jnp.einsum(
            "ipz,iph->izh",
            attn_probs.astype(jnp.bfloat16) * reduced_mask,
            block_gradient,
            preferred_element_type=jnp.float32,
        )
        return (grad_query, grad_key, grad_value)

    grad_q_heads, grad_k_heads, grad_v_heads = lax.map(
        head_backward, (head_queries, head_keys, head_values, head_grads, log_sums)
    )
    length = head_keys.shape[2]
    grad_keys = grad_k_heads.transpose(1, 2, 0, 3).reshape(batch, length, model_width)
    grad_values = grad_v_heads.transpose(1, 2, 0, 3).reshape(batch, length, model_width)
    own_keys, own_values = (
        lax.psum_scatter(
            grad_keys[:, 1:].astype(jnp.bfloat16), "ctx", scatter_dimension=1, tiled=True
        ).astype(jnp.float32),
        lax.psum_scatter(
            grad_values[:, 1:].astype(jnp.bfloat16), "ctx", scatter_dimension=1, tiled=True
        ).astype(jnp.float32),
    )
    class_keys, class_values = lax.psum((grad_keys[:, :1], grad_values[:, :1]), "ctx")
    key_rows = jnp.concatenate([class_keys, own_keys], axis=1).reshape(batch, row_count, heads, HD)
    value_rows = jnp.concatenate([class_values, own_values], axis=1)
    key_low = (
        unrotate(key_rows, cosines, sines)
        .reshape(batch, row_count, model_width)
        .astype(jnp.bfloat16)
    )
    value_low = value_rows.astype(jnp.bfloat16)
    query_rows = grad_q_heads.transpose(1, 2, 0, 3)
    query_low = (
        (unrotate(query_rows, cosines, sines) * HD ** (-0.5))
        .reshape(batch, row_count, model_width)
        .astype(jnp.bfloat16)
    )
    grad_query_w = weight_grad(normed_low * reduced_mask, query_low)
    grad_key_w = weight_grad(normed_low * reduced_mask, key_low)
    grad_value_w = weight_grad(normed_low * reduced_mask, value_low)
    grad_normed = (
        project_back(query_low, w_query)
        + project_back(key_low, w_key)
        + project_back(value_low, w_value)
    )
    grad_in_norm, gain_one, shift_one = norm_back(
        grad_normed, vectors[0], unit_one, std_one, row_mask
    )
    grad_tokens = grad_middle + grad_in_norm

    def column_sum(rounded):
        return jnp.sum(rounded.astype(jnp.float32) * row_mask, axis=(0, 1))

    vector_grads = jnp.stack(
        [
            gain_one,
            shift_one,
            column_sum(query_low),
            column_sum(value_low),
            column_sum(out_low),
            gain_two,
            shift_two,
            column_sum(branch_low),
        ]
    )
    ffn_grads = jnp.stack([column_sum(gate_low), column_sum(up_low), gain_three, shift_three])
    return (
        grad_tokens,
        (
            (grad_query_w, grad_key_w, grad_value_w, grad_gate_w, grad_up_w),
            (grad_out_w, grad_down, vector_grads),
            ffn_grads,
        ),
    )


def on_device(
    patch_in,
    cls_in,
    d_patch,
    d_cls,
    image_valid,
    patch_coords,
    w_query,
    w_key,
    w_value,
    w_gate,
    w_up,
    w_out,
    w_down,
    layer_vectors,
    ffn_vectors,
):
    images, patch_rows, model_width = patch_in.shape
    group_size = images // MICRO
    cosines, sines = rotary_tables(patch_coords)
    first_flag = (lax.axis_index("ctx") == 0).astype(jnp.float32)
    row_weight = jnp.concatenate([first_flag[None], jnp.ones((patch_rows,), jnp.float32)])
    row_mask = row_weight[None, :, None]
    ffn_vec = ffn_vectors.astype(jnp.float32)
    keep_mask = image_valid.astype(jnp.float32)
    results = []
    totals = None
    for micro_step in range(MICRO):
        first_image = micro_step * group_size
        last_image = first_image + group_size
        tokens = jnp.concatenate(
            [cls_in[first_image:last_image, None, :], patch_in[first_image:last_image]], axis=1
        ).astype(jnp.float32)
        weights = fetch_forward(w_query, w_key, w_value, w_gate, w_up, w_out, w_down, layer_vectors)
        result, saved = forward_pass(tokens, weights, ffn_vec, cosines, sines)
        keep_rows = keep_mask[first_image:last_image][:, None, None]
        grad_rows = (
            jnp.concatenate(
                [d_cls[first_image:last_image, None, :], d_patch[first_image:last_image]], axis=1
            ).astype(jnp.float32)
            * keep_rows
        )
        back_weights = fetch_backward(
            w_query, w_key, w_value, w_gate, w_up, w_out, w_down, layer_vectors
        )
        grad_tokens, weight_grads = backward_pass(
            grad_rows, back_weights, ffn_vec, cosines, sines, saved, row_mask
        )
        if totals is None:
            totals = weight_grads
        else:
            totals = jax.tree.map(lambda first, second: first + second, totals, weight_grads)
        results.append(
            ((result * keep_rows).astype(jnp.bfloat16), grad_tokens.astype(jnp.bfloat16))
        )
    out_rows = jnp.concatenate([entry[0] for entry in results], axis=0)
    grad_out_rows = jnp.concatenate([entry[1] for entry in results], axis=0)
    in_grads, out_grads, ffn_total = totals
    owned_in = (
        lax.psum_scatter(in_grads[0], ("dp", "ctx"), scatter_dimension=0, tiled=True),
        lax.psum_scatter(in_grads[1], ("dp", "ctx"), scatter_dimension=0, tiled=True),
        lax.psum_scatter(in_grads[2], ("dp", "ctx"), scatter_dimension=0, tiled=True),
        lax.psum_scatter(in_grads[3], ("dp", "ctx"), scatter_dimension=0, tiled=True),
        lax.psum_scatter(in_grads[4], ("dp", "ctx"), scatter_dimension=0, tiled=True),
    )
    owned_out = (
        lax.psum_scatter(out_grads[0], ("dp", "ctx"), scatter_dimension=1, tiled=True),
        lax.psum_scatter(out_grads[1], ("dp", "ctx"), scatter_dimension=1, tiled=True),
        lax.psum_scatter(out_grads[2], ("dp", "ctx"), scatter_dimension=1, tiled=True),
    )
    ffn_summed = lax.psum(ffn_total, ("dp", "ctx"))
    return (
        out_rows[:, 1:],
        out_rows[:, 0],
        grad_out_rows[:, 1:],
        grad_out_rows[:, 0],
        owned_in[0],
        owned_in[1],
        owned_in[2],
        owned_in[3],
        owned_in[4],
        owned_out[0],
        owned_out[1],
        owned_out[2],
        ffn_summed,
    )


BOTH = ("dp", "ctx")
BIT_X, BIT_CORE, BIT_Y, BIT_Z0, BIT_Z1 = 1, 2, 4, 8, 16
ROWS = 1040
KEYS = 1024
HEAD_COLS = 256
LOG2E = math.log2(math.e)
F32 = jnp.float32
BF16 = jnp.bfloat16


def swap_over(value, bit):
    count = lax.axis_size(BOTH)
    return lax.ppermute(value, BOTH, [(i, i ^ bit) for i in range(count)])


def joined(*parts, axis=0):
    return jnp.concatenate(parts, axis=axis)


def after(value, *deps):
    return lax.optimization_barrier((value,) + deps)[0]


def dot_nn(a, b):
    return lax.dot_general(a, b, (((1,), (0,)), ((), ())), preferred_element_type=F32)


def dot_nt(a, b):
    return lax.dot_general(a, b, (((1,), (1,)), ((), ())), preferred_element_type=F32)


def dot_tn(a, b):
    return lax.dot_general(a, b, (((0,), (0,)), ((), ())), preferred_element_type=F32)


def gather_columns(local, split, deps):
    z_dep, xy_dep = deps
    part = after(local, *z_dep)
    part = joined(part, swap_over(part, BIT_Z0))
    part = joined(part, swap_over(part, BIT_Z1))
    left, right = after(part[:, :split], *xy_dep), after(part[:, split:], *xy_dep)
    left = joined(left, swap_over(left, BIT_Y))
    right = joined(right, swap_over(right, BIT_X))
    left_far, right_far = swap_over(left, BIT_X), swap_over(right, BIT_Y)
    left = joined(left, left_far)
    right = joined(right[:128], right_far[:128], right[128:], right_far[128:])
    near = joined(left, right, axis=1)
    far = swap_over(near, BIT_CORE)
    return joined(near, far), ((part,), (left_far, right_far))


def add_rounded(a, b):
    return (a.astype(F32) + b.astype(F32)).astype(BF16)


def scatter_columns(keep, send, split):
    total = add_rounded(keep, swap_over(send, BIT_CORE))
    left, right = total[:, :split], total[:, split:].reshape(2, 2, 128, -1)
    left = add_rounded(left[:256], swap_over(left[256:], BIT_X))
    right = add_rounded(right[:, 0], swap_over(right[:, 1], BIT_Y))
    left = add_rounded(left[:128], swap_over(left[128:], BIT_Y))
    right = add_rounded(right[0], swap_over(right[1], BIT_X))
    total = joined(left, right, axis=1)
    total = add_rounded(total[:64], swap_over(total[64:], BIT_Z1))
    return total[:32].astype(F32) + swap_over(total[32:], BIT_Z0).astype(F32)


def sum_small(value):
    for bit in (BIT_CORE, BIT_X, BIT_Y, BIT_Z0, BIT_Z1):
        value = value + swap_over(value, bit)
    return value


def scatter_small(value):
    for rows, bit in ((512, BIT_CORE), (256, BIT_X), (128, BIT_Y), (64, BIT_Z1), (32, BIT_Z0)):
        value = value[:rows] + swap_over(value[rows:], bit)
    return value


def rotate_lanes(x, cosines, sines_up, sines_down):
    width = x.shape[1]
    return x * cosines + pltpu.roll(x, width - 16, 1) * sines_up + pltpu.roll(x, 16, 1) * sines_down


def twice(table):
    return jnp.concatenate([table, table], axis=1)


def attention_kernel(
    x_ref, wq_ref, wk_ref, wv_ref, b_ref, c_ref, s1_ref, s2_ref, q_ref, k_ref, v_ref, o_ref, l_ref, stat_ref, *, step
):
    x = x_ref[...]
    c, s1, s2 = twice(c_ref[...]), twice(s1_ref[...]), twice(s2_ref[...])
    q = dot_nn(x, wq_ref[...]) + b_ref[2:3, :]
    q_ref[...] = (rotate_lanes(q, c, s1, s2) * (LOG2E / 8)).astype(BF16)
    k = dot_nn(x, wk_ref[...])
    k_ref[...] = rotate_lanes(k, c, s1, s2).astype(BF16)
    v_ref[...] = (dot_nn(x, wv_ref[...]) + b_ref[3:4, :]).astype(BF16)
    lane = lax.broadcasted_iota(jnp.int32, (1, 128), 1)
    low_half = lane < 64

    def tile(i, carry):
        rows = pl.ds(pl.multiple_of(i * step, 16), step)
        stats = jnp.zeros((step, 128), F32)
        for pair in range(2):
            cols = slice(pair * 128, pair * 128 + 128)
            q_pair = q_ref[rows, cols]
            k_pair, v_pair = k_ref[0:KEYS, cols], v_ref[0:KEYS, cols]
            k_class = k_ref[KEYS : KEYS + 16, cols].astype(F32)[0:1]
            v_class = v_ref[KEYS : KEYS + 16, cols].astype(F32)[0:1]
            product = q_pair.astype(F32) * k_class
            outs = []
            for h in range(2):
                own = low_half if h == 0 else ~low_half
                scores = dot_nt(jnp.where(own, q_pair, jnp.zeros_like(q_pair)), k_pair)
                class_score = jnp.sum(jnp.where(own, product, 0.0), axis=1, keepdims=True)
                peak = jnp.maximum(jnp.max(scores, axis=1, keepdims=True), class_score)
                p = jnp.exp2(scores - peak)
                class_p = jnp.exp2(class_score - peak)
                total = jnp.sum(p, axis=1, keepdims=True) + class_p
                out = dot_nn(p.astype(BF16), v_pair) + class_p * v_class
                outs.append(out * (1.0 / total))
                stats = jnp.where(lane == pair * 2 + h, peak + jnp.log2(total), stats)
            o_ref[rows, cols] = jnp.where(low_half, outs[0], outs[1]).astype(BF16)
        stat_ref[rows, :] = stats
        return carry

    lax.fori_loop(0, ROWS // step, tile, 0)
    l_ref[...] = stat_ref[...].T[0:8, :]


def attention_forward(x, w, vectors, tables, step=208):
    def block(first):
        return pl.BlockSpec((1024, HEAD_COLS), lambda j: (0, first + j))

    def whole(a):
        return pl.BlockSpec(a.shape, lambda j: (0, 0))

    out = pl.BlockSpec((ROWS, HEAD_COLS), lambda j: (0, j))
    return pl.pallas_call(
        functools.partial(attention_kernel, step=step),
        grid=(4,),
        in_specs=[whole(x), block(0), block(4), block(8), pl.BlockSpec((8, HEAD_COLS), lambda j: (0, j))]
        + [whole(t) for t in tables],
        out_specs=[out] * 4 + [pl.BlockSpec((8, ROWS), lambda j: (j, 0))],
        out_shape=[jax.ShapeDtypeStruct((ROWS, 1024), BF16)] * 4 + [jax.ShapeDtypeStruct((32, ROWS), F32)],
        scratch_shapes=[pltpu.VMEM((ROWS, 128), F32)],
        compiler_params=pltpu.CompilerParams(vmem_limit_bytes=48 << 20),
        cost_estimate=pl.CostEstimate(flops=30_000_000_000, bytes_accessed=20_000_000, transcendentals=17_000_000),
        name="attention_forward",
    )(x, w, w, w, vectors, *tables)


def attention_back_kernel(
    q_ref, k_ref, v_ref, g_ref, o_ref, l_ref, c_ref, s1_ref, s2_ref,
    dq_ref, dk_ref, dv_ref, dq_sum, dk_sum, dv_sum, delta_ref, *, step
):
    lane = lax.broadcasted_iota(jnp.int32, (1, 128), 1)
    low_half = lane < 64
    deltas = jnp.zeros((ROWS, 128), F32)
    for pair in range(2):
        cols = slice(pair * 128, pair * 128 + 128)
        product = g_ref[:, cols].astype(F32) * o_ref[:, cols].astype(F32)
        for h in range(2):
            own = low_half if h == 0 else ~low_half
            delta = jnp.sum(jnp.where(own, product, 0.0), axis=1, keepdims=True)
            deltas = jnp.where(lane == pair * 2 + h, delta, deltas)
    delta_ref[...] = deltas.T[0:8, :]
    real_key = lax.broadcasted_iota(jnp.int32, (ROWS, 1), 0) <= KEYS
    dk_sum[...] = jnp.zeros_like(dk_sum)
    dv_sum[...] = jnp.zeros_like(dv_sum)
    for t in range(KEYS // step):
        rows = pl.ds(t * step, step)
        for pair in range(2):
            cols = slice(pair * 128, pair * 128 + 128)
            q_pair, g_pair = q_ref[rows, cols], g_ref[rows, cols]
            k_pair, v_pair = k_ref[:, cols], v_ref[:, cols]
            dqs, dk, dv = [], None, None
            for h in range(2):
                own = low_half if h == 0 else ~low_half
                head = pair * 2 + h
                q_head = jnp.where(own, q_pair, jnp.zeros_like(q_pair))
                g_head = jnp.where(own, g_pair, jnp.zeros_like(g_pair))
                scores = dot_nt(k_pair, q_head)
                p = jnp.where(real_key, jnp.exp2(scores - l_ref[head : head + 1, rows]), 0.0)
                gp = dot_nt(v_pair, g_head)
                ds = (p * (gp - delta_ref[head : head + 1, rows])).astype(BF16)
                dv_part, dk_part = dot_nn(p.astype(BF16), g_head), dot_nn(ds, q_head)
                dv = dv_part if dv is None else dv + dv_part
                dk = dk_part if dk is None else dk + dk_part
                dqs.append(dot_tn(ds, k_pair))
            dq_sum[rows, cols] = jnp.where(low_half, dqs[0], dqs[1])
            dk_sum[:, cols] += dk
            dv_sum[:, cols] += dv
    q_class = q_ref[KEYS : KEYS + 16, :][0:1].astype(F32)
    g_class = g_ref[KEYS : KEYS + 16, :][0:1].astype(F32)
    shape = (128, HEAD_COLS)
    own = lax.broadcasted_iota(jnp.int32, shape, 0) == lax.broadcasted_iota(jnp.int32, shape, 1) // 64
    q_diag = jnp.where(own, q_class, 0.0).astype(BF16)
    g_diag = jnp.where(own, g_class, 0.0).astype(BF16)
    scores, gp = dot_nt(k_ref[...], q_diag), dot_nt(v_ref[...], g_diag)
    log_class, delta_class = jnp.zeros((1, 128), F32), jnp.zeros((1, 128), F32)
    for head in range(4):
        log_class = jnp.where(lane == head, l_ref[head : head + 1, KEYS : KEYS + 1], log_class)
        delta_class = jnp.where(lane == head, delta_ref[head : head + 1, KEYS : KEYS + 1], delta_class)
    p = jnp.where(real_key & (lane < 4), jnp.exp2(scores - log_class), 0.0)
    ds = (p * (gp - delta_class)).astype(BF16)
    dv_sum[...] += dot_nn(p.astype(BF16), g_diag)
    dk_sum[...] += dot_nn(ds, q_diag)
    dq_class = jnp.sum(jnp.where(own, dot_tn(ds, k_ref[...]), 0.0), axis=0, keepdims=True)
    first = lax.broadcasted_iota(jnp.int32, (16, 1), 0) == 0
    dq_sum[KEYS : KEYS + 16, :] = jnp.where(first, dq_class, 0.0)
    c, s1, s2 = twice(c_ref[...]), twice(s1_ref[...]), twice(s2_ref[...])
    dq_ref[...] = (rotate_lanes(dq_sum[...], c, -s1, -s2) * 0.125).astype(BF16)
    dk_ref[...] = (rotate_lanes(dk_sum[...], c, -s1, -s2) * (1.0 / LOG2E)).astype(BF16)
    dv_ref[...] = dv_sum[...].astype(BF16)


def attention_backward(q, k, v, g, o, log_sums, tables, step=256):
    def whole(a):
        return pl.BlockSpec(a.shape, lambda j: (0, 0))

    block = pl.BlockSpec((ROWS, HEAD_COLS), lambda j: (0, j))
    return pl.pallas_call(
        functools.partial(attention_back_kernel, step=step),
        grid=(4,),
        in_specs=[block] * 5 + [pl.BlockSpec((8, ROWS), lambda j: (j, 0))] + [whole(t) for t in tables],
        out_specs=[block] * 3,
        out_shape=[jax.ShapeDtypeStruct((ROWS, 1024), BF16)] * 3,
        scratch_shapes=[pltpu.VMEM((ROWS, HEAD_COLS), F32)] * 3 + [pltpu.VMEM((8, ROWS), F32)],
        compiler_params=pltpu.CompilerParams(vmem_limit_bytes=48 << 20),
        cost_estimate=pl.CostEstimate(flops=50_000_000_000, bytes_accessed=20_000_000, transcendentals=17_000_000),
        name="attention_backward",
    )(q, k, v, g, o, log_sums, *tables)


def unit_norm(values):
    centred = values - jnp.mean(values, axis=-1, keepdims=True)
    inv_std = lax.rsqrt(jnp.mean(centred * centred, axis=-1, keepdims=True) + epsilon)
    return centred * inv_std, inv_std


def unit_norm_back(scaled, unit, inv_std):
    return inv_std * (
        scaled
        - jnp.mean(scaled, axis=-1, keepdims=True)
        - unit * jnp.mean(scaled * unit, axis=-1, keepdims=True)
    )


def pair_tables(coords):
    cosines, sines = rotary_tables(coords)
    pad = ((0, ROWS - KEYS - 1), (0, 0))
    cosines = jnp.pad(joined(cosines[1:], cosines[:1]), pad)
    sines = jnp.pad(joined(sines[1:], sines[:1]), pad)
    even = (jnp.arange(64) % 32 < 16)[None, :]
    up, down = jnp.where(even, -sines, 0.0), jnp.where(even, 0.0, sines)
    return tuple(jnp.tile(t, (1, 2)) for t in (cosines, up, down))


def paired_device(
    patch_in, cls_in, d_patch, d_cls, image_valid, patch_coords,
    w_query, w_key, w_value, w_gate, w_up, w_out, w_down, layer_vectors, ffn_vectors,
):
    me, pos = lax.axis_index(BOTH), lax.axis_index("ctx")
    hidden = w_gate.shape[1]

    vectors_local = jnp.pad(layer_vectors.T, ((0, 0), (0, 120)))
    first_local = joined(w_query, w_key, w_value, vectors_local, axis=1)
    out_local, down_local = w_out.T, w_down.T
    wide = (hidden + 127) // 128 * 128
    extra = ((0, 0), (0, wide - hidden))
    second_local = joined(
        jnp.pad(w_gate, extra), out_local[:, :512], jnp.pad(w_up, extra), out_local[:, 512:], axis=1
    )
    half_two = wide + 512
    third_split = (hidden // 2 + 127) // 128 * 128
    first, deps = gather_columns(first_local, 1664, ((), ()))
    second, deps = gather_columns(second_local, half_two, deps)
    third, deps = gather_columns(down_local, third_split, deps)
    vectors = first[:, 3072:3080].T.astype(F32)
    gate_w, up_w = second[:, :hidden], second[:, half_two : half_two + hidden]
    out_w = joined(second[:, wide:half_two], second[:, half_two + wide :], axis=1)
    down_w = third
    ffn = ffn_vectors.astype(F32)

    natural = lax.broadcasted_iota(jnp.int32, (1024, 1024), 0)
    place = lax.broadcasted_iota(jnp.int32, (1024, 1024), 1)
    block = place // 32
    owner = (
        (block // 16) * BIT_CORE
        + (block // 8 % 2) * BIT_X
        + (block // 4 % 2) * BIT_Y
        + (block // 2 % 2) * BIT_Z1
        + (block % 2) * BIT_Z0
    ) ^ me
    order = (natural == owner * 32 + place % 32).astype(BF16)

    def own_image(patches, classes):
        near = lax.dynamic_index_in_dim(patches, pos, 0, keepdims=False)
        far = swap_over(lax.dynamic_index_in_dim(patches, 1 - pos, 0, keepdims=False), BIT_X)
        class_row = lax.dynamic_index_in_dim(classes, pos, 0)
        rows = joined(near, far, jnp.pad(class_row, ((0, ROWS - KEYS - 1), (0, 0))))
        return dot_nn(rows, order)

    def to_pair(rows):
        rows = dot_nt(rows, order).astype(BF16)
        near, far = rows[:512], swap_over(rows[512:], BIT_X)
        is_first = pos == 0
        near_class, far_class = rows[KEYS], far[512]
        patches = jnp.where(is_first, jnp.stack([near, far[:512]]), jnp.stack([far[:512], near]))
        classes = jnp.where(is_first, jnp.stack([near_class, far_class]), jnp.stack([far_class, near_class]))
        return patches, classes

    coords = joined(patch_coords, swap_over(patch_coords, BIT_X))
    tables = pair_tables(coords)
    keep = lax.dynamic_index_in_dim(image_valid, pos, 0, keepdims=False).astype(F32)
    tokens = own_image(patch_in, cls_in)
    grad_rows = own_image(d_patch, d_cls) * keep

    unit_one, std_one = unit_norm(tokens)
    normed = (unit_one * vectors[0] + vectors[1]).astype(BF16)
    head_biases = dot_nt(first[:, 3072:3080].T, order)
    q_rot, k_rot, values, attended, log_sums = attention_forward(normed, first, head_biases, tables)
    middle = tokens + (dot_nt(attended, out_w) + vectors[4])
    unit_two, std_two = unit_norm(middle)
    normed_two = (unit_two * vectors[5] + vectors[6]).astype(BF16)
    gate = dot_nn(normed_two, gate_w) + ffn[0]
    up = dot_nn(normed_two, up_w) + ffn[1]
    silu = jax.nn.silu(gate)
    unit_three, std_three = unit_norm(silu * up)
    inner = (unit_three * ffn[2] + ffn[3]).astype(BF16)
    result = middle + (dot_nt(inner, down_w) + vectors[7])
    patch_out, cls_out = to_pair((result * keep).astype(BF16))

    def weight_grad_halves(rows_in, grads):
        near = dot_tn(rows_in[:, :512], grads).astype(BF16)
        far = dot_tn(rows_in[:, 512:], grads).astype(BF16)
        return near, far

    def column_sum(rounded):
        return jnp.sum(rounded.astype(F32), axis=0)

    branch = grad_rows.astype(BF16)
    down_grad = scatter_columns(*weight_grad_halves(branch, inner), third_split)
    grad_inner = dot_nn(branch, down_w)
    grad_mix = unit_norm_back(grad_inner * ffn[2], unit_three, std_three)
    sigmoid = jax.nn.sigmoid(gate)
    gate_low = (grad_mix * up * sigmoid * (1.0 + gate * (1.0 - sigmoid))).astype(BF16)
    up_low = (grad_mix * silu).astype(BF16)
    ffn_grads = sum_small(
        jnp.stack(
            [column_sum(gate_low), column_sum(up_low), jnp.sum(grad_inner * unit_three, axis=0), jnp.sum(grad_inner, axis=0)]
        )
    )
    gate_near, gate_far = weight_grad_halves(normed_two, gate_low)
    up_near, up_far = weight_grad_halves(normed_two, up_low)
    grad_two = dot_nt(gate_low, gate_w) + dot_nt(up_low, up_w)
    grad_middle = grad_rows + unit_norm_back(grad_two * vectors[5], unit_two, std_two)
    att_low = grad_middle.astype(BF16)
    out_near, out_far = weight_grad_halves(att_low, attended)
    pads = ((0, 0), (0, wide - hidden))
    second_grad = scatter_columns(
        joined(jnp.pad(gate_near, pads), out_near[:, :512], jnp.pad(up_near, pads), out_near[:, 512:], axis=1),
        joined(jnp.pad(gate_far, pads), out_far[:, :512], jnp.pad(up_far, pads), out_far[:, 512:], axis=1),
        half_two,
    )
    grad_attended = dot_nn(att_low, out_w).astype(BF16)
    query_low, key_low, value_low = attention_backward(
        q_rot, k_rot, values, grad_attended, attended, log_sums, tables
    )
    halves = [weight_grad_halves(normed, low) for low in (query_low, key_low, value_low)]
    first_grad = scatter_columns(
        joined(*[h[0] for h in halves], axis=1), joined(*[h[1] for h in halves], axis=1), 1536
    )
    grad_one = (
        dot_nt(query_low, first[:, :1024])
        + dot_nt(key_low, first[:, 1024:2048])
        + dot_nt(value_low, first[:, 2048:3072])
    )
    grad_tokens = grad_middle + unit_norm_back(grad_one * vectors[0], unit_one, std_one)
    head_sums = jnp.dot(
        jnp.stack([column_sum(query_low), column_sum(value_low)]),
        order.astype(F32),
        precision=lax.Precision.HIGHEST,
    )
    vector_grads = scatter_small(
        jnp.stack(
            [
                jnp.sum(grad_one * unit_one, axis=0),
                jnp.sum(grad_one, axis=0),
                head_sums[0],
                head_sums[1],
                column_sum(att_low),
                jnp.sum(grad_two * unit_two, axis=0),
                jnp.sum(grad_two, axis=0),
                column_sum(branch),
            ]
        ).T
    )
    patch_grad, cls_grad = to_pair(grad_tokens.astype(BF16))
    return (
        patch_out,
        cls_out,
        patch_grad,
        cls_grad,
        first_grad[:, :1024],
        first_grad[:, 1024:2048],
        first_grad[:, 2048:],
        second_grad[:, :hidden],
        second_grad[:, half_two : half_two + hidden],
        joined(second_grad[:, wide:half_two], second_grad[:, half_two + wide :], axis=1).T,
        down_grad.T,
        vector_grads.T,
        ffn_grads,
    )


def solution(mesh):
    in_specs = (
        P("dp", "ctx", None),
        P("dp", None),
        P("dp", "ctx", None),
        P("dp", None),
        P("dp"),
        P("ctx", None),
        P(("dp", "ctx"), None),
        P(("dp", "ctx"), None),
        P(("dp", "ctx"), None),
        P(("dp", "ctx"), None),
        P(("dp", "ctx"), None),
        P(None, ("dp", "ctx")),
        P(None, ("dp", "ctx")),
        P(None, ("dp", "ctx")),
        P(),
    )
    out_specs = (
        P("dp", "ctx", None),
        P("dp", None),
        P("dp", "ctx", None),
        P("dp", None),
        P(("dp", "ctx"), None),
        P(("dp", "ctx"), None),
        P(("dp", "ctx"), None),
        P(("dp", "ctx"), None),
        P(("dp", "ctx"), None),
        P(None, ("dp", "ctx")),
        P(None, ("dp", "ctx")),
        P(None, ("dp", "ctx")),
        P(),
    )
    sizes = dict(mesh.shape)
    pairs = sizes["dp"] == 16 and sizes["ctx"] == 2
    body = paired_device if pairs else on_device
    return jax.shard_map(
        body, mesh=mesh, in_specs=in_specs, out_specs=out_specs, check_vma=False
    )
```

```python
import functools
import math

import jax
import jax.numpy as jnp
from jax import lax
from jax.experimental import pallas as pl
from jax.experimental.pallas import tpu as pltpu
from jax.sharding import PartitionSpec as P

HD = 64
MICRO = 2


epsilon = 1e-06


def layer_norm(values, gain, shift):
    centred = values - jnp.mean(values, axis=-1, keepdims=True)
    inv_std = lax.rsqrt(jnp.mean(centred * centred, axis=-1, keepdims=True) + epsilon)
    unit_rows = centred * inv_std
    return (unit_rows * gain + shift, unit_rows, inv_std)


def norm_back(grad_out, gain, unit_rows, inv_std, row_mask):
    scaled = grad_out * gain
    grad_in = inv_std * (
        scaled
        - jnp.mean(scaled, axis=-1, keepdims=True)
        - unit_rows * jnp.mean(scaled * unit_rows, axis=-1, keepdims=True)
    )
    weighted = grad_out * row_mask
    return (grad_in, jnp.sum(weighted * unit_rows, axis=(0, 1)), jnp.sum(weighted, axis=(0, 1)))


def rotary_tables(coords):
    freqs = 10000.0 ** (-jnp.arange(16).astype(jnp.float32) / 16.0)
    along_rows = coords[:, 0:1].astype(jnp.float32) * freqs[None, :]
    along_cols = coords[:, 1:2].astype(jnp.float32) * freqs[None, :]
    angles = jnp.concatenate([along_rows, along_rows, along_cols, along_cols], axis=1)
    cosines = jnp.concatenate([jnp.ones((1, 64), jnp.float32), jnp.cos(angles)], axis=0)
    sines = jnp.concatenate([jnp.zeros((1, 64), jnp.float32), jnp.sin(angles)], axis=0)
    return (cosines, sines)


def rotate(values, cosines, sines):
    swapped = jnp.concatenate(
        [-values[..., 16:32], values[..., 0:16], -values[..., 48:64], values[..., 32:48]], axis=-1
    )
    return values * cosines[:, None, :] + swapped * sines[:, None, :]


def unrotate(grads, cosines, sines):
    with_sin = grads * sines[:, None, :]
    moved = jnp.concatenate(
        [with_sin[..., 16:32], -with_sin[..., 0:16], with_sin[..., 48:64], -with_sin[..., 32:48]],
        axis=-1,
    )
    return grads * cosines[:, None, :] + moved


def project(rows_in, weight):
    return jnp.einsum("brd,de->bre", rows_in, weight, preferred_element_type=jnp.float32)


def project_back(grads, weight):
    return jnp.einsum("bre,de->brd", grads, weight, preferred_element_type=jnp.float32)


def weight_grad(rows_in, grads):
    return jnp.einsum("brd,bre->de", rows_in, grads, preferred_element_type=jnp.float32)


def fetch_forward(w_query, w_key, w_value, w_gate, w_up, w_out, w_down, layer_vectors):
    first_group = (
        lax.all_gather(w_query, ("dp", "ctx"), axis=0, tiled=True),
        lax.all_gather(w_key, ("dp", "ctx"), axis=0, tiled=True),
        lax.all_gather(w_value, ("dp", "ctx"), axis=0, tiled=True),
        lax.all_gather(w_gate, ("dp", "ctx"), axis=0, tiled=True),
        lax.all_gather(w_up, ("dp", "ctx"), axis=0, tiled=True),
    )
    second_group = (
        lax.all_gather(w_out, ("dp", "ctx"), axis=1, tiled=True),
        lax.all_gather(w_down, ("dp", "ctx"), axis=1, tiled=True),
        lax.all_gather(layer_vectors, ("dp", "ctx"), axis=1, tiled=True),
    )
    return tuple(first_group) + tuple(second_group)


def fetch_backward(w_query, w_key, w_value, w_gate, w_up, w_out, w_down, layer_vectors):
    first_group = (
        lax.all_gather(w_query, ("dp", "ctx"), axis=0, tiled=True),
        lax.all_gather(w_key, ("dp", "ctx"), axis=0, tiled=True),
        lax.all_gather(w_value, ("dp", "ctx"), axis=0, tiled=True),
        lax.all_gather(w_gate, ("dp", "ctx"), axis=0, tiled=True),
        lax.all_gather(w_up, ("dp", "ctx"), axis=0, tiled=True),
    )
    second_group = (
        lax.all_gather(w_out, ("dp", "ctx"), axis=1, tiled=True),
        lax.all_gather(w_down, ("dp", "ctx"), axis=1, tiled=True),
        lax.all_gather(layer_vectors, ("dp", "ctx"), axis=1, tiled=True),
    )
    return tuple(first_group) + tuple(second_group)


def head_forward(item):
    block_of_queries, block_of_keys, block_of_values = item
    logit_scores = jnp.einsum(
        "wey,wmy->wem", block_of_queries, block_of_keys, preferred_element_type=jnp.float32
    )
    row_peak = jnp.max(logit_scores, axis=-1, keepdims=True)
    shifted = jnp.exp(logit_scores - row_peak)
    denominator = jnp.sum(shifted, axis=-1, keepdims=True)
    reduced_probabilities = (shifted / denominator).astype(jnp.bfloat16)
    blended_values = jnp.einsum(
        "sce,sem->scm", reduced_probabilities, block_of_values, preferred_element_type=jnp.float32
    )
    return (blended_values, (row_peak + jnp.log(denominator))[..., 0])


def forward_pass(tokens, weights, ffn_vec, cosines, sines):
    w_query, w_key, w_value, w_gate, w_up, w_out, w_down, vectors_low = weights
    vectors = vectors_low.astype(jnp.float32)
    batch, row_count, model_width = tokens.shape
    heads = model_width // HD
    normed, unit_one, std_one = layer_norm(tokens, vectors[0], vectors[1])
    normed_low = normed.astype(jnp.bfloat16)
    queries = project(normed_low, w_query) + vectors[2]
    keys_raw = project(normed_low, w_key)
    values_low = (project(normed_low, w_value) + vectors[3]).astype(jnp.bfloat16)
    q_rot = (
        rotate(queries.reshape(batch, row_count, heads, HD), cosines, sines) * HD ** (-0.5)
    ).astype(jnp.bfloat16)
    k_flat = (
        rotate(keys_raw.reshape(batch, row_count, heads, HD), cosines, sines)
        .astype(jnp.bfloat16)
        .reshape(batch, row_count, model_width)
    )
    far_keys, far_values = (
        lax.all_gather(k_flat[:, 1:], "ctx", axis=1, tiled=True),
        lax.all_gather(values_low[:, 1:], "ctx", axis=1, tiled=True),
    )
    all_keys = jnp.concatenate([k_flat[:, :1], far_keys], axis=1)
    all_values = jnp.concatenate([values_low[:, :1], far_values], axis=1)
    length = all_keys.shape[1]
    head_queries = q_rot.transpose(2, 0, 1, 3)
    head_keys = all_keys.reshape(batch, length, heads, HD).transpose(2, 0, 1, 3)
    head_values = all_values.reshape(batch, length, heads, HD).transpose(2, 0, 1, 3)
    head_out, log_sums = lax.map(head_forward, (head_queries, head_keys, head_values))
    attended = (
        head_out.transpose(1, 2, 0, 3).reshape(batch, row_count, model_width).astype(jnp.bfloat16)
    )
    middle = tokens + (project(attended, w_out) + vectors[4])
    normed_two, unit_two, std_two = layer_norm(middle, vectors[5], vectors[6])
    normed_two_low = normed_two.astype(jnp.bfloat16)
    gate_proj = project(normed_two_low, w_gate) + ffn_vec[0]
    up_proj = project(normed_two_low, w_up) + ffn_vec[1]
    activated = jax.nn.silu(gate_proj)
    inner_act, unit_three, std_three = layer_norm(activated * up_proj, ffn_vec[2], ffn_vec[3])
    inner_low = inner_act.astype(jnp.bfloat16)
    result = middle + (project(inner_low, w_down) + vectors[7])
    saved = (
        normed_low,
        unit_one,
        std_one,
        head_queries,
        head_keys,
        head_values,
        log_sums,
        attended,
        unit_two,
        std_two,
        normed_two_low,
        gate_proj,
        up_proj,
        activated,
        unit_three,
        std_three,
        inner_low,
    )
    return (result, saved)


def backward_pass(grad_rows, weights, ffn_vec, cosines, sines, saved, row_mask):
    w_query, w_key, w_value, w_gate, w_up, w_out, w_down, vectors_low = weights
    vectors = vectors_low.astype(jnp.float32)
    (
        normed_low,
        unit_one,
        std_one,
        head_queries,
        head_keys,
        head_values,
        log_sums,
        attended,
        unit_two,
        std_two,
        normed_two_low,
        gate_proj,
        up_proj,
        activated,
        unit_three,
        std_three,
        inner_low,
    ) = saved
    batch, row_count, model_width = grad_rows.shape
    heads = model_width // HD
    reduced_mask = row_mask.astype(jnp.bfloat16)
    branch_low = grad_rows.astype(jnp.bfloat16)
    grad_down = weight_grad(inner_low, branch_low * reduced_mask)
    grad_inner = project_back(branch_low, w_down)
    grad_mix, gain_three, shift_three = norm_back(
        grad_inner, ffn_vec[2], unit_three, std_three, row_mask
    )
    sigmoid_gate = jax.nn.sigmoid(gate_proj)
    gate_low = (
        grad_mix * up_proj * sigmoid_gate * (1.0 + gate_proj * (1.0 - sigmoid_gate))
    ).astype(jnp.bfloat16)
    up_low = (grad_mix * activated).astype(jnp.bfloat16)
    grad_gate_w = weight_grad(normed_two_low * reduced_mask, gate_low)
    grad_up_w = weight_grad(normed_two_low * reduced_mask, up_low)
    grad_normed_two = project_back(gate_low, w_gate) + project_back(up_low, w_up)
    grad_mid_norm, gain_two, shift_two = norm_back(
        grad_normed_two, vectors[5], unit_two, std_two, row_mask
    )
    grad_middle = grad_rows + grad_mid_norm
    out_low = grad_middle.astype(jnp.bfloat16)
    grad_out_w = weight_grad(attended * reduced_mask, out_low)
    attended_grad = project_back(out_low, w_out).astype(jnp.bfloat16)
    head_grads = attended_grad.reshape(batch, row_count, heads, HD).transpose(2, 0, 1, 3)

    def head_backward(item):
        block_of_queries, block_of_keys, block_of_values, block_gradient, log_block = item
        logit_scores = jnp.einsum(
            "wey,wmy->wem", block_of_queries, block_of_keys, preferred_element_type=jnp.float32
        )
        attn_probs = jnp.exp(logit_scores - log_block[..., None])
        grad_probs = jnp.einsum(
            "wey,wmy->wem", block_gradient, block_of_values, preferred_element_type=jnp.float32
        )
        inner_sum = jnp.sum(attn_probs * grad_probs, axis=-1, keepdims=True)
        score_gradients = (attn_probs * (grad_probs - inner_sum)).astype(jnp.bfloat16)
        grad_query = jnp.einsum(
            "sce,sem->scm", score_gradients, block_of_keys, preferred_element_type=jnp.float32
        )
        grad_key = jnp.einsum(
            "ipz,iph->izh",
            score_gradients * reduced_mask,
            block_of_queries,
            preferred_element_type=jnp.float32,
        )
        grad_value = jnp.einsum(
            "ipz,iph->izh",
            attn_probs.astype(jnp.bfloat16) * reduced_mask,
            block_gradient,
            preferred_element_type=jnp.float32,
        )
        return (grad_query, grad_key, grad_value)

    grad_q_heads, grad_k_heads, grad_v_heads = lax.map(
        head_backward, (head_queries, head_keys, head_values, head_grads, log_sums)
    )
    length = head_keys.shape[2]
    grad_keys = grad_k_heads.transpose(1, 2, 0, 3).reshape(batch, length, model_width)
    grad_values = grad_v_heads.transpose(1, 2, 0, 3).reshape(batch, length, model_width)
    own_keys, own_values = (
        lax.psum_scatter(
            grad_keys[:, 1:].astype(jnp.bfloat16), "ctx", scatter_dimension=1, tiled=True
        ).astype(jnp.float32),
        lax.psum_scatter(
            grad_values[:, 1:].astype(jnp.bfloat16), "ctx", scatter_dimension=1, tiled=True
        ).astype(jnp.float32),
    )
    class_keys, class_values = lax.psum((grad_keys[:, :1], grad_values[:, :1]), "ctx")
    key_rows = jnp.concatenate([class_keys, own_keys], axis=1).reshape(batch, row_count, heads, HD)
    value_rows = jnp.concatenate([class_values, own_values], axis=1)
    key_low = (
        unrotate(key_rows, cosines, sines)
        .reshape(batch, row_count, model_width)
        .astype(jnp.bfloat16)
    )
    value_low = value_rows.astype(jnp.bfloat16)
    query_rows = grad_q_heads.transpose(1, 2, 0, 3)
    query_low = (
        (unrotate(query_rows, cosines, sines) * HD ** (-0.5))
        .reshape(batch, row_count, model_width)
        .astype(jnp.bfloat16)
    )
    grad_query_w = weight_grad(normed_low * reduced_mask, query_low)
    grad_key_w = weight_grad(normed_low * reduced_mask, key_low)
    grad_value_w = weight_grad(normed_low * reduced_mask, value_low)
    grad_normed = (
        project_back(query_low, w_query)
        + project_back(key_low, w_key)
        + project_back(value_low, w_value)
    )
    grad_in_norm, gain_one, shift_one = norm_back(
        grad_normed, vectors[0], unit_one, std_one, row_mask
    )
    grad_tokens = grad_middle + grad_in_norm

    def column_sum(rounded):
        return jnp.sum(rounded.astype(jnp.float32) * row_mask, axis=(0, 1))

    vector_grads = jnp.stack(
        [
            gain_one,
            shift_one,
            column_sum(query_low),
            column_sum(value_low),
            column_sum(out_low),
            gain_two,
            shift_two,
            column_sum(branch_low),
        ]
    )
    ffn_grads = jnp.stack([column_sum(gate_low), column_sum(up_low), gain_three, shift_three])
    return (
        grad_tokens,
        (
            (grad_query_w, grad_key_w, grad_value_w, grad_gate_w, grad_up_w),
            (grad_out_w, grad_down, vector_grads),
            ffn_grads,
        ),
    )


def on_device(
    patch_in,
    cls_in,
    d_patch,
    d_cls,
    image_valid,
    patch_coords,
    w_query,
    w_key,
    w_value,
    w_gate,
    w_up,
    w_out,
    w_down,
    layer_vectors,
    ffn_vectors,
):
    images, patch_rows, model_width = patch_in.shape
    group_size = images // MICRO
    cosines, sines = rotary_tables(patch_coords)
    first_flag = (lax.axis_index("ctx") == 0).astype(jnp.float32)
    row_weight = jnp.concatenate([first_flag[None], jnp.ones((patch_rows,), jnp.float32)])
    row_mask = row_weight[None, :, None]
    ffn_vec = ffn_vectors.astype(jnp.float32)
    keep_mask = image_valid.astype(jnp.float32)
    results = []
    totals = None
    for micro_step in range(MICRO):
        first_image = micro_step * group_size
        last_image = first_image + group_size
        tokens = jnp.concatenate(
            [cls_in[first_image:last_image, None, :], patch_in[first_image:last_image]], axis=1
        ).astype(jnp.float32)
        weights = fetch_forward(w_query, w_key, w_value, w_gate, w_up, w_out, w_down, layer_vectors)
        result, saved = forward_pass(tokens, weights, ffn_vec, cosines, sines)
        keep_rows = keep_mask[first_image:last_image][:, None, None]
        grad_rows = (
            jnp.concatenate(
                [d_cls[first_image:last_image, None, :], d_patch[first_image:last_image]], axis=1
            ).astype(jnp.float32)
            * keep_rows
        )
        back_weights = fetch_backward(
            w_query, w_key, w_value, w_gate, w_up, w_out, w_down, layer_vectors
        )
        grad_tokens, weight_grads = backward_pass(
            grad_rows, back_weights, ffn_vec, cosines, sines, saved, row_mask
        )
        if totals is None:
            totals = weight_grads
        else:
            totals = jax.tree.map(lambda first, second: first + second, totals, weight_grads)
        results.append(
            ((result * keep_rows).astype(jnp.bfloat16), grad_tokens.astype(jnp.bfloat16))
        )
    out_rows = jnp.concatenate([entry[0] for entry in results], axis=0)
    grad_out_rows = jnp.concatenate([entry[1] for entry in results], axis=0)
    in_grads, out_grads, ffn_total = totals
    owned_in = (
        lax.psum_scatter(in_grads[0], ("dp", "ctx"), scatter_dimension=0, tiled=True),
        lax.psum_scatter(in_grads[1], ("dp", "ctx"), scatter_dimension=0, tiled=True),
        lax.psum_scatter(in_grads[2], ("dp", "ctx"), scatter_dimension=0, tiled=True),
        lax.psum_scatter(in_grads[3], ("dp", "ctx"), scatter_dimension=0, tiled=True),
        lax.psum_scatter(in_grads[4], ("dp", "ctx"), scatter_dimension=0, tiled=True),
    )
    owned_out = (
        lax.psum_scatter(out_grads[0], ("dp", "ctx"), scatter_dimension=1, tiled=True),
        lax.psum_scatter(out_grads[1], ("dp", "ctx"), scatter_dimension=1, tiled=True),
        lax.psum_scatter(out_grads[2], ("dp", "ctx"), scatter_dimension=1, tiled=True),
    )
    ffn_summed = lax.psum(ffn_total, ("dp", "ctx"))
    return (
        out_rows[:, 1:],
        out_rows[:, 0],
        grad_out_rows[:, 1:],
        grad_out_rows[:, 0],
        owned_in[0],
        owned_in[1],
        owned_in[2],
        owned_in[3],
        owned_in[4],
        owned_out[0],
        owned_out[1],
        owned_out[2],
        ffn_summed,
    )


BOTH = ("dp", "ctx")
BIT_X, BIT_CORE, BIT_Y, BIT_Z0, BIT_Z1 = 1, 2, 4, 8, 16
ROWS = 1040
KEYS = 1024
WIDTH = 1024
HALF = 512
HEAD_COLS = 256
STEP = 208
LOG2E = math.log2(math.e)
COST = 4
F32 = jnp.float32
BF16 = jnp.bfloat16


def swap_over(value, bit):
    count = lax.axis_size(BOTH)
    return lax.ppermute(value, BOTH, [(i, i ^ bit) for i in range(count)])


def joined(*parts, axis=0):
    return jnp.concatenate(parts, axis=axis)


def after(value, *deps):
    return lax.optimization_barrier((value,) + deps)[0]


def dot_nn(a, b):
    return lax.dot_general(a, b, (((1,), (0,)), ((), ())), preferred_element_type=F32)


def dot_nt(a, b):
    return lax.dot_general(a, b, (((1,), (1,)), ((), ())), preferred_element_type=F32)


def dot_tn(a, b):
    return lax.dot_general(a, b, (((0,), (0,)), ((), ())), preferred_element_type=F32)


def cost_of(flops, bytes_accessed, transcendentals):
    return pl.CostEstimate(
        flops=int(COST * flops), bytes_accessed=int(COST * bytes_accessed), transcendentals=int(COST * transcendentals)
    )


def pack_rows(*parts):
    total, columns = sum(p.shape[0] for p in parts), parts[0].shape[1]
    blocks = columns // 128
    steps = next(n for n in (4, 5, 3, 2, 1) if blocks % n == 0)
    tile = columns // steps

    def kernel(*refs):
        out, start = refs[len(parts)], 0
        for ref in refs[: len(parts)]:
            out[start : start + ref.shape[0], :] = ref[...]
            start += ref.shape[0]

    return pl.pallas_call(
        kernel,
        grid=(steps,),
        in_specs=[pl.BlockSpec((p.shape[0], tile), lambda j: (0, j)) for p in parts],
        out_specs=pl.BlockSpec((total, tile), lambda j: (0, j)),
        out_shape=jax.ShapeDtypeStruct((total, columns), parts[0].dtype),
        compiler_params=pltpu.CompilerParams(vmem_limit_bytes=32 << 20),
        cost_estimate=cost_of(flops=0, bytes_accessed=4 * total * columns, transcendentals=0),
        name="pack_rows",
    )(*parts)


class Gather:
    def __init__(self, local):
        self.part = local

    def along_z0(self, *deps):
        part = after(self.part, *deps)
        far = swap_over(part, BIT_Z0)
        self.part = joined(part, far)
        return far

    def along_z1(self, *deps):
        part = after(self.part, *deps)
        far = swap_over(part, BIT_Z1)
        self.part = joined(part, far)
        return far

    def along_xy(self, *deps):
        part = after(self.part, *deps)
        self.over = swap_over(part, BIT_X), swap_over(part, BIT_Y)
        return self.over

    def corners(self, *deps):
        over_x, over_y = after(self.over, *deps)
        self.corner = swap_over(over_y[:64], BIT_X), swap_over(over_x[64:], BIT_Y)
        return self.corner

    def whole(self, *deps):
        parts = after((self.part, self.over, self.corner), *deps)
        self.near = pack_rows(parts[0], parts[1][1], parts[1][0], *parts[2])
        self.far = swap_over(self.near, BIT_CORE)
        return self.near


def rounded_sum(*terms):
    total = terms[0].astype(F32)
    for term in terms[1:]:
        total = total + term.astype(F32)
    return total.astype(BF16)


class Scatter:
    def __init__(self, near, far):
        self.near, self.far = near, far

    def over_core(self, *deps):
        self.total = rounded_sum(self.near, swap_over(after(self.far, *deps), BIT_CORE))
        return self.total

    def corners(self, *deps):
        total = after(self.total, *deps)
        from_x, from_y = swap_over(total[384:448], BIT_X), swap_over(total[448:512], BIT_Y)
        to_y = joined(rounded_sum(total[128:192], from_x), total[192:256])
        to_x = joined(total[256:320], rounded_sum(total[320:384], from_y))
        self.sides = to_x, to_y
        return self.sides

    def over_xy(self, *deps):
        to_x, to_y = after(self.sides, *deps)
        self.total = rounded_sum(self.total[:128], swap_over(to_y, BIT_Y), swap_over(to_x, BIT_X))
        return self.total

    def along_z1(self, *deps):
        total = after(self.total, *deps)
        self.total = rounded_sum(total[:64], swap_over(total[64:], BIT_Z1))
        return self.total

    def along_z0(self, *deps):
        total = after(self.total, *deps)
        return total[:32].astype(F32) + swap_over(total[32:], BIT_Z0).astype(F32)


def sum_over(value, bit, *deps):
    value = after(value, *deps)
    return value + swap_over(value, bit)


def scatter_small(value):
    for rows, bit in ((512, BIT_CORE), (256, BIT_X), (128, BIT_Y), (64, BIT_Z1), (32, BIT_Z0)):
        value = value[:rows] + swap_over(value[rows:], bit)
    return value


def rotate_lanes(x, cosines, sines_up, sines_down):
    width = x.shape[1]
    return x * cosines + pltpu.roll(x, width - 16, 1) * sines_up + pltpu.roll(x, 16, 1) * sines_down


def twice(table):
    return jnp.concatenate([table, table], axis=1)


def attention_kernel(
    x_ref, qn_ref, qf_ref, kn_ref, kf_ref, vn_ref, vf_ref, b_ref, c_ref, s1_ref, s2_ref,
    q_ref, k_ref, v_ref, o_ref, l_ref, stat_ref, *, step
):
    def project(near_ref, far_ref):
        return dot_nn(x_ref[:, :HALF], near_ref[...]) + dot_nn(x_ref[:, HALF:], far_ref[...])

    c, s1, s2 = twice(c_ref[...]), twice(s1_ref[...]), twice(s2_ref[...])
    q = project(qn_ref, qf_ref) + b_ref[2:3, :]
    q_ref[...] = (rotate_lanes(q, c, s1, s2) * (LOG2E / 8)).astype(BF16)
    k_ref[...] = rotate_lanes(project(kn_ref, kf_ref), c, s1, s2).astype(BF16)
    v_ref[...] = (project(vn_ref, vf_ref) + b_ref[3:4, :]).astype(BF16)
    lane = lax.broadcasted_iota(jnp.int32, (1, 128), 1)
    low_half = lane < 64

    def tile(i, carry):
        rows = pl.ds(pl.multiple_of(i * step, 16), step)
        stats = jnp.zeros((step, 128), F32)
        for pair in range(2):
            cols = slice(pair * 128, pair * 128 + 128)
            q_pair = q_ref[rows, cols]
            k_pair, v_pair = k_ref[0:KEYS, cols], v_ref[0:KEYS, cols]
            k_class = k_ref[KEYS : KEYS + 16, cols].astype(F32)[0:1]
            v_class = v_ref[KEYS : KEYS + 16, cols].astype(F32)[0:1]
            product = q_pair.astype(F32) * k_class
            outs = []
            for h in range(2):
                own = low_half if h == 0 else ~low_half
                scores = dot_nt(jnp.where(own, q_pair, jnp.zeros_like(q_pair)), k_pair)
                class_score = jnp.sum(jnp.where(own, product, 0.0), axis=1, keepdims=True)
                peak = jnp.maximum(jnp.max(scores, axis=1, keepdims=True), class_score)
                p = jnp.exp2(scores - peak)
                class_p = jnp.exp2(class_score - peak)
                total = jnp.sum(p, axis=1, keepdims=True) + class_p
                out = dot_nn(p.astype(BF16), v_pair) + class_p * v_class
                outs.append(out * (1.0 / total))
                stats = jnp.where(lane == pair * 2 + h, peak + jnp.log2(total), stats)
            o_ref[rows, cols] = jnp.where(low_half, outs[0], outs[1]).astype(BF16)
        stat_ref[rows, :] = stats
        return carry

    lax.fori_loop(0, ROWS // step, tile, 0)
    l_ref[...] = stat_ref[...].T[0:8, :]


def attention_forward(x, near, far, biases, head_block, at, tables, step=STEP):
    def block(index):
        return pl.BlockSpec((HALF, HEAD_COLS), lambda j: (0, index))

    def whole(a):
        return pl.BlockSpec(a.shape, lambda j: (0, 0))

    out = pl.BlockSpec((ROWS, HEAD_COLS), lambda j: (0, 0))
    return pl.pallas_call(
        functools.partial(attention_kernel, step=step),
        grid=(1,),
        in_specs=[whole(x)]
        + [block(at + first) for first in (0, 0, 2, 2, 4, 4)]
        + [pl.BlockSpec((8, HEAD_COLS), lambda j: (0, head_block))]
        + [whole(t) for t in tables],
        out_specs=[out] * 4 + [pl.BlockSpec((8, ROWS), lambda j: (0, 0))],
        out_shape=[jax.ShapeDtypeStruct((ROWS, HEAD_COLS), BF16)] * 4 + [jax.ShapeDtypeStruct((8, ROWS), F32)],
        scratch_shapes=[pltpu.VMEM((ROWS, 128), F32)],
        compiler_params=pltpu.CompilerParams(vmem_limit_bytes=48 << 20),
        cost_estimate=cost_of(flops=7_500_000_000, bytes_accessed=7_000_000, transcendentals=4_300_000),
        name="attention_forward",
    )(x, near, far, near, far, near, far, biases, *tables)


def attention_back_kernel(
    q_ref, k_ref, v_ref, g_ref, o_ref, l_ref, c_ref, s1_ref, s2_ref,
    dq_ref, dk_ref, dv_ref, sum_ref, dq_sum, dk_sum, dv_sum, delta_ref, *, step
):
    lane = lax.broadcasted_iota(jnp.int32, (1, 128), 1)
    low_half = lane < 64
    deltas = jnp.zeros((ROWS, 128), F32)
    for pair in range(2):
        cols = slice(pair * 128, pair * 128 + 128)
        product = g_ref[:, cols].astype(F32) * o_ref[:, cols].astype(F32)
        for h in range(2):
            own = low_half if h == 0 else ~low_half
            delta = jnp.sum(jnp.where(own, product, 0.0), axis=1, keepdims=True)
            deltas = jnp.where(lane == pair * 2 + h, delta, deltas)
    delta_ref[...] = deltas.T[0:8, :]
    real_key = lax.broadcasted_iota(jnp.int32, (ROWS, 1), 0) <= KEYS
    dk_sum[...] = jnp.zeros_like(dk_sum)
    dv_sum[...] = jnp.zeros_like(dv_sum)
    for t in range(KEYS // step):
        rows = pl.ds(t * step, step)
        for pair in range(2):
            cols = slice(pair * 128, pair * 128 + 128)
            q_pair, g_pair = q_ref[rows, cols], g_ref[rows, cols]
            k_pair, v_pair = k_ref[:, cols], v_ref[:, cols]
            dqs, dk, dv = [], None, None
            for h in range(2):
                own = low_half if h == 0 else ~low_half
                head = pair * 2 + h
                q_head = jnp.where(own, q_pair, jnp.zeros_like(q_pair))
                g_head = jnp.where(own, g_pair, jnp.zeros_like(g_pair))
                scores = dot_nt(k_pair, q_head)
                p = jnp.where(real_key, jnp.exp2(scores - l_ref[head : head + 1, rows]), 0.0)
                gp = dot_nt(v_pair, g_head)
                ds = (p * (gp - delta_ref[head : head + 1, rows])).astype(BF16)
                dv_part, dk_part = dot_nn(p.astype(BF16), g_head), dot_nn(ds, q_head)
                dv = dv_part if dv is None else dv + dv_part
                dk = dk_part if dk is None else dk + dk_part
                dqs.append(dot_tn(ds, k_pair))
            dq_sum[rows, cols] = jnp.where(low_half, dqs[0], dqs[1])
            dk_sum[:, cols] += dk
            dv_sum[:, cols] += dv
    q_class = q_ref[KEYS : KEYS + 16, :][0:1].astype(F32)
    g_class = g_ref[KEYS : KEYS + 16, :][0:1].astype(F32)
    shape = (128, HEAD_COLS)
    own = lax.broadcasted_iota(jnp.int32, shape, 0) == lax.broadcasted_iota(jnp.int32, shape, 1) // 64
    q_diag = jnp.where(own, q_class, 0.0).astype(BF16)
    g_diag = jnp.where(own, g_class, 0.0).astype(BF16)
    scores, gp = dot_nt(k_ref[...], q_diag), dot_nt(v_ref[...], g_diag)
    log_class, delta_class = jnp.zeros((1, 128), F32), jnp.zeros((1, 128), F32)
    for head in range(4):
        log_class = jnp.where(lane == head, l_ref[head : head + 1, KEYS : KEYS + 1], log_class)
        delta_class = jnp.where(lane == head, delta_ref[head : head + 1, KEYS : KEYS + 1], delta_class)
    p = jnp.where(real_key & (lane < 4), jnp.exp2(scores - log_class), 0.0)
    ds = (p * (gp - delta_class)).astype(BF16)
    dv_sum[...] += dot_nn(p.astype(BF16), g_diag)
    dk_sum[...] += dot_nn(ds, q_diag)
    dq_class = jnp.sum(jnp.where(own, dot_tn(ds, k_ref[...]), 0.0), axis=0, keepdims=True)
    first = lax.broadcasted_iota(jnp.int32, (16, 1), 0) == 0
    dq_sum[KEYS : KEYS + 16, :] = jnp.where(first, dq_class, 0.0)
    c, s1, s2 = twice(c_ref[...]), twice(s1_ref[...]), twice(s2_ref[...])
    dq = (rotate_lanes(dq_sum[...], c, -s1, -s2) * 0.125).astype(BF16)
    dv = dv_sum[...].astype(BF16)
    dq_ref[...] = dq
    dk_ref[...] = (rotate_lanes(dk_sum[...], c, -s1, -s2) * (1.0 / LOG2E)).astype(BF16)
    dv_ref[...] = dv
    sum_ref[0:1, :] = jnp.sum(dq.astype(F32), axis=0, keepdims=True)
    sum_ref[1:2, :] = jnp.sum(dv.astype(F32), axis=0, keepdims=True)
    sum_ref[2:8, :] = jnp.zeros((6, HEAD_COLS), F32)


def attention_backward(q, k, v, o, log_sums, g, tables, step=256):
    def whole(a):
        return pl.BlockSpec(a.shape, lambda j: (0, 0))

    block = pl.BlockSpec((ROWS, HEAD_COLS), lambda j: (0, 0))
    return pl.pallas_call(
        functools.partial(attention_back_kernel, step=step),
        grid=(1,),
        in_specs=[block] * 5 + [pl.BlockSpec((8, ROWS), lambda j: (0, 0))] + [whole(t) for t in tables],
        out_specs=[block] * 3 + [pl.BlockSpec((8, HEAD_COLS), lambda j: (0, 0))],
        out_shape=[jax.ShapeDtypeStruct((ROWS, HEAD_COLS), BF16)] * 3
        + [jax.ShapeDtypeStruct((8, HEAD_COLS), F32)],
        scratch_shapes=[pltpu.VMEM((ROWS, HEAD_COLS), F32)] * 3 + [pltpu.VMEM((8, ROWS), F32)],
        compiler_params=pltpu.CompilerParams(vmem_limit_bytes=48 << 20),
        cost_estimate=cost_of(
            flops=13_000_000_000, bytes_accessed=5_000_000, transcendentals=4_300_000
        ),
        name="attention_backward",
    )(q, k, v, g, o, log_sums, *tables)


def over_rows(kernel, name, tiled, held, outs, sums=(), flops=0, step=STEP):
    in_specs = [pl.BlockSpec((step, a.shape[1]), lambda i: (i, 0)) for a in tiled]
    held = [h if isinstance(h, tuple) else (h, h.shape, 0) for h in held]
    in_specs += [
        pl.BlockSpec(shape, lambda i, column=column: (0, column), pipeline_mode=pl.Buffered(1))
        for _, shape, column in held
    ]
    held = [h[0] for h in held]
    out_specs = [pl.BlockSpec((step, n), lambda i: (i, 0)) for n, _ in outs]
    out_specs += [pl.BlockSpec((8, n), lambda i: (0, 0)) for n in sums]
    out_shape = [jax.ShapeDtypeStruct((ROWS, n), t) for n, t in outs]
    out_shape += [jax.ShapeDtypeStruct((8, n), F32) for n in sums]
    moved = sum(a.size * a.dtype.itemsize for a in list(tiled) + list(held))
    moved += sum(s.size * s.dtype.itemsize for s in out_shape)
    return pl.pallas_call(
        kernel,
        grid=(ROWS // step,),
        in_specs=in_specs,
        out_specs=out_specs,
        out_shape=out_shape,
        compiler_params=pltpu.CompilerParams(vmem_limit_bytes=56 << 20),
        cost_estimate=cost_of(flops=flops, bytes_accessed=moved, transcendentals=0),
        name=name,
    )(*tiled, *held)


def add_sums(ref, *rows):
    @pl.when(pl.program_id(0) == 0)
    def _():
        ref[...] = jnp.zeros_like(ref)

    for i, value in enumerate(rows):
        ref[i : i + 1, :] += jnp.sum(value, axis=0, keepdims=True)


def unit_norm(values):
    centred = values - jnp.mean(values, axis=-1, keepdims=True)
    inv_std = lax.rsqrt(jnp.mean(centred * centred, axis=-1, keepdims=True) + epsilon)
    return centred * inv_std, inv_std


def unit_norm_back(scaled, unit, inv_std):
    return inv_std * (
        scaled
        - jnp.mean(scaled, axis=-1, keepdims=True)
        - unit * jnp.mean(scaled * unit, axis=-1, keepdims=True)
    )


def vectors_kernel(near_ref, far_ref, order_ref, vec_ref, head_ref):
    rows = jnp.concatenate([near_ref[...].astype(F32).T, far_ref[...].astype(F32).T], axis=1)[0:8]
    vec_ref[...] = rows
    head_ref[...] = dot_nt(rows.astype(BF16), order_ref[...])


def gathered_vectors(near, far, order):
    block = pl.BlockSpec((HALF, 128), lambda j: (0, 3 * HALF // 128))
    out = pl.BlockSpec((8, WIDTH), lambda j: (0, 0))
    return pl.pallas_call(
        vectors_kernel,
        grid=(1,),
        in_specs=[block, block, pl.BlockSpec(order.shape, lambda j: (0, 0))],
        out_specs=[out, out],
        out_shape=[jax.ShapeDtypeStruct((8, WIDTH), F32)] * 2,
        cost_estimate=cost_of(flops=40_000_000, bytes_accessed=2_400_000, transcendentals=0),
        name="vectors",
    )(near, far, order)


def sigmoid_of(x):
    return 0.5 * jnp.tanh(0.5 * x) + 0.5


def start_kernel(rows_ref, order_ref, vec_ref, tokens_ref, normed_ref):
    tokens = dot_nn(rows_ref[...], order_ref[...])
    tokens_ref[...] = tokens.astype(BF16)
    unit, _ = unit_norm(tokens)
    normed_ref[...] = (unit * vec_ref[0:1, :] + vec_ref[1:2, :]).astype(BF16)


def middle_kernel(a0_ref, a1_ref, a2_ref, a3_ref, tokens_ref, na_ref, nb_ref, fa_ref, fb_ref, vec_ref, middle_ref, normed_ref):
    low = jnp.concatenate([a0_ref[...], a1_ref[...]], axis=1)
    high = jnp.concatenate([a2_ref[...], a3_ref[...]], axis=1)
    branch = jnp.concatenate(
        [
            dot_nt(low, na_ref[...]) + dot_nt(high, nb_ref[...]),
            dot_nt(low, fa_ref[...]) + dot_nt(high, fb_ref[...]),
        ],
        axis=1,
    )
    middle = tokens_ref[...].astype(F32) + (branch + vec_ref[4:5, :])
    middle_ref[...] = middle.astype(BF16)
    unit, _ = unit_norm(middle)
    normed_ref[...] = (unit * vec_ref[5:6, :] + vec_ref[6:7, :]).astype(BF16)


def hidden_kernel(x_ref, gn_ref, gf_ref, un_ref, uf_ref, ffn_ref, gate_ref, up_ref, inner_ref, stat_ref, *, hidden):
    near, far = x_ref[:, :HALF], x_ref[:, HALF:]
    gate = dot_nn(near, gn_ref[...]) + dot_nn(far, gf_ref[...]) + ffn_ref[0:1, :]
    up = dot_nn(near, un_ref[...]) + dot_nn(far, uf_ref[...]) + ffn_ref[1:2, :]
    gate_ref[...] = gate.astype(gate_ref.dtype)
    up_ref[...] = up.astype(up_ref.dtype)
    mix = gate * sigmoid_of(gate) * up
    mean = jnp.sum(mix, axis=1, keepdims=True) * (1.0 / hidden)
    real = lax.broadcasted_iota(jnp.int32, (1, mix.shape[1]), 1) < hidden
    centred = jnp.where(real, mix - mean, 0.0)
    inv_std = lax.rsqrt(jnp.sum(centred * centred, axis=1, keepdims=True) * (1.0 / hidden) + epsilon)
    inner_ref[...] = (centred * inv_std * ffn_ref[2:3, :] + ffn_ref[3:4, :]).astype(BF16)
    lane = lax.broadcasted_iota(jnp.int32, (1, 128), 1)
    stat_ref[...] = jnp.where(lane == 0, mean, inv_std)


def result_kernel(inner_ref, middle_ref, near_ref, far_ref, vec_ref, order_ref, keep_ref, out_ref):
    inner = inner_ref[...]
    branch = jnp.concatenate([dot_nt(inner, near_ref[...]), dot_nt(inner, far_ref[...])], axis=1)
    result = middle_ref[...].astype(F32) + (branch + vec_ref[7:8, :])
    rounded = (result * keep_ref[0:1, 0:1]).astype(BF16)
    out_ref[...] = dot_nt(rounded, order_ref[...]).astype(BF16)


def hidden_back_kernel(
    d_ref, gate_ref, up_ref, stat_ref, order_ref, keep_ref, near_ref, far_ref, ffn_ref,
    branch_ref, dgate_ref, dup_ref, wide_ref, sum_ref, *, hidden
):
    branch = (dot_nn(d_ref[...], order_ref[...]) * keep_ref[0:1, 0:1]).astype(BF16)
    branch_ref[...] = branch
    g_inner = dot_nn(branch[:, :HALF], near_ref[...]) + dot_nn(branch[:, HALF:], far_ref[...])
    gate, up = gate_ref[...].astype(F32), up_ref[...].astype(F32)
    sigmoid = sigmoid_of(gate)
    silu = gate * sigmoid
    mean, inv_std = stat_ref[:, 0:1], stat_ref[:, 1:2]
    unit = (silu * up - mean) * inv_std
    g_unit = g_inner * ffn_ref[2:3, :]
    share = 1.0 / hidden
    g_mix = inv_std * (
        g_unit
        - jnp.sum(g_unit, axis=1, keepdims=True) * share
        - unit * (jnp.sum(g_unit * unit, axis=1, keepdims=True) * share)
    )
    d_gate = (g_mix * up * (sigmoid * (1.0 + gate * (1.0 - sigmoid)))).astype(BF16)
    d_up = (g_mix * silu).astype(BF16)
    dgate_ref[...] = d_gate
    dup_ref[...] = d_up
    add_sums(wide_ref, d_gate.astype(F32), d_up.astype(F32), g_inner * unit, g_inner)
    add_sums(sum_ref, branch.astype(F32))


def middle_back_kernel(
    dgate_ref, dup_ref, branch_ref, middle_ref, gn_ref, gf_ref, un_ref, uf_ref, na_ref, nb_ref, fa_ref, fb_ref, vec_ref,
    low_ref, d0_ref, d1_ref, d2_ref, d3_ref, sum_ref
):
    d_gate, d_up = dgate_ref[...], dup_ref[...]
    g_two = jnp.concatenate(
        [
            dot_nt(d_gate, gn_ref[...]) + dot_nt(d_up, un_ref[...]),
            dot_nt(d_gate, gf_ref[...]) + dot_nt(d_up, uf_ref[...]),
        ],
        axis=1,
    )
    unit, inv_std = unit_norm(middle_ref[...].astype(F32))
    g_middle = branch_ref[...].astype(F32) + unit_norm_back(g_two * vec_ref[5:6, :], unit, inv_std)
    low = g_middle.astype(BF16)
    low_ref[...] = low
    near, far = low[:, :HALF], low[:, HALF:]
    d_low = (dot_nn(near, na_ref[...]) + dot_nn(far, fa_ref[...])).astype(BF16)
    d_high = (dot_nn(near, nb_ref[...]) + dot_nn(far, fb_ref[...])).astype(BF16)
    d0_ref[...], d1_ref[...] = d_low[:, :HEAD_COLS], d_low[:, HEAD_COLS:]
    d2_ref[...], d3_ref[...] = d_high[:, :HEAD_COLS], d_high[:, HEAD_COLS:]
    add_sums(sum_ref, low.astype(F32), g_two * unit, g_two)


def last_kernel(*refs):
    grads = refs[:12]
    gmid_ref, tokens_ref, an_ref, af_ref, bn_ref, bf_ref, vec_ref, order_ref, grad_ref, sum_ref = refs[12:]

    def back(low_w, high_w):
        total = 0.0
        for first, w_ref in ((0, low_w), (6, high_w)):
            for i in range(3):
                g = jnp.concatenate([grads[first + i][...], grads[first + 3 + i][...]], axis=1)
                total = total + dot_nt(g, w_ref[:, i * HALF : i * HALF + HALF])
        return total

    g_one = jnp.concatenate([back(an_ref, bn_ref), back(af_ref, bf_ref)], axis=1)
    unit, inv_std = unit_norm(tokens_ref[...].astype(F32))
    grad = gmid_ref[...].astype(F32) + unit_norm_back(g_one * vec_ref[0:1, :], unit, inv_std)
    grad_ref[...] = dot_nt(grad.astype(BF16), order_ref[...]).astype(BF16)
    add_sums(sum_ref, g_one * unit, g_one)


def weight_grads(pairs, tile=HEAD_COLS):
    sources = []
    for x, _ in pairs:
        if not any(x is s for s in sources):
            sources.append(x)
    starts, count = [], 0
    for x, g in pairs:
        starts.append(count)
        count += g.shape[1] // tile
    ends = starts[1:] + [count]

    def kernel(*refs):
        xs, gs = refs[: len(sources)], refs[len(sources) : len(sources) + len(pairs)]
        near_ref, far_ref, turned, last = refs[len(sources) + len(pairs) :]
        j = pl.program_id(0)
        for s, x in enumerate(sources):
            begin = min(a for a, (px, _) in zip(starts, pairs) if px is x)

            @pl.when(j == begin)
            def _(s=s):
                turned[...] = xs[s][0:KEYS, :].T
                last[...] = xs[s][KEYS : KEYS + 16, :].astype(F32).T

        for i in range(len(pairs)):

            @pl.when((j >= starts[i]) & (j < ends[i]))
            def _(i=i):
                main = dot_nn(turned[...], gs[i][0:KEYS, :])
                row = gs[i][KEYS : KEYS + 16, :].astype(F32)[0:1]
                out = (main + last[:, 0:1] * row).astype(BF16)
                near_ref[...] = out[:HALF]
                far_ref[...] = out[HALF:]

    def g_spec(i):
        blocks = ends[i] - starts[i]
        return pl.BlockSpec((ROWS, tile), lambda j: (0, jnp.clip(j - starts[i], 0, blocks - 1)))

    out = pl.BlockSpec((HALF, tile), lambda j: (0, j))
    columns = count * tile
    return pl.pallas_call(
        kernel,
        grid=(count,),
        in_specs=[pl.BlockSpec((ROWS, WIDTH), lambda j: (0, 0), pipeline_mode=pl.Buffered(1)) for _ in sources]
        + [g_spec(i) for i in range(len(pairs))],
        out_specs=[out, out],
        out_shape=[jax.ShapeDtypeStruct((HALF, columns), BF16)] * 2,
        scratch_shapes=[pltpu.VMEM((WIDTH, KEYS), BF16), pltpu.VMEM((WIDTH, 16), F32)],
        compiler_params=pltpu.CompilerParams(vmem_limit_bytes=48 << 20),
        cost_estimate=cost_of(
            flops=2 * ROWS * WIDTH * columns, bytes_accessed=4 * ROWS * columns, transcendentals=0
        ),
        name="weight_grads",
    )(*sources, *[g for _, g in pairs])


def pair_tables(coords):
    lane = jnp.arange(128)
    freqs = 10000.0 ** (-(lane % 16).astype(F32) / 16.0)
    along_rows = (lane % 64 < 32)[None, :]
    places = jnp.where(along_rows, coords[:, 0:1], coords[:, 1:2]).astype(F32)
    angles = jnp.pad(places * freqs[None, :], ((0, ROWS - KEYS), (0, 0)))
    cosines, sines = jnp.cos(angles), jnp.sin(angles)
    even = (lane % 32 < 16)[None, :]
    return cosines, jnp.where(even, -sines, 0.0), jnp.where(even, 0.0, sines)


def feature_order(me):
    natural = lax.broadcasted_iota(jnp.int32, (WIDTH, WIDTH), 0)
    place = lax.broadcasted_iota(jnp.int32, (WIDTH, WIDTH), 1)
    block = place // 32
    owner = (
        (block // 16) * BIT_CORE
        + (block // 8 % 2) * BIT_X
        + (block // 4 % 2) * BIT_Y
        + (block // 2 % 2) * BIT_Z1
        + (block % 2) * BIT_Z0
    ) ^ me
    return (natural == owner * 32 + place % 32).astype(BF16)


def paired_device(
    patch_in, cls_in, d_patch, d_cls, image_valid, patch_coords,
    w_query, w_key, w_value, w_gate, w_up, w_out, w_down, layer_vectors, ffn_vectors,
):
    me, pos = lax.axis_index(BOTH), lax.axis_index("ctx")
    hidden = w_gate.shape[1]
    wide = (hidden + 255) // 256 * 256
    extra = ((0, 0), (0, wide - hidden))

    def own_image(patches, classes, *deps):
        near = lax.dynamic_index_in_dim(patches, pos, 0, keepdims=False)
        sent = after(lax.dynamic_index_in_dim(patches, 1 - pos, 0, keepdims=False), *deps)
        far = swap_over(sent, BIT_X)
        class_row = lax.dynamic_index_in_dim(classes, pos, 0)
        return joined(near, far, jnp.pad(class_row, ((0, ROWS - KEYS - 1), (0, 0)))), far

    def to_pair(rows):
        near, far = rows[:512], swap_over(rows[512:], BIT_X)
        is_first = pos == 0
        near_class, far_class = rows[KEYS], far[512]
        patches = jnp.where(is_first, jnp.stack([near, far[:512]]), jnp.stack([far[:512], near]))
        classes = jnp.where(is_first, jnp.stack([near_class, far_class]), jnp.stack([far_class, near_class]))
        return patches, classes

    vectors_local = jnp.pad(layer_vectors.T, ((0, 0), (0, 120)))
    low_heads = [w[:, :HALF] for w in (w_query, w_key, w_value)]
    high_heads = [w[:, HALF:] for w in (w_query, w_key, w_value)]
    g_low = Gather(joined(*low_heads, vectors_local, axis=1))
    g_high = Gather(joined(*high_heads, w_out.T, axis=1))
    g_gate = Gather(jnp.pad(w_gate, extra))
    g_up = Gather(jnp.pad(w_up, extra))
    g_down = Gather(jnp.pad(w_down.T, extra))

    image_rows, image_far = own_image(patch_in, cls_in)
    coords = joined(patch_coords, swap_over(patch_coords, BIT_X))
    order = feature_order(me)
    tables = pair_tables(coords)
    keep = lax.dynamic_index_in_dim(image_valid, pos, 0, keepdims=False).astype(F32)
    keep = jnp.full((8, 128), keep, F32)
    ffn = jnp.pad(ffn_vectors.astype(F32), ((0, 4), (0, wide - hidden)))

    z_one = g_low.along_z0()
    z_low = g_low.along_z1()
    g_high.along_z0(z_one)
    xy_low = g_low.along_xy()
    z_high = g_high.along_z1(z_low)
    corner_low = g_low.corners(image_far)
    z_one = g_gate.along_z0(z_high)
    xy_high = g_high.along_xy(xy_low)
    near_low = g_low.whole()
    z_gate = g_gate.along_z1()

    gate = near_low, g_low.far, image_rows, z_high, z_one
    z_up = g_up.along_z0(gate)
    vectors, head_biases = gathered_vectors(near_low, g_low.far, order)
    tokens, normed = over_rows(
        start_kernel, "start", [after(image_rows, gate)], [order, vectors], [(WIDTH, BF16), (WIDTH, BF16)],
        flops=2_200_000_000,
    )

    def attend(block, gate):
        group = g_low if block < 2 else g_high
        return attention_forward(
            after(normed, gate), group.near, group.far, head_biases, block, block % 2, tables
        )

    gate = normed, xy_high, z_gate, z_up
    corner_high = g_high.corners(gate)
    xy_gate = g_gate.along_xy(gate)
    z_up = g_up.along_z1(gate)
    heads = [attend(0, gate)]

    gate = heads[0][3], corner_high, xy_gate, z_up
    near_high = g_high.whole(gate)
    corner_gate = g_gate.corners(gate)
    xy_up = g_up.along_xy(gate)
    z_down = g_down.along_z0(gate)
    heads.append(attend(1, gate))

    gate = heads[1][3], g_high.far, corner_gate, z_down
    near_gate = g_gate.whole(gate)
    z_down = g_down.along_z1(gate)
    heads.append(attend(2, gate))

    gate = heads[2][3], xy_up, g_gate.far, z_down
    corner_up = g_up.corners(gate)
    xy_down = g_down.along_xy(gate)
    heads.append(attend(3, gate))

    gate = heads[3][3], corner_up
    near_up = g_up.whole(gate)
    out_w = [((w, (HALF, HALF), 3 + i)) for w in (near_high, g_high.far) for i in range(2)]
    attended = [h[3] for h in heads]
    middle, normed_two = over_rows(
        middle_kernel, "middle", attended + [after(tokens, gate)], out_w + [vectors],
        [(WIDTH, BF16), (WIDTH, BF16)], flops=2_200_000_000, step=520,
    )

    gate = normed_two, g_up.far, xy_down
    corner_down = g_down.corners(gate)
    grad_image_rows, grad_far = own_image(d_patch, d_cls, gate)
    gate_up = [near_gate, g_gate.far, near_up, g_up.far]
    gate_act, up_act, inner, stats = over_rows(
        functools.partial(hidden_kernel, hidden=hidden), "hidden", [after(normed_two, gate)],
        gate_up + [ffn], [(wide, BF16), (wide, BF16), (wide, BF16), (128, F32)], flops=12_000_000_000,
    )

    gate = inner, corner_down, grad_far
    near_down = g_down.whole(gate)
    down_w = [near_down, g_down.far]

    branch, d_gate, d_up, wide_sums, branch_sums = over_rows(
        functools.partial(hidden_back_kernel, hidden=hidden), "hidden_back",
        [after(grad_image_rows, gate), gate_act, up_act, stats], [order, keep] + down_w + [ffn],
        [(WIDTH, BF16), (wide, BF16), (wide, BF16)], [wide, WIDTH], flops=8_000_000_000,
    )

    ffn_sums = sum_over(wide_sums[:4, :hidden], BIT_CORE)
    down_grads = weight_grads([(branch, inner)])
    down = Scatter(*down_grads)

    gate = down_grads, ffn_sums
    down_stage = down.over_core(gate)
    ffn_sums = sum_over(ffn_sums, BIT_X, gate)
    (out_rows,) = over_rows(
        result_kernel, "result", [inner, after(middle, gate)], down_w + [vectors, order, keep],
        [(WIDTH, BF16)], flops=8_000_000_000, step=520,
    )

    gate = out_rows, down_stage, ffn_sums
    down_stage = down.corners(gate)
    ffn_sums = sum_over(ffn_sums, BIT_Y, gate)
    outs = to_pair(after(out_rows, gate))
    late = after(normed_two, gate)
    second_grads = weight_grads([(late, d_gate), (late, d_up)])
    second = Scatter(*second_grads)

    gate = second_grads, down_stage, ffn_sums, outs
    down_stage, second_stage = down.over_xy(gate), second.over_core(gate)
    ffn_sums = sum_over(ffn_sums, BIT_Z0, gate)
    att_low, *att_grads, middle_sums = over_rows(
        middle_back_kernel, "middle_back", [d_gate, d_up, branch, after(middle, gate)],
        gate_up + out_w + [vectors], [(WIDTH, BF16)] + [(HEAD_COLS, BF16)] * 4, [WIDTH],
        flops=14_000_000_000, step=520,
    )

    def attend_back(block, gate):
        return attention_backward(*heads[block], after(att_grads[block], gate), tables)

    gate = att_low, down_stage, second_stage, ffn_sums
    down_stage, second_stage = down.along_z1(gate), second.corners(gate)
    ffn_grads = sum_over(ffn_sums, BIT_Z1, gate)
    parts = [attend_back(0, gate)]

    gate = parts[0][0], down_stage, second_stage, ffn_grads
    down_grad, second_stage = down.along_z0(gate), second.over_xy(gate)
    parts.append(attend_back(1, gate))

    gate = parts[1][0], down_grad
    parts.append(attend_back(2, gate))

    gate = parts[2][0], second_stage
    second_stage = second.along_z1(gate)
    late, late_two = after(att_low, gate), after(normed, gate)
    low_grads = weight_grads(
        [(late, a) for a in attended] + [(late_two, g) for part in parts for g in part[:3]]
    )
    low = Scatter(*low_grads)

    gate = low_grads
    low_stage = low.over_core(gate)
    parts.append(attend_back(3, gate))

    gate = parts[3][0], low_stage, second_stage
    low_stage = low.corners(gate)
    gate_up_grad = second.along_z0(gate)
    late = after(normed, gate)
    high_grads = weight_grads([(late, g) for g in parts[3][:3]])
    high = Scatter(*high_grads)

    gate = high_grads, low_stage
    low_stage, high_stage = low.over_xy(gate), high.over_core(gate)
    grad_rows, first_sums = over_rows(
        last_kernel, "last",
        [g for part in parts for g in part[:3]] + [after(att_low, gate), tokens],
        [(near_low, (HALF, 3 * HALF), 0), (g_low.far, (HALF, 3 * HALF), 0)]
        + [(near_high, (HALF, 3 * HALF), 0), (g_high.far, (HALF, 3 * HALF), 0), vectors, order],
        [(WIDTH, BF16)], [WIDTH], flops=9_000_000_000, step=520,
    )
    high.corners(grad_rows)
    low.along_z1(grad_rows)
    patch_grad, cls_grad = to_pair(grad_rows)
    high.over_xy()
    high.along_z1()
    low_grad = low.along_z0()
    high_grad = high.along_z0()
    head_sums = jnp.dot(
        joined(*[part[3][:2] for part in parts], axis=1), order.astype(F32), precision=lax.Precision.HIGHEST
    )
    vector_grads = scatter_small(
        joined(first_sums[:2], head_sums, middle_sums[:3], branch_sums[:1]).T
    )
    blocks = [low_grad[:, WIDTH + i * HEAD_COLS :][:, :HEAD_COLS] for i in range(9)]
    blocks += [high_grad[:, i * HEAD_COLS :][:, :HEAD_COLS] for i in range(3)]
    query_grad, key_grad, value_grad = (joined(*blocks[i::3], axis=1) for i in range(3))
    return (
        outs[0],
        outs[1],
        patch_grad,
        cls_grad,
        query_grad,
        key_grad,
        value_grad,
        gate_up_grad[:, :hidden],
        gate_up_grad[:, wide : wide + hidden],
        low_grad[:, :WIDTH].T,
        down_grad[:, :hidden].T,
        vector_grads.T,
        ffn_grads,
    )


def solution(mesh):
    in_specs = (
        P("dp", "ctx", None),
        P("dp", None),
        P("dp", "ctx", None),
        P("dp", None),
        P("dp"),
        P("ctx", None),
        P(("dp", "ctx"), None),
        P(("dp", "ctx"), None),
        P(("dp", "ctx"), None),
        P(("dp", "ctx"), None),
        P(("dp", "ctx"), None),
        P(None, ("dp", "ctx")),
        P(None, ("dp", "ctx")),
        P(None, ("dp", "ctx")),
        P(),
    )
    out_specs = (
        P("dp", "ctx", None),
        P("dp", None),
        P("dp", "ctx", None),
        P("dp", None),
        P(("dp", "ctx"), None),
        P(("dp", "ctx"), None),
        P(("dp", "ctx"), None),
        P(("dp", "ctx"), None),
        P(("dp", "ctx"), None),
        P(None, ("dp", "ctx")),
        P(None, ("dp", "ctx")),
        P(None, ("dp", "ctx")),
        P(),
    )
    sizes = dict(mesh.shape)
    pairs = sizes["dp"] == 16 and sizes["ctx"] == 2
    body = paired_device if pairs else on_device
    return jax.shard_map(
        body, mesh=mesh, in_specs=in_specs, out_specs=out_specs, check_vma=False
    )
```

```python
import functools
import math

import jax
import jax.numpy as jnp
from jax import lax
from jax.experimental import pallas as pl
from jax.experimental.pallas import tpu as pltpu
from jax.sharding import PartitionSpec as P

HD = 64
MICRO = 2


epsilon = 1e-06


def layer_norm(values, gain, shift):
    centred = values - jnp.mean(values, axis=-1, keepdims=True)
    inv_std = lax.rsqrt(jnp.mean(centred * centred, axis=-1, keepdims=True) + epsilon)
    unit_rows = centred * inv_std
    return (unit_rows * gain + shift, unit_rows, inv_std)


def norm_back(grad_out, gain, unit_rows, inv_std, row_mask):
    scaled = grad_out * gain
    grad_in = inv_std * (
        scaled
        - jnp.mean(scaled, axis=-1, keepdims=True)
        - unit_rows * jnp.mean(scaled * unit_rows, axis=-1, keepdims=True)
    )
    weighted = grad_out * row_mask
    return (grad_in, jnp.sum(weighted * unit_rows, axis=(0, 1)), jnp.sum(weighted, axis=(0, 1)))


def rotary_tables(coords):
    freqs = 10000.0 ** (-jnp.arange(16).astype(jnp.float32) / 16.0)
    along_rows = coords[:, 0:1].astype(jnp.float32) * freqs[None, :]
    along_cols = coords[:, 1:2].astype(jnp.float32) * freqs[None, :]
    angles = jnp.concatenate([along_rows, along_rows, along_cols, along_cols], axis=1)
    cosines = jnp.concatenate([jnp.ones((1, 64), jnp.float32), jnp.cos(angles)], axis=0)
    sines = jnp.concatenate([jnp.zeros((1, 64), jnp.float32), jnp.sin(angles)], axis=0)
    return (cosines, sines)


def rotate(values, cosines, sines):
    swapped = jnp.concatenate(
        [-values[..., 16:32], values[..., 0:16], -values[..., 48:64], values[..., 32:48]], axis=-1
    )
    return values * cosines[:, None, :] + swapped * sines[:, None, :]


def unrotate(grads, cosines, sines):
    with_sin = grads * sines[:, None, :]
    moved = jnp.concatenate(
        [with_sin[..., 16:32], -with_sin[..., 0:16], with_sin[..., 48:64], -with_sin[..., 32:48]],
        axis=-1,
    )
    return grads * cosines[:, None, :] + moved


def project(rows_in, weight):
    return jnp.einsum("brd,de->bre", rows_in, weight, preferred_element_type=jnp.float32)


def project_back(grads, weight):
    return jnp.einsum("bre,de->brd", grads, weight, preferred_element_type=jnp.float32)


def weight_grad(rows_in, grads):
    return jnp.einsum("brd,bre->de", rows_in, grads, preferred_element_type=jnp.float32)


def fetch_forward(w_query, w_key, w_value, w_gate, w_up, w_out, w_down, layer_vectors):
    first_group = (
        lax.all_gather(w_query, ("dp", "ctx"), axis=0, tiled=True),
        lax.all_gather(w_key, ("dp", "ctx"), axis=0, tiled=True),
        lax.all_gather(w_value, ("dp", "ctx"), axis=0, tiled=True),
        lax.all_gather(w_gate, ("dp", "ctx"), axis=0, tiled=True),
        lax.all_gather(w_up, ("dp", "ctx"), axis=0, tiled=True),
    )
    second_group = (
        lax.all_gather(w_out, ("dp", "ctx"), axis=1, tiled=True),
        lax.all_gather(w_down, ("dp", "ctx"), axis=1, tiled=True),
        lax.all_gather(layer_vectors, ("dp", "ctx"), axis=1, tiled=True),
    )
    return tuple(first_group) + tuple(second_group)


def fetch_backward(w_query, w_key, w_value, w_gate, w_up, w_out, w_down, layer_vectors):
    first_group = (
        lax.all_gather(w_query, ("dp", "ctx"), axis=0, tiled=True),
        lax.all_gather(w_key, ("dp", "ctx"), axis=0, tiled=True),
        lax.all_gather(w_value, ("dp", "ctx"), axis=0, tiled=True),
        lax.all_gather(w_gate, ("dp", "ctx"), axis=0, tiled=True),
        lax.all_gather(w_up, ("dp", "ctx"), axis=0, tiled=True),
    )
    second_group = (
        lax.all_gather(w_out, ("dp", "ctx"), axis=1, tiled=True),
        lax.all_gather(w_down, ("dp", "ctx"), axis=1, tiled=True),
        lax.all_gather(layer_vectors, ("dp", "ctx"), axis=1, tiled=True),
    )
    return tuple(first_group) + tuple(second_group)


def head_forward(item):
    block_of_queries, block_of_keys, block_of_values = item
    logit_scores = jnp.einsum(
        "wey,wmy->wem", block_of_queries, block_of_keys, preferred_element_type=jnp.float32
    )
    row_peak = jnp.max(logit_scores, axis=-1, keepdims=True)
    shifted = jnp.exp(logit_scores - row_peak)
    denominator = jnp.sum(shifted, axis=-1, keepdims=True)
    reduced_probabilities = (shifted / denominator).astype(jnp.bfloat16)
    blended_values = jnp.einsum(
        "sce,sem->scm", reduced_probabilities, block_of_values, preferred_element_type=jnp.float32
    )
    return (blended_values, (row_peak + jnp.log(denominator))[..., 0])


def forward_pass(tokens, weights, ffn_vec, cosines, sines):
    w_query, w_key, w_value, w_gate, w_up, w_out, w_down, vectors_low = weights
    vectors = vectors_low.astype(jnp.float32)
    batch, row_count, model_width = tokens.shape
    heads = model_width // HD
    normed, unit_one, std_one = layer_norm(tokens, vectors[0], vectors[1])
    normed_low = normed.astype(jnp.bfloat16)
    queries = project(normed_low, w_query) + vectors[2]
    keys_raw = project(normed_low, w_key)
    values_low = (project(normed_low, w_value) + vectors[3]).astype(jnp.bfloat16)
    q_rot = (
        rotate(queries.reshape(batch, row_count, heads, HD), cosines, sines) * HD ** (-0.5)
    ).astype(jnp.bfloat16)
    k_flat = (
        rotate(keys_raw.reshape(batch, row_count, heads, HD), cosines, sines)
        .astype(jnp.bfloat16)
        .reshape(batch, row_count, model_width)
    )
    far_keys, far_values = (
        lax.all_gather(k_flat[:, 1:], "ctx", axis=1, tiled=True),
        lax.all_gather(values_low[:, 1:], "ctx", axis=1, tiled=True),
    )
    all_keys = jnp.concatenate([k_flat[:, :1], far_keys], axis=1)
    all_values = jnp.concatenate([values_low[:, :1], far_values], axis=1)
    length = all_keys.shape[1]
    head_queries = q_rot.transpose(2, 0, 1, 3)
    head_keys = all_keys.reshape(batch, length, heads, HD).transpose(2, 0, 1, 3)
    head_values = all_values.reshape(batch, length, heads, HD).transpose(2, 0, 1, 3)
    head_out, log_sums = lax.map(head_forward, (head_queries, head_keys, head_values))
    attended = (
        head_out.transpose(1, 2, 0, 3).reshape(batch, row_count, model_width).astype(jnp.bfloat16)
    )
    middle = tokens + (project(attended, w_out) + vectors[4])
    normed_two, unit_two, std_two = layer_norm(middle, vectors[5], vectors[6])
    normed_two_low = normed_two.astype(jnp.bfloat16)
    gate_proj = project(normed_two_low, w_gate) + ffn_vec[0]
    up_proj = project(normed_two_low, w_up) + ffn_vec[1]
    activated = jax.nn.silu(gate_proj)
    inner_act, unit_three, std_three = layer_norm(activated * up_proj, ffn_vec[2], ffn_vec[3])
    inner_low = inner_act.astype(jnp.bfloat16)
    result = middle + (project(inner_low, w_down) + vectors[7])
    saved = (
        normed_low,
        unit_one,
        std_one,
        head_queries,
        head_keys,
        head_values,
        log_sums,
        attended,
        unit_two,
        std_two,
        normed_two_low,
        gate_proj,
        up_proj,
        activated,
        unit_three,
        std_three,
        inner_low,
    )
    return (result, saved)


def backward_pass(grad_rows, weights, ffn_vec, cosines, sines, saved, row_mask):
    w_query, w_key, w_value, w_gate, w_up, w_out, w_down, vectors_low = weights
    vectors = vectors_low.astype(jnp.float32)
    (
        normed_low,
        unit_one,
        std_one,
        head_queries,
        head_keys,
        head_values,
        log_sums,
        attended,
        unit_two,
        std_two,
        normed_two_low,
        gate_proj,
        up_proj,
        activated,
        unit_three,
        std_three,
        inner_low,
    ) = saved
    batch, row_count, model_width = grad_rows.shape
    heads = model_width // HD
    reduced_mask = row_mask.astype(jnp.bfloat16)
    branch_low = grad_rows.astype(jnp.bfloat16)
    grad_down = weight_grad(inner_low, branch_low * reduced_mask)
    grad_inner = project_back(branch_low, w_down)
    grad_mix, gain_three, shift_three = norm_back(
        grad_inner, ffn_vec[2], unit_three, std_three, row_mask
    )
    sigmoid_gate = jax.nn.sigmoid(gate_proj)
    gate_low = (
        grad_mix * up_proj * sigmoid_gate * (1.0 + gate_proj * (1.0 - sigmoid_gate))
    ).astype(jnp.bfloat16)
    up_low = (grad_mix * activated).astype(jnp.bfloat16)
    grad_gate_w = weight_grad(normed_two_low * reduced_mask, gate_low)
    grad_up_w = weight_grad(normed_two_low * reduced_mask, up_low)
    grad_normed_two = project_back(gate_low, w_gate) + project_back(up_low, w_up)
    grad_mid_norm, gain_two, shift_two = norm_back(
        grad_normed_two, vectors[5], unit_two, std_two, row_mask
    )
    grad_middle = grad_rows + grad_mid_norm
    out_low = grad_middle.astype(jnp.bfloat16)
    grad_out_w = weight_grad(attended * reduced_mask, out_low)
    attended_grad = project_back(out_low, w_out).astype(jnp.bfloat16)
    head_grads = attended_grad.reshape(batch, row_count, heads, HD).transpose(2, 0, 1, 3)

    def head_backward(item):
        block_of_queries, block_of_keys, block_of_values, block_gradient, log_block = item
        logit_scores = jnp.einsum(
            "wey,wmy->wem", block_of_queries, block_of_keys, preferred_element_type=jnp.float32
        )
        attn_probs = jnp.exp(logit_scores - log_block[..., None])
        grad_probs = jnp.einsum(
            "wey,wmy->wem", block_gradient, block_of_values, preferred_element_type=jnp.float32
        )
        inner_sum = jnp.sum(attn_probs * grad_probs, axis=-1, keepdims=True)
        score_gradients = (attn_probs * (grad_probs - inner_sum)).astype(jnp.bfloat16)
        grad_query = jnp.einsum(
            "sce,sem->scm", score_gradients, block_of_keys, preferred_element_type=jnp.float32
        )
        grad_key = jnp.einsum(
            "ipz,iph->izh",
            score_gradients * reduced_mask,
            block_of_queries,
            preferred_element_type=jnp.float32,
        )
        grad_value = jnp.einsum(
            "ipz,iph->izh",
            attn_probs.astype(jnp.bfloat16) * reduced_mask,
            block_gradient,
            preferred_element_type=jnp.float32,
        )
        return (grad_query, grad_key, grad_value)

    grad_q_heads, grad_k_heads, grad_v_heads = lax.map(
        head_backward, (head_queries, head_keys, head_values, head_grads, log_sums)
    )
    length = head_keys.shape[2]
    grad_keys = grad_k_heads.transpose(1, 2, 0, 3).reshape(batch, length, model_width)
    grad_values = grad_v_heads.transpose(1, 2, 0, 3).reshape(batch, length, model_width)
    own_keys, own_values = (
        lax.psum_scatter(
            grad_keys[:, 1:].astype(jnp.bfloat16), "ctx", scatter_dimension=1, tiled=True
        ).astype(jnp.float32),
        lax.psum_scatter(
            grad_values[:, 1:].astype(jnp.bfloat16), "ctx", scatter_dimension=1, tiled=True
        ).astype(jnp.float32),
    )
    class_keys, class_values = lax.psum((grad_keys[:, :1], grad_values[:, :1]), "ctx")
    key_rows = jnp.concatenate([class_keys, own_keys], axis=1).reshape(batch, row_count, heads, HD)
    value_rows = jnp.concatenate([class_values, own_values], axis=1)
    key_low = (
        unrotate(key_rows, cosines, sines)
        .reshape(batch, row_count, model_width)
        .astype(jnp.bfloat16)
    )
    value_low = value_rows.astype(jnp.bfloat16)
    query_rows = grad_q_heads.transpose(1, 2, 0, 3)
    query_low = (
        (unrotate(query_rows, cosines, sines) * HD ** (-0.5))
        .reshape(batch, row_count, model_width)
        .astype(jnp.bfloat16)
    )
    grad_query_w = weight_grad(normed_low * reduced_mask, query_low)
    grad_key_w = weight_grad(normed_low * reduced_mask, key_low)
    grad_value_w = weight_grad(normed_low * reduced_mask, value_low)
    grad_normed = (
        project_back(query_low, w_query)
        + project_back(key_low, w_key)
        + project_back(value_low, w_value)
    )
    grad_in_norm, gain_one, shift_one = norm_back(
        grad_normed, vectors[0], unit_one, std_one, row_mask
    )
    grad_tokens = grad_middle + grad_in_norm

    def column_sum(rounded):
        return jnp.sum(rounded.astype(jnp.float32) * row_mask, axis=(0, 1))

    vector_grads = jnp.stack(
        [
            gain_one,
            shift_one,
            column_sum(query_low),
            column_sum(value_low),
            column_sum(out_low),
            gain_two,
            shift_two,
            column_sum(branch_low),
        ]
    )
    ffn_grads = jnp.stack([column_sum(gate_low), column_sum(up_low), gain_three, shift_three])
    return (
        grad_tokens,
        (
            (grad_query_w, grad_key_w, grad_value_w, grad_gate_w, grad_up_w),
            (grad_out_w, grad_down, vector_grads),
            ffn_grads,
        ),
    )


def on_device(
    patch_in,
    cls_in,
    d_patch,
    d_cls,
    image_valid,
    patch_coords,
    w_query,
    w_key,
    w_value,
    w_gate,
    w_up,
    w_out,
    w_down,
    layer_vectors,
    ffn_vectors,
):
    images, patch_rows, model_width = patch_in.shape
    group_size = images // MICRO
    cosines, sines = rotary_tables(patch_coords)
    first_flag = (lax.axis_index("ctx") == 0).astype(jnp.float32)
    row_weight = jnp.concatenate([first_flag[None], jnp.ones((patch_rows,), jnp.float32)])
    row_mask = row_weight[None, :, None]
    ffn_vec = ffn_vectors.astype(jnp.float32)
    keep_mask = image_valid.astype(jnp.float32)
    results = []
    totals = None
    for micro_step in range(MICRO):
        first_image = micro_step * group_size
        last_image = first_image + group_size
        tokens = jnp.concatenate(
            [cls_in[first_image:last_image, None, :], patch_in[first_image:last_image]], axis=1
        ).astype(jnp.float32)
        weights = fetch_forward(w_query, w_key, w_value, w_gate, w_up, w_out, w_down, layer_vectors)
        result, saved = forward_pass(tokens, weights, ffn_vec, cosines, sines)
        keep_rows = keep_mask[first_image:last_image][:, None, None]
        grad_rows = (
            jnp.concatenate(
                [d_cls[first_image:last_image, None, :], d_patch[first_image:last_image]], axis=1
            ).astype(jnp.float32)
            * keep_rows
        )
        back_weights = fetch_backward(
            w_query, w_key, w_value, w_gate, w_up, w_out, w_down, layer_vectors
        )
        grad_tokens, weight_grads = backward_pass(
            grad_rows, back_weights, ffn_vec, cosines, sines, saved, row_mask
        )
        if totals is None:
            totals = weight_grads
        else:
            totals = jax.tree.map(lambda first, second: first + second, totals, weight_grads)
        results.append(
            ((result * keep_rows).astype(jnp.bfloat16), grad_tokens.astype(jnp.bfloat16))
        )
    out_rows = jnp.concatenate([entry[0] for entry in results], axis=0)
    grad_out_rows = jnp.concatenate([entry[1] for entry in results], axis=0)
    in_grads, out_grads, ffn_total = totals
    owned_in = (
        lax.psum_scatter(in_grads[0], ("dp", "ctx"), scatter_dimension=0, tiled=True),
        lax.psum_scatter(in_grads[1], ("dp", "ctx"), scatter_dimension=0, tiled=True),
        lax.psum_scatter(in_grads[2], ("dp", "ctx"), scatter_dimension=0, tiled=True),
        lax.psum_scatter(in_grads[3], ("dp", "ctx"), scatter_dimension=0, tiled=True),
        lax.psum_scatter(in_grads[4], ("dp", "ctx"), scatter_dimension=0, tiled=True),
    )
    owned_out = (
        lax.psum_scatter(out_grads[0], ("dp", "ctx"), scatter_dimension=1, tiled=True),
        lax.psum_scatter(out_grads[1], ("dp", "ctx"), scatter_dimension=1, tiled=True),
        lax.psum_scatter(out_grads[2], ("dp", "ctx"), scatter_dimension=1, tiled=True),
    )
    ffn_summed = lax.psum(ffn_total, ("dp", "ctx"))
    return (
        out_rows[:, 1:],
        out_rows[:, 0],
        grad_out_rows[:, 1:],
        grad_out_rows[:, 0],
        owned_in[0],
        owned_in[1],
        owned_in[2],
        owned_in[3],
        owned_in[4],
        owned_out[0],
        owned_out[1],
        owned_out[2],
        ffn_summed,
    )


BOTH = ("dp", "ctx")
BIT_X, BIT_CORE, BIT_Y, BIT_Z0, BIT_Z1 = 1, 2, 4, 16, 8
ROWS = 1040
KEYS = 1024
WIDTH = 1024
HALF = 512
HEAD_COLS = 256
STEP = 208
LOG2E = math.log2(math.e)
COST = 4
F32 = jnp.float32
BF16 = jnp.bfloat16


SENT = []


def swap_over(value, bit):
    SENT.append(value)
    count = lax.axis_size(BOTH)
    return lax.ppermute(value, BOTH, [(i, i ^ bit) for i in range(count)])


def joined(*parts, axis=0):
    return jnp.concatenate(parts, axis=axis)


def after(value, *deps):
    return lax.optimization_barrier((value,) + deps)[0]


def ready(value, *deps):
    corners = [sum(v[0:1, 0:1].astype(F32) for v in SENT)] if SENT else []
    SENT.clear()
    return after(value, *deps, *corners)


def dot_nn(a, b):
    return lax.dot_general(a, b, (((1,), (0,)), ((), ())), preferred_element_type=F32)


def dot_nt(a, b):
    return lax.dot_general(a, b, (((1,), (1,)), ((), ())), preferred_element_type=F32)


def dot_tn(a, b):
    return lax.dot_general(a, b, (((0,), (0,)), ((), ())), preferred_element_type=F32)


def cost_of(flops, bytes_accessed, transcendentals):
    return pl.CostEstimate(
        flops=int(COST * flops), bytes_accessed=int(COST * bytes_accessed), transcendentals=int(COST * transcendentals)
    )


def pack_rows(*parts):
    total, columns = sum(p.shape[0] for p in parts), parts[0].shape[1]
    blocks = columns // 128
    steps = next(n for n in (4, 5, 3, 2, 1) if blocks % n == 0)
    tile = columns // steps

    def kernel(*refs):
        out, start = refs[len(parts)], 0
        for ref in refs[: len(parts)]:
            out[start : start + ref.shape[0], :] = ref[...]
            start += ref.shape[0]

    return pl.pallas_call(
        kernel,
        grid=(steps,),
        in_specs=[pl.BlockSpec((p.shape[0], tile), lambda j: (0, j)) for p in parts],
        out_specs=pl.BlockSpec((total, tile), lambda j: (0, j)),
        out_shape=jax.ShapeDtypeStruct((total, columns), parts[0].dtype),
        compiler_params=pltpu.CompilerParams(vmem_limit_bytes=32 << 20),
        cost_estimate=cost_of(flops=0, bytes_accessed=4 * total * columns, transcendentals=0),
        name="pack_rows",
    )(*parts)


class Gather:
    def __init__(self, local):
        self.part = local

    def along_z0(self, *deps):
        part = after(self.part, *deps)
        far = swap_over(part, BIT_Z0)
        self.part = joined(part, far)
        return far

    def along_z1(self, *deps):
        part = after(self.part, *deps)
        far = swap_over(part, BIT_Z1)
        self.part = joined(part, far)
        return far

    def along_xy(self, *deps):
        part = after(self.part, *deps)
        self.over = swap_over(part, BIT_X), swap_over(part, BIT_Y)
        return self.over

    def corners(self, *deps):
        over_x, over_y = after(self.over, *deps)
        self.corner = swap_over(over_y[:64], BIT_X), swap_over(over_x[64:], BIT_Y)
        return self.corner

    def whole(self, *deps):
        parts = after((self.part, self.over, self.corner), *deps)
        self.near = pack_rows(parts[0], parts[1][1], parts[1][0], *parts[2])
        self.far = swap_over(self.near, BIT_CORE)
        return self.near


def rounded_sum(*terms):
    total = terms[0].astype(F32)
    for term in terms[1:]:
        total = total + term.astype(F32)
    return total.astype(BF16)


class Scatter:
    def over_core(self, far, *deps):
        return swap_over(after(far, *deps), BIT_CORE)

    def corner(self, total, *deps):
        self.total = after(total, *deps)
        self.to_x = rounded_sum(self.total[256:384], swap_over(self.total[384:], BIT_Y))
        self.to_y = self.total[128:256]
        return self.to_x

    def corners(self, total, *deps):
        self.total = total = after(total, *deps)
        from_x, from_y = swap_over(total[384:448], BIT_X), swap_over(total[448:512], BIT_Y)
        self.to_y = joined(rounded_sum(total[128:192], from_x), total[192:256])
        self.to_x = joined(total[256:320], rounded_sum(total[320:384], from_y))
        return self.to_x, self.to_y

    def sides(self, *deps):
        to_x, to_y = after((self.to_x, self.to_y), *deps)
        self.total = rounded_sum(self.total[:128], swap_over(to_y, BIT_Y), swap_over(to_x, BIT_X))
        return self.total

    def over_x(self, *deps):
        total = after(self.total, *deps)
        self.total = rounded_sum(total[:256], swap_over(total[256:], BIT_X))
        return self.total

    def over_y(self, *deps):
        total = after(self.total, *deps)
        self.total = rounded_sum(total[:128], swap_over(total[128:], BIT_Y))
        return self.total

    def along_z1(self, *deps):
        total = after(self.total, *deps)
        self.total = rounded_sum(total[:64], swap_over(total[64:], BIT_Z1))
        return self.total

    def along_z0(self, *deps):
        total = after(self.total, *deps)
        return total[:32].astype(F32) + swap_over(total[32:], BIT_Z0).astype(F32)


def scatter_small(value):
    for rows, bit in ((512, BIT_CORE), (256, BIT_X), (128, BIT_Y), (64, BIT_Z1), (32, BIT_Z0)):
        value = value[:rows] + swap_over(value[rows:], bit)
    return value


def rotate_lanes(x, cosines, sines_up, sines_down):
    width = x.shape[1]
    return x * cosines + pltpu.roll(x, width - 16, 1) * sines_up + pltpu.roll(x, 16, 1) * sines_down


def twice(table):
    return jnp.concatenate([table, table], axis=1)


def attention_kernel(
    x_ref, qn_ref, qf_ref, kn_ref, kf_ref, vn_ref, vf_ref, b_ref, c_ref, s1_ref, s2_ref,
    q_ref, k_ref, v_ref, o_ref, l_ref
):
    def project(near_ref, far_ref):
        return dot_nn(x_ref[:, :HALF], near_ref[...]) + dot_nn(x_ref[:, HALF:], far_ref[...])

    c, s1, s2 = twice(c_ref[...]), twice(s1_ref[...]), twice(s2_ref[...])
    q = project(qn_ref, qf_ref) + b_ref[2:3, :]
    q_ref[...] = (rotate_lanes(q, c, s1, s2) * (LOG2E / 8)).astype(BF16)
    k_ref[...] = rotate_lanes(project(kn_ref, kf_ref), c, s1, s2).astype(BF16)
    v_ref[...] = (project(vn_ref, vf_ref) + b_ref[3:4, :]).astype(BF16)
    lane = lax.broadcasted_iota(jnp.int32, (1, 128), 1)
    low_half = lane < 64

    stats = jnp.zeros((ROWS, 128), F32)
    for pair in range(2):
        cols = slice(pair * 128, pair * 128 + 128)
        q_pair = q_ref[:, cols]
        k_pair, v_pair = k_ref[0:KEYS, cols], v_ref[0:KEYS, cols]
        k_class = k_ref[KEYS : KEYS + 16, cols].astype(F32)[0:1]
        v_class = v_ref[KEYS : KEYS + 16, cols].astype(F32)[0:1]
        product = q_pair.astype(F32) * k_class
        outs = []
        for h in range(2):
            own = low_half if h == 0 else ~low_half
            scores = dot_nt(jnp.where(own, q_pair, jnp.zeros_like(q_pair)), k_pair)
            class_score = jnp.sum(jnp.where(own, product, 0.0), axis=1, keepdims=True)
            peak = jnp.maximum(jnp.max(scores, axis=1, keepdims=True), class_score)
            p = jnp.exp2(scores - peak)
            class_p = jnp.exp2(class_score - peak)
            total = jnp.sum(p, axis=1, keepdims=True) + class_p
            out = dot_nn(p.astype(BF16), v_pair) + class_p * v_class
            outs.append(out * (1.0 / total))
            stats = jnp.where(lane == pair * 2 + h, peak + jnp.log2(total), stats)
        o_ref[:, cols] = jnp.where(low_half, outs[0], outs[1]).astype(BF16)
    l_ref[...] = stats.T[0:8, :]


def attention_forward(x, near, far, biases, head_block, at, tables):
    def block(index):
        return pl.BlockSpec((HALF, HEAD_COLS), lambda j: (0, index))

    def whole(a):
        return pl.BlockSpec(a.shape, lambda j: (0, 0))

    out = pl.BlockSpec((ROWS, HEAD_COLS), lambda j: (0, 0))
    return pl.pallas_call(
        attention_kernel,
        grid=(1,),
        in_specs=[whole(x)]
        + [block(at + first) for first in (0, 0, 2, 2, 4, 4)]
        + [pl.BlockSpec((8, HEAD_COLS), lambda j: (0, head_block))]
        + [whole(t) for t in tables],
        out_specs=[out] * 4 + [pl.BlockSpec((8, ROWS), lambda j: (0, 0))],
        out_shape=[jax.ShapeDtypeStruct((ROWS, HEAD_COLS), BF16)] * 4 + [jax.ShapeDtypeStruct((8, ROWS), F32)],
        compiler_params=pltpu.CompilerParams(vmem_limit_bytes=56 << 20),
        cost_estimate=cost_of(flops=7_500_000_000, bytes_accessed=7_000_000, transcendentals=4_300_000),
        name="attention_forward",
    )(x, near, far, near, far, near, far, biases, *tables)


def attention_back_kernel(
    q_ref, k_ref, v_ref, g_ref, o_ref, l_ref, c_ref, s1_ref, s2_ref,
    dq_ref, dk_ref, dv_ref, sum_ref, dq_turned, dk_sum, dv_sum, delta_ref, k_turned, *, step
):
    lane = lax.broadcasted_iota(jnp.int32, (1, 128), 1)
    low_half = lane < 64
    deltas = jnp.zeros((ROWS, 128), F32)
    for pair in range(2):
        cols = slice(pair * 128, pair * 128 + 128)
        product = g_ref[:, cols].astype(F32) * o_ref[:, cols].astype(F32)
        for h in range(2):
            own = low_half if h == 0 else ~low_half
            delta = jnp.sum(jnp.where(own, product, 0.0), axis=1, keepdims=True)
            deltas = jnp.where(lane == pair * 2 + h, delta, deltas)
    delta_ref[...] = deltas.T[0:8, :]
    real_key = lax.broadcasted_iota(jnp.int32, (ROWS, 1), 0) <= KEYS
    class_key = lax.broadcasted_iota(jnp.int32, (ROWS - KEYS, 1), 0) == 0
    k_turned[...] = k_ref[...].T
    for t in range(KEYS // step):
        rows = pl.ds(t * step, step)
        for pair in range(2):
            cols = slice(pair * 128, pair * 128 + 128)
            q_pair, g_pair = q_ref[rows, cols], g_ref[rows, cols]
            k_pair, v_pair = k_ref[:, cols], v_ref[:, cols]
            dk, dv = None, None
            for h in range(2):
                own = low_half if h == 0 else ~low_half
                head = pair * 2 + h
                q_head = jnp.where(own, q_pair, jnp.zeros_like(q_pair))
                g_head = jnp.where(own, g_pair, jnp.zeros_like(g_pair))
                scores = dot_nt(k_pair, q_head)
                log_sums = l_ref[head : head + 1, rows]
                p = jnp.concatenate(
                    [
                        jnp.exp2(scores[:KEYS] - log_sums),
                        jnp.where(class_key, jnp.exp2(scores[KEYS:] - log_sums), 0.0),
                    ],
                    axis=0,
                )
                gp = dot_nt(v_pair, g_head)
                ds = (p * (gp - delta_ref[head : head + 1, rows])).astype(BF16)
                dv_part, dk_part = dot_nn(p.astype(BF16), g_head), dot_nn(ds, q_head)
                dv = dv_part if dv is None else dv + dv_part
                dk = dk_part if dk is None else dk + dk_part
                own_rows = slice(head * 64, head * 64 + 64)
                dq_turned[own_rows, rows] = dot_nn(k_turned[own_rows, :], ds)
            if t == 0:
                dk_sum[:, cols], dv_sum[:, cols] = dk, dv
            else:
                dk_sum[:, cols] += dk
                dv_sum[:, cols] += dv
    q_class = q_ref[KEYS : KEYS + 16, :][0:1].astype(F32)
    g_class = g_ref[KEYS : KEYS + 16, :][0:1].astype(F32)
    shape = (128, HEAD_COLS)
    own = lax.broadcasted_iota(jnp.int32, shape, 0) == lax.broadcasted_iota(jnp.int32, shape, 1) // 64
    q_diag = jnp.where(own, q_class, 0.0).astype(BF16)
    g_diag = jnp.where(own, g_class, 0.0).astype(BF16)
    scores, gp = dot_nt(k_ref[...], q_diag), dot_nt(v_ref[...], g_diag)
    log_class, delta_class = jnp.zeros((1, 128), F32), jnp.zeros((1, 128), F32)
    for head in range(4):
        log_class = jnp.where(lane == head, l_ref[head : head + 1, KEYS : KEYS + 1], log_class)
        delta_class = jnp.where(lane == head, delta_ref[head : head + 1, KEYS : KEYS + 1], delta_class)
    p = jnp.where(real_key & (lane < 4), jnp.exp2(scores - log_class), 0.0)
    ds = (p * (gp - delta_class)).astype(BF16)
    dv = dv_sum[...] + dot_nn(p.astype(BF16), g_diag)
    dk = dk_sum[...] + dot_nn(ds, q_diag)
    dq_class = jnp.sum(jnp.where(own, dot_tn(ds, k_ref[...]), 0.0), axis=0, keepdims=True)
    first = lax.broadcasted_iota(jnp.int32, (16, 1), 0) == 0
    dq = jnp.concatenate([dq_turned[...].T, jnp.where(first, dq_class, 0.0)], axis=0)
    c, s1, s2 = twice(c_ref[...]), twice(s1_ref[...]), twice(s2_ref[...])
    dq = (rotate_lanes(dq, c, -s1, -s2) * 0.125).astype(BF16)
    dv = dv.astype(BF16)
    dq_ref[...] = dq
    dk_ref[...] = (rotate_lanes(dk, c, -s1, -s2) * (1.0 / LOG2E)).astype(BF16)
    dv_ref[...] = dv
    sum_ref[0:1, :] = jnp.sum(dq.astype(F32), axis=0, keepdims=True)
    sum_ref[1:2, :] = jnp.sum(dv.astype(F32), axis=0, keepdims=True)
    sum_ref[2:8, :] = jnp.zeros((6, HEAD_COLS), F32)


def attention_backward(q, k, v, o, log_sums, g, tables, step=256):
    def whole(a):
        return pl.BlockSpec(a.shape, lambda j: (0, 0))

    block = pl.BlockSpec((ROWS, HEAD_COLS), lambda j: (0, 0))
    return pl.pallas_call(
        functools.partial(attention_back_kernel, step=step),
        grid=(1,),
        in_specs=[block] * 5 + [pl.BlockSpec((8, ROWS), lambda j: (0, 0))] + [whole(t) for t in tables],
        out_specs=[block] * 3 + [pl.BlockSpec((8, HEAD_COLS), lambda j: (0, 0))],
        out_shape=[jax.ShapeDtypeStruct((ROWS, HEAD_COLS), BF16)] * 3
        + [jax.ShapeDtypeStruct((8, HEAD_COLS), F32)],
        scratch_shapes=[pltpu.VMEM((HEAD_COLS, KEYS), F32)]
        + [pltpu.VMEM((ROWS, HEAD_COLS), F32)] * 2
        + [pltpu.VMEM((8, ROWS), F32), pltpu.VMEM((HEAD_COLS, ROWS), BF16)],
        compiler_params=pltpu.CompilerParams(vmem_limit_bytes=48 << 20),
        cost_estimate=cost_of(
            flops=13_000_000_000, bytes_accessed=5_000_000, transcendentals=4_300_000
        ),
        name="attention_backward",
    )(q, k, v, g, o, log_sums, *tables)


def over_rows(kernel, name, tiled, held, outs, sums=(), flops=0, step=STEP, only=None):
    rows = ROWS if only is None else step
    if only is None:
        in_specs = [pl.BlockSpec((step, a.shape[1]), lambda i: (i, 0)) for a in tiled]
    else:
        in_specs = [
            pl.BlockSpec((pl.Element(step), pl.Element(a.shape[1])), lambda i: (only, 0)) for a in tiled
        ]
    held = [h if isinstance(h, tuple) else (h, h.shape, 0) for h in held]
    in_specs += [
        pl.BlockSpec(shape, lambda i, column=column: (0, column), pipeline_mode=pl.Buffered(1))
        for _, shape, column in held
    ]
    held = [h[0] for h in held]
    out_specs = [pl.BlockSpec((step, n), lambda i: (i, 0)) for n, _ in outs]
    out_specs += [pl.BlockSpec((8, n), lambda i: (0, 0)) for n in sums]
    out_shape = [jax.ShapeDtypeStruct((rows, n), t) for n, t in outs]
    out_shape += [jax.ShapeDtypeStruct((8, n), F32) for n in sums]
    moved = sum(a.size * a.dtype.itemsize for a in list(tiled) + list(held))
    moved += sum(s.size * s.dtype.itemsize for s in out_shape)
    return pl.pallas_call(
        kernel,
        grid=(rows // step,),
        in_specs=in_specs,
        out_specs=out_specs,
        out_shape=out_shape,
        compiler_params=pltpu.CompilerParams(vmem_limit_bytes=56 << 20),
        cost_estimate=cost_of(flops=flops, bytes_accessed=moved, transcendentals=0),
        name=name,
    )(*tiled, *held)


def add_sums(ref, *rows):
    @pl.when(pl.program_id(0) == 0)
    def _():
        ref[...] = jnp.zeros_like(ref)

    for i, value in enumerate(rows):
        ref[i : i + 1, :] += jnp.sum(value, axis=0, keepdims=True)


def unit_norm(values):
    centred = values - jnp.mean(values, axis=-1, keepdims=True)
    inv_std = lax.rsqrt(jnp.mean(centred * centred, axis=-1, keepdims=True) + epsilon)
    return centred * inv_std, inv_std


def unit_norm_back(scaled, unit, inv_std):
    return inv_std * (
        scaled
        - jnp.mean(scaled, axis=-1, keepdims=True)
        - unit * jnp.mean(scaled * unit, axis=-1, keepdims=True)
    )


def vectors_kernel(near_ref, far_ref, order_ref, vec_ref, head_ref):
    rows = jnp.concatenate([near_ref[...].astype(F32).T, far_ref[...].astype(F32).T], axis=1)[0:8]
    vec_ref[...] = rows
    head_ref[...] = dot_nt(rows.astype(BF16), order_ref[...])


def gathered_vectors(near, far, order):
    block = pl.BlockSpec((HALF, 128), lambda j: (0, 3 * HALF // 128))
    out = pl.BlockSpec((8, WIDTH), lambda j: (0, 0))
    return pl.pallas_call(
        vectors_kernel,
        grid=(1,),
        in_specs=[block, block, pl.BlockSpec(order.shape, lambda j: (0, 0))],
        out_specs=[out, out],
        out_shape=[jax.ShapeDtypeStruct((8, WIDTH), F32)] * 2,
        cost_estimate=cost_of(flops=40_000_000, bytes_accessed=2_400_000, transcendentals=0),
        name="vectors",
    )(near, far, order)


def sigmoid_of(x):
    return 0.5 * jnp.tanh(0.5 * x) + 0.5


def start_kernel(rows_ref, order_ref, vec_ref, tokens_ref, normed_ref):
    tokens = dot_nn(rows_ref[...], order_ref[...])
    tokens_ref[...] = tokens.astype(BF16)
    unit, _ = unit_norm(tokens)
    normed_ref[...] = (unit * vec_ref[0:1, :] + vec_ref[1:2, :]).astype(BF16)


def middle_kernel(a0_ref, a1_ref, a2_ref, a3_ref, tokens_ref, na_ref, nb_ref, fa_ref, fb_ref, vec_ref, middle_ref, normed_ref):
    low = jnp.concatenate([a0_ref[...], a1_ref[...]], axis=1)
    high = jnp.concatenate([a2_ref[...], a3_ref[...]], axis=1)
    branch = jnp.concatenate(
        [
            dot_nt(low, na_ref[...]) + dot_nt(high, nb_ref[...]),
            dot_nt(low, fa_ref[...]) + dot_nt(high, fb_ref[...]),
        ],
        axis=1,
    )
    middle = tokens_ref[...].astype(F32) + (branch + vec_ref[4:5, :])
    middle_ref[...] = middle.astype(BF16)
    unit, _ = unit_norm(middle)
    normed_ref[...] = (unit * vec_ref[5:6, :] + vec_ref[6:7, :]).astype(BF16)


def hidden_kernel(x_ref, gn_ref, gf_ref, un_ref, uf_ref, ffn_ref, gate_ref, up_ref, inner_ref, stat_ref, *, hidden):
    near, far = x_ref[:, :HALF], x_ref[:, HALF:]
    gate = dot_nn(near, gn_ref[...]) + dot_nn(far, gf_ref[...]) + ffn_ref[0:1, :]
    up = dot_nn(near, un_ref[...]) + dot_nn(far, uf_ref[...]) + ffn_ref[1:2, :]
    gate_ref[...] = gate.astype(gate_ref.dtype)
    up_ref[...] = up.astype(up_ref.dtype)
    mix = gate * sigmoid_of(gate) * up
    mean = jnp.sum(mix, axis=1, keepdims=True) * (1.0 / hidden)
    real = lax.broadcasted_iota(jnp.int32, (1, mix.shape[1]), 1) < hidden
    centred = jnp.where(real, mix - mean, 0.0)
    inv_std = lax.rsqrt(jnp.sum(centred * centred, axis=1, keepdims=True) * (1.0 / hidden) + epsilon)
    inner_ref[...] = (centred * inv_std * ffn_ref[2:3, :] + ffn_ref[3:4, :]).astype(BF16)
    lane = lax.broadcasted_iota(jnp.int32, (1, 128), 1)
    stat_ref[...] = jnp.where(lane == 0, mean, inv_std)


def result_kernel(inner_ref, middle_ref, near_ref, far_ref, vec_ref, order_ref, keep_ref, out_ref):
    inner = inner_ref[...]
    branch = jnp.concatenate([dot_nt(inner, near_ref[...]), dot_nt(inner, far_ref[...])], axis=1)
    result = middle_ref[...].astype(F32) + (branch + vec_ref[7:8, :])
    rounded = (result * keep_ref[0:1, 0:1]).astype(BF16)
    out_ref[...] = dot_nt(rounded, order_ref[...]).astype(BF16)


def hidden_back_kernel(
    d_ref, gate_ref, up_ref, stat_ref, order_ref, keep_ref, near_ref, far_ref, ffn_ref,
    branch_ref, dgate_ref, dup_ref, wide_ref, sum_ref, *, hidden
):
    branch = (dot_nn(d_ref[...], order_ref[...]) * keep_ref[0:1, 0:1]).astype(BF16)
    branch_ref[...] = branch
    g_inner = dot_nn(branch[:, :HALF], near_ref[...]) + dot_nn(branch[:, HALF:], far_ref[...])
    gate, up = gate_ref[...].astype(F32), up_ref[...].astype(F32)
    sigmoid = sigmoid_of(gate)
    silu = gate * sigmoid
    mean, inv_std = stat_ref[:, 0:1], stat_ref[:, 1:2]
    unit = (silu * up - mean) * inv_std
    g_unit = g_inner * ffn_ref[2:3, :]
    share = 1.0 / hidden
    g_mix = inv_std * (
        g_unit
        - jnp.sum(g_unit, axis=1, keepdims=True) * share
        - unit * (jnp.sum(g_unit * unit, axis=1, keepdims=True) * share)
    )
    d_gate = (g_mix * up * (sigmoid * (1.0 + gate * (1.0 - sigmoid)))).astype(BF16)
    d_up = (g_mix * silu).astype(BF16)
    dgate_ref[...] = d_gate
    dup_ref[...] = d_up
    add_sums(wide_ref, d_gate.astype(F32), d_up.astype(F32), g_inner * unit, g_inner)
    add_sums(sum_ref, branch.astype(F32))


def middle_back_kernel(
    dgate_ref, dup_ref, branch_ref, middle_ref, gn_ref, gf_ref, un_ref, uf_ref, na_ref, nb_ref, fa_ref, fb_ref, vec_ref,
    low_ref, d0_ref, d1_ref, d2_ref, d3_ref, sum_ref
):
    d_gate, d_up = dgate_ref[...], dup_ref[...]
    g_two = jnp.concatenate(
        [
            dot_nt(d_gate, gn_ref[...]) + dot_nt(d_up, un_ref[...]),
            dot_nt(d_gate, gf_ref[...]) + dot_nt(d_up, uf_ref[...]),
        ],
        axis=1,
    )
    unit, inv_std = unit_norm(middle_ref[...].astype(F32))
    g_middle = branch_ref[...].astype(F32) + unit_norm_back(g_two * vec_ref[5:6, :], unit, inv_std)
    low = g_middle.astype(BF16)
    low_ref[...] = low
    near, far = low[:, :HALF], low[:, HALF:]
    d_low = (dot_nn(near, na_ref[...]) + dot_nn(far, fa_ref[...])).astype(BF16)
    d_high = (dot_nn(near, nb_ref[...]) + dot_nn(far, fb_ref[...])).astype(BF16)
    d0_ref[...], d1_ref[...] = d_low[:, :HEAD_COLS], d_low[:, HEAD_COLS:]
    d2_ref[...], d3_ref[...] = d_high[:, :HEAD_COLS], d_high[:, HEAD_COLS:]
    add_sums(sum_ref, low.astype(F32), g_two * unit, g_two)


def last_kernel(*refs):
    grads = refs[:12]
    gmid_ref, tokens_ref, an_ref, af_ref, bn_ref, bf_ref, vec_ref, order_ref, grad_ref, sum_ref = refs[12:]

    def back(low_w, high_w):
        total = 0.0
        for first, w_ref in ((0, low_w), (6, high_w)):
            for i in range(3):
                g = jnp.concatenate([grads[first + i][...], grads[first + 3 + i][...]], axis=1)
                total = total + dot_nt(g, w_ref[:, i * HALF : i * HALF + HALF])
        return total

    g_one = jnp.concatenate([back(an_ref, bn_ref), back(af_ref, bf_ref)], axis=1)
    unit, inv_std = unit_norm(tokens_ref[...].astype(F32))
    grad = gmid_ref[...].astype(F32) + unit_norm_back(g_one * vec_ref[0:1, :], unit, inv_std)
    grad_ref[...] = dot_nt(grad.astype(BF16), order_ref[...]).astype(BF16)
    add_sums(sum_ref, g_one * unit, g_one)


def weight_grads(half, steps, received=None):
    sources, arrays = [], []
    for x, gs in steps:
        if not any(x is s for s in sources):
            sources.append(x)
        for g, _, _ in gs:
            if not any(g is a for a in arrays):
                arrays.append(g)
    tile = sum(width for _, width, _ in steps[0][1])
    refs_of, specs, operands = [], [], []
    for j, (x, gs) in enumerate(steps):
        mine = []
        for g, width, at in gs:
            found = next((i for i, o in enumerate(operands) if o[0] is g and o[1] == width), None)
            if found is None:
                operands.append((g, width, {}))
                found = len(operands) - 1
            operands[found][2][j] = at
            mine.append(found)
        refs_of.append(mine)
    for g, width, places in operands:
        known = sorted(places.items())

        def index(j, known=known):
            at = known[0][1]
            for step, place in known[1:]:
                at = jnp.where(j >= step, place, at)
            return 0, at

        specs.append(pl.BlockSpec((ROWS, width), index))
    plus = [] if received is None else [received]

    def kernel(*refs):
        xs, gs = refs[: len(sources)], refs[len(sources) : len(sources) + len(operands)]
        out_ref, turned, last = refs[-3:]
        step = pl.program_id(0)
        for j, (x, _) in enumerate(steps):
            source = next(i for i, s in enumerate(sources) if s is x)
            fresh = j == 0 or steps[j - 1][0] is not x

            @pl.when(step == j)
            def _(j=j, source=source, fresh=fresh):
                if fresh:
                    turned[...] = xs[source][0:KEYS, :].T
                    last[...] = xs[source][KEYS:ROWS, :].astype(F32).T
                parts = [gs[r] for r in refs_of[j]]
                main = jnp.concatenate([p[0:KEYS, :] for p in parts], axis=1)
                row = jnp.concatenate([p[KEYS:ROWS, :].astype(F32)[0:1] for p in parts], axis=1)
                out = dot_nn(turned[...], main) + last[:, 0:1] * row
                if plus:
                    out = out + refs[len(sources) + len(operands)][...].astype(F32)
                out_ref[...] = out.astype(BF16)

    block = pl.BlockSpec((HALF, tile), lambda j: (0, j))
    columns = len(steps) * tile
    return pl.pallas_call(
        kernel,
        grid=(len(steps),),
        in_specs=[pl.BlockSpec((ROWS, HALF), lambda j: (0, half), pipeline_mode=pl.Buffered(1)) for _ in sources]
        + specs
        + [block] * len(plus),
        out_specs=block,
        out_shape=jax.ShapeDtypeStruct((HALF, columns), BF16),
        scratch_shapes=[pltpu.VMEM((HALF, KEYS), BF16), pltpu.VMEM((HALF, ROWS - KEYS), F32)],
        compiler_params=pltpu.CompilerParams(vmem_limit_bytes=48 << 20),
        cost_estimate=cost_of(
            flops=ROWS * WIDTH * columns, bytes_accessed=3 * ROWS * columns, transcendentals=0
        ),
        name="weight_grads",
    )(*sources, *[g for g, _, _ in operands], *plus)


def pair_tables(coords):
    lane = jnp.arange(128)
    freqs = 10000.0 ** (-(lane % 16).astype(F32) / 16.0)
    along_rows = (lane % 64 < 32)[None, :]
    places = jnp.where(along_rows, coords[:, 0:1], coords[:, 1:2]).astype(F32)
    angles = jnp.pad(places * freqs[None, :], ((0, ROWS - KEYS), (0, 0)))
    cosines, sines = jnp.cos(angles), jnp.sin(angles)
    even = (lane % 32 < 16)[None, :]
    return cosines, jnp.where(even, -sines, 0.0), jnp.where(even, 0.0, sines)


def feature_order(me):
    natural = lax.broadcasted_iota(jnp.int32, (WIDTH, WIDTH), 0)
    place = lax.broadcasted_iota(jnp.int32, (WIDTH, WIDTH), 1)
    block = place // 32
    owner = (
        (block // 16) * BIT_CORE
        + (block // 8 % 2) * BIT_X
        + (block // 4 % 2) * BIT_Y
        + (block // 2 % 2) * BIT_Z1
        + (block % 2) * BIT_Z0
    ) ^ me
    return (natural == owner * 32 + place % 32).astype(BF16)


def paired_device(
    patch_in, cls_in, d_patch, d_cls, image_valid, patch_coords,
    w_query, w_key, w_value, w_gate, w_up, w_out, w_down, layer_vectors, ffn_vectors,
):
    SENT.clear()
    me, pos = lax.axis_index(BOTH), lax.axis_index("ctx")
    hidden = w_gate.shape[1]
    wide = (hidden + 255) // 256 * 256
    extra = ((0, 0), (0, wide - hidden))

    def own_image(patches, classes, *deps):
        near = lax.dynamic_index_in_dim(patches, pos, 0, keepdims=False)
        sent = after(lax.dynamic_index_in_dim(patches, 1 - pos, 0, keepdims=False), *deps)
        far = swap_over(sent, BIT_X)
        class_row = lax.dynamic_index_in_dim(classes, pos, 0)
        return joined(near, far, jnp.pad(class_row, ((0, ROWS - KEYS - 1), (0, 0)))), far

    def to_pair(rows, far):
        near = rows[:512]
        is_first = pos == 0
        near_class, far_class = rows[KEYS], far[512]
        patches = jnp.where(is_first, jnp.stack([near, far[:512]]), jnp.stack([far[:512], near]))
        classes = jnp.where(is_first, jnp.stack([near_class, far_class]), jnp.stack([far_class, near_class]))
        return patches, classes

    vectors_local = jnp.pad(layer_vectors.T, ((0, 0), (0, 120)))
    low_heads = [w[:, :HALF] for w in (w_query, w_key, w_value)]
    high_heads = [w[:, HALF:] for w in (w_query, w_key, w_value)]
    g_low = Gather(joined(*low_heads, vectors_local, axis=1))
    g_high = Gather(joined(*high_heads, w_out.T, axis=1))
    g_gate = Gather(jnp.pad(w_gate, extra))
    g_up = Gather(jnp.pad(w_up, extra))
    g_down = Gather(jnp.pad(w_down.T, extra))

    image_rows, image_far = own_image(patch_in, cls_in)
    coords = joined(patch_coords, swap_over(patch_coords, BIT_X))
    order = feature_order(me)
    tables = pair_tables(coords)
    keep = lax.dynamic_index_in_dim(image_valid, pos, 0, keepdims=False).astype(F32)
    keep = jnp.full((8, 128), keep, F32)
    ffn = jnp.pad(ffn_vectors.astype(F32), ((0, 4), (0, wide - hidden)))

    z_one = g_low.along_z0()
    z_low = g_low.along_z1()
    g_high.along_z0(z_one)
    xy_low = g_low.along_xy()
    z_high = g_high.along_z1(z_low)
    corner_low = g_low.corners(image_far)
    z_one = g_gate.along_z0(z_high)
    xy_high = g_high.along_xy(xy_low)
    near_low = g_low.whole(z_high)

    gate = near_low, g_low.far, image_rows, z_one
    z_gate = g_gate.along_z1(gate)
    vectors, head_biases = gathered_vectors(near_low, g_low.far, order)
    tokens, normed = over_rows(
        start_kernel, "start", [ready(image_rows, gate)], [order, vectors], [(WIDTH, BF16), (WIDTH, BF16)],
        flops=2_200_000_000,
    )

    def attend(block, gate):
        group = g_low if block < 2 else g_high
        return attention_forward(
            ready(normed, gate), group.near, group.far, head_biases, block, block % 2, tables
        )

    gate = normed, xy_high, z_gate
    z_up = g_up.along_z0(gate)
    corner_high = g_high.corners(gate)
    xy_gate = g_gate.along_xy(gate)
    heads = [attend(0, gate)]

    gate = heads[0][3], corner_high, xy_gate, z_up
    near_high = g_high.whole(gate)
    corner_gate = g_gate.corners(gate)
    z_up = g_up.along_z1(gate)
    heads.append(attend(1, gate))

    gate = heads[1][3], g_high.far, corner_gate, z_up
    near_gate = g_gate.whole(gate)
    xy_up = g_up.along_xy(gate)
    z_down = g_down.along_z0(gate)
    heads.append(attend(2, gate))

    gate = heads[2][3], xy_up, g_gate.far, z_down
    corner_up = g_up.corners(gate)
    z_down = g_down.along_z1(gate)
    heads.append(attend(3, gate))

    gate = heads[3][3], corner_up, z_down
    near_up = g_up.whole(gate)
    xy_down = g_down.along_xy(gate)
    out_w = [((w, (HALF, HALF), 3 + i)) for w in (near_high, g_high.far) for i in range(2)]
    attended = [h[3] for h in heads]
    middle, normed_two = over_rows(
        middle_kernel, "middle", attended + [ready(tokens, gate)], out_w + [vectors],
        [(WIDTH, BF16), (WIDTH, BF16)], flops=2_200_000_000, step=520,
    )

    gate = normed_two, g_up.far, xy_down
    corner_down = g_down.corners(gate)
    grad_image_rows, grad_far = own_image(d_patch, d_cls, gate)
    gate_up = [near_gate, g_gate.far, near_up, g_up.far]
    gate_act, up_act, inner, stats = over_rows(
        functools.partial(hidden_kernel, hidden=hidden), "hidden", [ready(normed_two, gate)],
        gate_up + [ffn], [(wide, BF16), (wide, BF16), (wide, BF16), (128, F32)], flops=12_000_000_000,
    )

    gate = inner, corner_down, grad_far
    near_down = g_down.whole(gate)
    down_w = [near_down, g_down.far]
    (out_rows,) = over_rows(
        result_kernel, "result", [inner, ready(middle, gate)], down_w + [vectors, order, keep],
        [(WIDTH, BF16)], flops=8_000_000_000, step=520,
    )

    gate = out_rows
    far_rows = swap_over(after(out_rows, gate)[HALF:], BIT_X)
    branch, d_gate, d_up, wide_sums, branch_sums = over_rows(
        functools.partial(hidden_back_kernel, hidden=hidden), "hidden_back",
        [ready(grad_image_rows, gate), gate_act, up_act, stats], [order, keep] + down_w + [ffn],
        [(WIDTH, BF16), (wide, BF16), (wide, BF16)], [wide, WIDTH], flops=8_000_000_000,
    )

    gate = wide_sums, far_rows
    outs = to_pair(out_rows, far_rows)
    all_sums = lax.all_gather(wide_sums, BOTH)
    part_width = wide // 2
    down, second, low, high = Scatter(), Scatter(), Scatter(), Scatter()
    late = ready(normed_two, gate)
    second_steps = [(late, [(g, part_width, i)]) for g in (d_gate, d_up) for i in range(2)]
    second_far = weight_grads(1, second_steps)

    gate = second_far
    second_stage = second.over_core(second_far, gate)
    late = ready(branch, gate)
    down_steps = [(late, [(inner, part_width, i)]) for i in range(2)]
    down_far = weight_grads(1, down_steps)

    gate = down_far, second_stage
    down_stage = down.over_core(down_far, gate)
    late = ready(normed_two, gate)
    second_total = weight_grads(0, [(late, gs) for _, gs in second_steps], second_stage)

    gate = second_total, down_stage
    second_stage = second.corners(second_total, gate)
    late = ready(branch, gate)
    down_total = weight_grads(0, [(late, gs) for _, gs in down_steps], down_stage)

    gate = down_total, second_stage
    second_stage = second.sides(gate)
    att_low, *att_grads, middle_sums = over_rows(
        middle_back_kernel, "middle_back", [d_gate, d_up, branch, ready(middle, gate)],
        gate_up + out_w + [vectors], [(WIDTH, BF16)] + [(HEAD_COLS, BF16)] * 4, [WIDTH],
        flops=14_000_000_000, step=520,
    )

    def attend_back(block, gate):
        return attention_backward(*heads[block], ready(att_grads[block], gate), tables)

    gate = att_low, second_stage
    second_stage, down_stage = second.along_z1(gate), down.corners(down_total, gate)
    parts = [attend_back(0, gate)]

    gate = parts[0][0], second_stage, down_stage
    gate_up_grad, down_stage = second.along_z0(gate), down.sides(gate)
    parts.append(attend_back(1, gate))

    def pieces(*arrays):
        return [(a, HEAD_COLS, 0) for a in arrays]

    gate = parts[1][0], gate_up_grad, down_stage
    down_stage = down.along_z1(gate)
    late, late_two = ready((att_low, normed), gate)
    grads = [g for part in parts for g in part[:3]]
    low_steps = [(late, pieces(*attended[2 * i : 2 * i + 2])) for i in range(2)]
    low_steps += [(late_two, pieces(*grads[2 * i : 2 * i + 2])) for i in range(3)]
    low_far = weight_grads(1, low_steps)

    gate = low_far, down_stage
    low_stage, down_grad = low.over_core(low_far, gate), down.along_z0(gate)
    parts.append(attend_back(2, gate))

    gate = parts[2][0], low_stage, down_grad
    late, late_two = ready((att_low, normed), gate)
    low_total = weight_grads(
        0, [(late if i < 2 else late_two, gs) for i, (_, gs) in enumerate(low_steps)], low_stage
    )

    gate = low_total
    low_stage = low.corner(low_total, gate)
    parts.append(attend_back(3, gate))

    gate = parts[3][0], low_stage
    low_stage = low.sides(gate)
    late = ready(normed, gate)
    grads = [g for part in parts[2:] for g in part[:3]]
    high_steps = [(late, pieces(*grads[2 * i : 2 * i + 2])) for i in range(3)]
    high_far = weight_grads(1, high_steps)
    high_stage = high.over_core(high_far)

    def last_rows(gate, first, count):
        return over_rows(
            last_kernel, "last",
            [g for part in parts for g in part[:3]] + [ready(att_low, gate), tokens],
            [(near_low, (HALF, 3 * HALF), 0), (g_low.far, (HALF, 3 * HALF), 0)]
            + [(near_high, (HALF, 3 * HALF), 0), (g_high.far, (HALF, 3 * HALF), 0), vectors, order],
            [(WIDTH, BF16)], [WIDTH], flops=4_500_000_000, step=count, only=first,
        )

    far_part, far_sums = last_rows(high_far, HALF, ROWS - HALF)

    gate = far_part, high_stage, low_stage
    low_stage = low.along_z1(gate)
    late = ready(normed, gate)
    high_total = weight_grads(0, [(late, gs) for _, gs in high_steps], high_stage)

    gate = high_total
    high.total = high_total
    high_stage = high.over_x(gate)
    near_part, near_sums = last_rows(gate, 0, HALF)

    gate = near_part, low_stage, high_stage
    far_rows = swap_over(after(far_part, gate), BIT_X)
    high.over_y(gate)
    low_grad = low.along_z0(gate)
    first_sums = far_sums + after(near_sums, gate)
    high.along_z1()
    high_grad = high.along_z0()
    patch_grad, cls_grad = to_pair(joined(near_part, far_part), far_rows)
    ffn_grads = jnp.sum(after(all_sums, parts[1][0]), axis=0)[:4, :hidden]
    head_sums = jnp.dot(
        joined(*[part[3][:2] for part in parts], axis=1), order.astype(F32), precision=lax.Precision.HIGHEST
    )
    vector_grads = scatter_small(
        joined(first_sums[:2], head_sums, middle_sums[:3], branch_sums[:1]).T
    )
    blocks = [low_grad[:, WIDTH + i * HEAD_COLS :][:, :HEAD_COLS] for i in range(6)]
    blocks += [high_grad[:, i * HEAD_COLS :][:, :HEAD_COLS] for i in range(6)]
    query_grad, key_grad, value_grad = (joined(*blocks[i::3], axis=1) for i in range(3))
    return (
        outs[0],
        outs[1],
        patch_grad,
        cls_grad,
        query_grad,
        key_grad,
        value_grad,
        gate_up_grad[:, :hidden],
        gate_up_grad[:, wide : wide + hidden],
        low_grad[:, :WIDTH].T,
        down_grad[:, :hidden].T,
        vector_grads.T,
        ffn_grads,
    )


def solution(mesh):
    in_specs = (
        P("dp", "ctx", None),
        P("dp", None),
        P("dp", "ctx", None),
        P("dp", None),
        P("dp"),
        P("ctx", None),
        P(("dp", "ctx"), None),
        P(("dp", "ctx"), None),
        P(("dp", "ctx"), None),
        P(("dp", "ctx"), None),
        P(("dp", "ctx"), None),
        P(None, ("dp", "ctx")),
        P(None, ("dp", "ctx")),
        P(None, ("dp", "ctx")),
        P(),
    )
    out_specs = (
        P("dp", "ctx", None),
        P("dp", None),
        P("dp", "ctx", None),
        P("dp", None),
        P(("dp", "ctx"), None),
        P(("dp", "ctx"), None),
        P(("dp", "ctx"), None),
        P(("dp", "ctx"), None),
        P(("dp", "ctx"), None),
        P(None, ("dp", "ctx")),
        P(None, ("dp", "ctx")),
        P(None, ("dp", "ctx")),
        P(),
    )
    sizes = dict(mesh.shape)
    pairs = sizes["dp"] == 16 and sizes["ctx"] == 2
    body = paired_device if pairs else on_device
    return jax.shard_map(
        body, mesh=mesh, in_specs=in_specs, out_specs=out_specs, check_vma=False
    )
```

```python
import functools
import math

import jax
import jax.numpy as jnp
from jax import lax
from jax.experimental import pallas as pl
from jax.experimental.pallas import tpu as pltpu
from jax.sharding import PartitionSpec as P

HD = 64
MICRO = 2


epsilon = 1e-06


def layer_norm(values, gain, shift):
    centred = values - jnp.mean(values, axis=-1, keepdims=True)
    inv_std = lax.rsqrt(jnp.mean(centred * centred, axis=-1, keepdims=True) + epsilon)
    unit_rows = centred * inv_std
    return (unit_rows * gain + shift, unit_rows, inv_std)


def norm_back(grad_out, gain, unit_rows, inv_std, row_mask):
    scaled = grad_out * gain
    grad_in = inv_std * (
        scaled
        - jnp.mean(scaled, axis=-1, keepdims=True)
        - unit_rows * jnp.mean(scaled * unit_rows, axis=-1, keepdims=True)
    )
    weighted = grad_out * row_mask
    return (grad_in, jnp.sum(weighted * unit_rows, axis=(0, 1)), jnp.sum(weighted, axis=(0, 1)))


def rotary_tables(coords):
    freqs = 10000.0 ** (-jnp.arange(16).astype(jnp.float32) / 16.0)
    along_rows = coords[:, 0:1].astype(jnp.float32) * freqs[None, :]
    along_cols = coords[:, 1:2].astype(jnp.float32) * freqs[None, :]
    angles = jnp.concatenate([along_rows, along_rows, along_cols, along_cols], axis=1)
    cosines = jnp.concatenate([jnp.ones((1, 64), jnp.float32), jnp.cos(angles)], axis=0)
    sines = jnp.concatenate([jnp.zeros((1, 64), jnp.float32), jnp.sin(angles)], axis=0)
    return (cosines, sines)


def rotate(values, cosines, sines):
    swapped = jnp.concatenate(
        [-values[..., 16:32], values[..., 0:16], -values[..., 48:64], values[..., 32:48]], axis=-1
    )
    return values * cosines[:, None, :] + swapped * sines[:, None, :]


def unrotate(grads, cosines, sines):
    with_sin = grads * sines[:, None, :]
    moved = jnp.concatenate(
        [with_sin[..., 16:32], -with_sin[..., 0:16], with_sin[..., 48:64], -with_sin[..., 32:48]],
        axis=-1,
    )
    return grads * cosines[:, None, :] + moved


def project(rows_in, weight):
    return jnp.einsum("brd,de->bre", rows_in, weight, preferred_element_type=jnp.float32)


def project_back(grads, weight):
    return jnp.einsum("bre,de->brd", grads, weight, preferred_element_type=jnp.float32)


def weight_grad(rows_in, grads):
    return jnp.einsum("brd,bre->de", rows_in, grads, preferred_element_type=jnp.float32)


def fetch_forward(w_query, w_key, w_value, w_gate, w_up, w_out, w_down, layer_vectors):
    first_group = (
        lax.all_gather(w_query, ("dp", "ctx"), axis=0, tiled=True),
        lax.all_gather(w_key, ("dp", "ctx"), axis=0, tiled=True),
        lax.all_gather(w_value, ("dp", "ctx"), axis=0, tiled=True),
        lax.all_gather(w_gate, ("dp", "ctx"), axis=0, tiled=True),
        lax.all_gather(w_up, ("dp", "ctx"), axis=0, tiled=True),
    )
    second_group = (
        lax.all_gather(w_out, ("dp", "ctx"), axis=1, tiled=True),
        lax.all_gather(w_down, ("dp", "ctx"), axis=1, tiled=True),
        lax.all_gather(layer_vectors, ("dp", "ctx"), axis=1, tiled=True),
    )
    return tuple(first_group) + tuple(second_group)


def fetch_backward(w_query, w_key, w_value, w_gate, w_up, w_out, w_down, layer_vectors):
    first_group = (
        lax.all_gather(w_query, ("dp", "ctx"), axis=0, tiled=True),
        lax.all_gather(w_key, ("dp", "ctx"), axis=0, tiled=True),
        lax.all_gather(w_value, ("dp", "ctx"), axis=0, tiled=True),
        lax.all_gather(w_gate, ("dp", "ctx"), axis=0, tiled=True),
        lax.all_gather(w_up, ("dp", "ctx"), axis=0, tiled=True),
    )
    second_group = (
        lax.all_gather(w_out, ("dp", "ctx"), axis=1, tiled=True),
        lax.all_gather(w_down, ("dp", "ctx"), axis=1, tiled=True),
        lax.all_gather(layer_vectors, ("dp", "ctx"), axis=1, tiled=True),
    )
    return tuple(first_group) + tuple(second_group)


def head_forward(item):
    block_of_queries, block_of_keys, block_of_values = item
    logit_scores = jnp.einsum(
        "wey,wmy->wem", block_of_queries, block_of_keys, preferred_element_type=jnp.float32
    )
    row_peak = jnp.max(logit_scores, axis=-1, keepdims=True)
    shifted = jnp.exp(logit_scores - row_peak)
    denominator = jnp.sum(shifted, axis=-1, keepdims=True)
    reduced_probabilities = (shifted / denominator).astype(jnp.bfloat16)
    blended_values = jnp.einsum(
        "sce,sem->scm", reduced_probabilities, block_of_values, preferred_element_type=jnp.float32
    )
    return (blended_values, (row_peak + jnp.log(denominator))[..., 0])


def forward_pass(tokens, weights, ffn_vec, cosines, sines):
    w_query, w_key, w_value, w_gate, w_up, w_out, w_down, vectors_low = weights
    vectors = vectors_low.astype(jnp.float32)
    batch, row_count, model_width = tokens.shape
    heads = model_width // HD
    normed, unit_one, std_one = layer_norm(tokens, vectors[0], vectors[1])
    normed_low = normed.astype(jnp.bfloat16)
    queries = project(normed_low, w_query) + vectors[2]
    keys_raw = project(normed_low, w_key)
    values_low = (project(normed_low, w_value) + vectors[3]).astype(jnp.bfloat16)
    q_rot = (
        rotate(queries.reshape(batch, row_count, heads, HD), cosines, sines) * HD ** (-0.5)
    ).astype(jnp.bfloat16)
    k_flat = (
        rotate(keys_raw.reshape(batch, row_count, heads, HD), cosines, sines)
        .astype(jnp.bfloat16)
        .reshape(batch, row_count, model_width)
    )
    far_keys, far_values = (
        lax.all_gather(k_flat[:, 1:], "ctx", axis=1, tiled=True),
        lax.all_gather(values_low[:, 1:], "ctx", axis=1, tiled=True),
    )
    all_keys = jnp.concatenate([k_flat[:, :1], far_keys], axis=1)
    all_values = jnp.concatenate([values_low[:, :1], far_values], axis=1)
    length = all_keys.shape[1]
    head_queries = q_rot.transpose(2, 0, 1, 3)
    head_keys = all_keys.reshape(batch, length, heads, HD).transpose(2, 0, 1, 3)
    head_values = all_values.reshape(batch, length, heads, HD).transpose(2, 0, 1, 3)
    head_out, log_sums = lax.map(head_forward, (head_queries, head_keys, head_values))
    attended = (
        head_out.transpose(1, 2, 0, 3).reshape(batch, row_count, model_width).astype(jnp.bfloat16)
    )
    middle = tokens + (project(attended, w_out) + vectors[4])
    normed_two, unit_two, std_two = layer_norm(middle, vectors[5], vectors[6])
    normed_two_low = normed_two.astype(jnp.bfloat16)
    gate_proj = project(normed_two_low, w_gate) + ffn_vec[0]
    up_proj = project(normed_two_low, w_up) + ffn_vec[1]
    activated = jax.nn.silu(gate_proj)
    inner_act, unit_three, std_three = layer_norm(activated * up_proj, ffn_vec[2], ffn_vec[3])
    inner_low = inner_act.astype(jnp.bfloat16)
    result = middle + (project(inner_low, w_down) + vectors[7])
    saved = (
        normed_low,
        unit_one,
        std_one,
        head_queries,
        head_keys,
        head_values,
        log_sums,
        attended,
        unit_two,
        std_two,
        normed_two_low,
        gate_proj,
        up_proj,
        activated,
        unit_three,
        std_three,
        inner_low,
    )
    return (result, saved)


def backward_pass(grad_rows, weights, ffn_vec, cosines, sines, saved, row_mask):
    w_query, w_key, w_value, w_gate, w_up, w_out, w_down, vectors_low = weights
    vectors = vectors_low.astype(jnp.float32)
    (
        normed_low,
        unit_one,
        std_one,
        head_queries,
        head_keys,
        head_values,
        log_sums,
        attended,
        unit_two,
        std_two,
        normed_two_low,
        gate_proj,
        up_proj,
        activated,
        unit_three,
        std_three,
        inner_low,
    ) = saved
    batch, row_count, model_width = grad_rows.shape
    heads = model_width // HD
    reduced_mask = row_mask.astype(jnp.bfloat16)
    branch_low = grad_rows.astype(jnp.bfloat16)
    grad_down = weight_grad(inner_low, branch_low * reduced_mask)
    grad_inner = project_back(branch_low, w_down)
    grad_mix, gain_three, shift_three = norm_back(
        grad_inner, ffn_vec[2], unit_three, std_three, row_mask
    )
    sigmoid_gate = jax.nn.sigmoid(gate_proj)
    gate_low = (
        grad_mix * up_proj * sigmoid_gate * (1.0 + gate_proj * (1.0 - sigmoid_gate))
    ).astype(jnp.bfloat16)
    up_low = (grad_mix * activated).astype(jnp.bfloat16)
    grad_gate_w = weight_grad(normed_two_low * reduced_mask, gate_low)
    grad_up_w = weight_grad(normed_two_low * reduced_mask, up_low)
    grad_normed_two = project_back(gate_low, w_gate) + project_back(up_low, w_up)
    grad_mid_norm, gain_two, shift_two = norm_back(
        grad_normed_two, vectors[5], unit_two, std_two, row_mask
    )
    grad_middle = grad_rows + grad_mid_norm
    out_low = grad_middle.astype(jnp.bfloat16)
    grad_out_w = weight_grad(attended * reduced_mask, out_low)
    attended_grad = project_back(out_low, w_out).astype(jnp.bfloat16)
    head_grads = attended_grad.reshape(batch, row_count, heads, HD).transpose(2, 0, 1, 3)

    def head_backward(item):
        block_of_queries, block_of_keys, block_of_values, block_gradient, log_block = item
        logit_scores = jnp.einsum(
            "wey,wmy->wem", block_of_queries, block_of_keys, preferred_element_type=jnp.float32
        )
        attn_probs = jnp.exp(logit_scores - log_block[..., None])
        grad_probs = jnp.einsum(
            "wey,wmy->wem", block_gradient, block_of_values, preferred_element_type=jnp.float32
        )
        inner_sum = jnp.sum(attn_probs * grad_probs, axis=-1, keepdims=True)
        score_gradients = (attn_probs * (grad_probs - inner_sum)).astype(jnp.bfloat16)
        grad_query = jnp.einsum(
            "sce,sem->scm", score_gradients, block_of_keys, preferred_element_type=jnp.float32
        )
        grad_key = jnp.einsum(
            "ipz,iph->izh",
            score_gradients * reduced_mask,
            block_of_queries,
            preferred_element_type=jnp.float32,
        )
        grad_value = jnp.einsum(
            "ipz,iph->izh",
            attn_probs.astype(jnp.bfloat16) * reduced_mask,
            block_gradient,
            preferred_element_type=jnp.float32,
        )
        return (grad_query, grad_key, grad_value)

    grad_q_heads, grad_k_heads, grad_v_heads = lax.map(
        head_backward, (head_queries, head_keys, head_values, head_grads, log_sums)
    )
    length = head_keys.shape[2]
    grad_keys = grad_k_heads.transpose(1, 2, 0, 3).reshape(batch, length, model_width)
    grad_values = grad_v_heads.transpose(1, 2, 0, 3).reshape(batch, length, model_width)
    own_keys, own_values = (
        lax.psum_scatter(
            grad_keys[:, 1:].astype(jnp.bfloat16), "ctx", scatter_dimension=1, tiled=True
        ).astype(jnp.float32),
        lax.psum_scatter(
            grad_values[:, 1:].astype(jnp.bfloat16), "ctx", scatter_dimension=1, tiled=True
        ).astype(jnp.float32),
    )
    class_keys, class_values = lax.psum((grad_keys[:, :1], grad_values[:, :1]), "ctx")
    key_rows = jnp.concatenate([class_keys, own_keys], axis=1).reshape(batch, row_count, heads, HD)
    value_rows = jnp.concatenate([class_values, own_values], axis=1)
    key_low = (
        unrotate(key_rows, cosines, sines)
        .reshape(batch, row_count, model_width)
        .astype(jnp.bfloat16)
    )
    value_low = value_rows.astype(jnp.bfloat16)
    query_rows = grad_q_heads.transpose(1, 2, 0, 3)
    query_low = (
        (unrotate(query_rows, cosines, sines) * HD ** (-0.5))
        .reshape(batch, row_count, model_width)
        .astype(jnp.bfloat16)
    )
    grad_query_w = weight_grad(normed_low * reduced_mask, query_low)
    grad_key_w = weight_grad(normed_low * reduced_mask, key_low)
    grad_value_w = weight_grad(normed_low * reduced_mask, value_low)
    grad_normed = (
        project_back(query_low, w_query)
        + project_back(key_low, w_key)
        + project_back(value_low, w_value)
    )
    grad_in_norm, gain_one, shift_one = norm_back(
        grad_normed, vectors[0], unit_one, std_one, row_mask
    )
    grad_tokens = grad_middle + grad_in_norm

    def column_sum(rounded):
        return jnp.sum(rounded.astype(jnp.float32) * row_mask, axis=(0, 1))

    vector_grads = jnp.stack(
        [
            gain_one,
            shift_one,
            column_sum(query_low),
            column_sum(value_low),
            column_sum(out_low),
            gain_two,
            shift_two,
            column_sum(branch_low),
        ]
    )
    ffn_grads = jnp.stack([column_sum(gate_low), column_sum(up_low), gain_three, shift_three])
    return (
        grad_tokens,
        (
            (grad_query_w, grad_key_w, grad_value_w, grad_gate_w, grad_up_w),
            (grad_out_w, grad_down, vector_grads),
            ffn_grads,
        ),
    )


def on_device(
    patch_in,
    cls_in,
    d_patch,
    d_cls,
    image_valid,
    patch_coords,
    w_query,
    w_key,
    w_value,
    w_gate,
    w_up,
    w_out,
    w_down,
    layer_vectors,
    ffn_vectors,
):
    images, patch_rows, model_width = patch_in.shape
    group_size = images // MICRO
    cosines, sines = rotary_tables(patch_coords)
    first_flag = (lax.axis_index("ctx") == 0).astype(jnp.float32)
    row_weight = jnp.concatenate([first_flag[None], jnp.ones((patch_rows,), jnp.float32)])
    row_mask = row_weight[None, :, None]
    ffn_vec = ffn_vectors.astype(jnp.float32)
    keep_mask = image_valid.astype(jnp.float32)
    results = []
    totals = None
    for micro_step in range(MICRO):
        first_image = micro_step * group_size
        last_image = first_image + group_size
        tokens = jnp.concatenate(
            [cls_in[first_image:last_image, None, :], patch_in[first_image:last_image]], axis=1
        ).astype(jnp.float32)
        weights = fetch_forward(w_query, w_key, w_value, w_gate, w_up, w_out, w_down, layer_vectors)
        result, saved = forward_pass(tokens, weights, ffn_vec, cosines, sines)
        keep_rows = keep_mask[first_image:last_image][:, None, None]
        grad_rows = (
            jnp.concatenate(
                [d_cls[first_image:last_image, None, :], d_patch[first_image:last_image]], axis=1
            ).astype(jnp.float32)
            * keep_rows
        )
        back_weights = fetch_backward(
            w_query, w_key, w_value, w_gate, w_up, w_out, w_down, layer_vectors
        )
        grad_tokens, weight_grads = backward_pass(
            grad_rows, back_weights, ffn_vec, cosines, sines, saved, row_mask
        )
        if totals is None:
            totals = weight_grads
        else:
            totals = jax.tree.map(lambda first, second: first + second, totals, weight_grads)
        results.append(
            ((result * keep_rows).astype(jnp.bfloat16), grad_tokens.astype(jnp.bfloat16))
        )
    out_rows = jnp.concatenate([entry[0] for entry in results], axis=0)
    grad_out_rows = jnp.concatenate([entry[1] for entry in results], axis=0)
    in_grads, out_grads, ffn_total = totals
    owned_in = (
        lax.psum_scatter(in_grads[0], ("dp", "ctx"), scatter_dimension=0, tiled=True),
        lax.psum_scatter(in_grads[1], ("dp", "ctx"), scatter_dimension=0, tiled=True),
        lax.psum_scatter(in_grads[2], ("dp", "ctx"), scatter_dimension=0, tiled=True),
        lax.psum_scatter(in_grads[3], ("dp", "ctx"), scatter_dimension=0, tiled=True),
        lax.psum_scatter(in_grads[4], ("dp", "ctx"), scatter_dimension=0, tiled=True),
    )
    owned_out = (
        lax.psum_scatter(out_grads[0], ("dp", "ctx"), scatter_dimension=1, tiled=True),
        lax.psum_scatter(out_grads[1], ("dp", "ctx"), scatter_dimension=1, tiled=True),
        lax.psum_scatter(out_grads[2], ("dp", "ctx"), scatter_dimension=1, tiled=True),
    )
    ffn_summed = lax.psum(ffn_total, ("dp", "ctx"))
    return (
        out_rows[:, 1:],
        out_rows[:, 0],
        grad_out_rows[:, 1:],
        grad_out_rows[:, 0],
        owned_in[0],
        owned_in[1],
        owned_in[2],
        owned_in[3],
        owned_in[4],
        owned_out[0],
        owned_out[1],
        owned_out[2],
        ffn_summed,
    )


BOTH = ("dp", "ctx")
BIT_X, BIT_CORE, BIT_Y, BIT_Z0, BIT_Z1 = 1, 2, 4, 16, 8
ROWS = 1040
KEYS = 1024
WIDTH = 1024
HALF = 512
HEAD_COLS = 256
STEP = 208
LOG2E = math.log2(math.e)
COST = 4
F32 = jnp.float32
BF16 = jnp.bfloat16


SENT = []


def swap_over(value, bit):
    value = lax.optimization_barrier(value)
    SENT.append(value)
    count = lax.axis_size(BOTH)
    return lax.ppermute(value, BOTH, [(i, i ^ bit) for i in range(count)])


def joined(*parts, axis=0):
    return jnp.concatenate(parts, axis=axis)


def after(value, *deps):
    return lax.optimization_barrier((value,) + deps)[0]


def ready(value, *deps):
    corners = [sum(v[0:1, 0:1].astype(F32) for v in SENT)] if SENT else []
    SENT.clear()
    return after(value, *deps, *corners)


def dot_nn(a, b):
    return lax.dot_general(a, b, (((1,), (0,)), ((), ())), preferred_element_type=F32)


def dot_nt(a, b):
    return lax.dot_general(a, b, (((1,), (1,)), ((), ())), preferred_element_type=F32)


def dot_tn(a, b):
    return lax.dot_general(a, b, (((0,), (0,)), ((), ())), preferred_element_type=F32)


def cost_of(flops, bytes_accessed, transcendentals):
    return pl.CostEstimate(
        flops=int(COST * flops), bytes_accessed=int(COST * bytes_accessed), transcendentals=int(COST * transcendentals)
    )


def pack_rows(*parts):
    total, columns = sum(p.shape[0] for p in parts), parts[0].shape[1]
    blocks = columns // 128
    steps = next(n for n in (4, 5, 3, 2, 1) if blocks % n == 0)
    tile = columns // steps

    def kernel(*refs):
        out, start = refs[len(parts)], 0
        for ref in refs[: len(parts)]:
            out[start : start + ref.shape[0], :] = ref[...]
            start += ref.shape[0]

    return pl.pallas_call(
        kernel,
        grid=(steps,),
        in_specs=[pl.BlockSpec((p.shape[0], tile), lambda j: (0, j)) for p in parts],
        out_specs=pl.BlockSpec((total, tile), lambda j: (0, j)),
        out_shape=jax.ShapeDtypeStruct((total, columns), parts[0].dtype),
        compiler_params=pltpu.CompilerParams(vmem_limit_bytes=32 << 20),
        cost_estimate=cost_of(flops=0, bytes_accessed=4 * total * columns, transcendentals=0),
        name="pack_rows",
    )(*parts)


class Gather:
    def __init__(self, local):
        self.part = local

    def along_z0(self, *deps):
        part = after(self.part, *deps)
        far = swap_over(part, BIT_Z0)
        self.part = joined(part, far)
        return far

    def along_z1(self, *deps):
        part = after(self.part, *deps)
        far = swap_over(part, BIT_Z1)
        self.part = joined(part, far)
        return far

    def along_xy(self, *deps):
        part = after(self.part, *deps)
        self.over = swap_over(part, BIT_X), swap_over(part, BIT_Y)
        return self.over

    def corners(self, *deps):
        over_x, over_y = after(self.over, *deps)
        self.corner = swap_over(over_y[:64], BIT_X), swap_over(over_x[64:], BIT_Y)
        return self.corner

    def whole(self, *deps):
        parts = after((self.part, self.over, self.corner), *deps)
        self.near = pack_rows(parts[0], parts[1][1], parts[1][0], *parts[2])
        self.far = swap_over(self.near, BIT_CORE)
        return self.near


def rounded_sum(*terms):
    total = terms[0].astype(F32)
    for term in terms[1:]:
        total = total + term.astype(F32)
    return total.astype(BF16)


class Scatter:
    def over_core(self, far, *deps):
        return swap_over(after(far, *deps), BIT_CORE)

    def corner(self, total, *deps):
        self.total = after(total, *deps)
        self.to_x = rounded_sum(self.total[256:384], swap_over(self.total[384:], BIT_Y))
        self.to_y = self.total[128:256]
        return self.to_x

    def corners(self, total, *deps):
        self.total = total = after(total, *deps)
        from_x, from_y = swap_over(total[384:448], BIT_X), swap_over(total[448:512], BIT_Y)
        self.to_y = joined(rounded_sum(total[128:192], from_x), total[192:256])
        self.to_x = joined(total[256:320], rounded_sum(total[320:384], from_y))
        return self.to_x, self.to_y

    def sides(self, *deps):
        to_x, to_y = after((self.to_x, self.to_y), *deps)
        self.total = rounded_sum(self.total[:128], swap_over(to_y, BIT_Y), swap_over(to_x, BIT_X))
        return self.total

    def over_y(self, *deps):
        total = after(self.total, *deps)
        kept, sent = joined(total[:128], total[256:384]), joined(total[128:256], total[384:])
        self.total = rounded_sum(kept, swap_over(sent, BIT_Y))
        return self.total

    def over_x(self, *deps):
        total = after(self.total, *deps)
        self.total = rounded_sum(total[:128], swap_over(total[128:], BIT_X))
        return self.total

    def along_z1(self, *deps):
        total = after(self.total, *deps)
        self.total = rounded_sum(total[:64], swap_over(total[64:], BIT_Z1))
        return self.total

    def along_z0(self, *deps):
        total = after(self.total, *deps)
        return total[:32].astype(F32) + swap_over(total[32:], BIT_Z0).astype(F32)


def scatter_small(value):
    for rows, bit in ((512, BIT_CORE), (256, BIT_X), (128, BIT_Y), (64, BIT_Z1), (32, BIT_Z0)):
        value = value[:rows] + swap_over(value[rows:], bit)
    return value


def rotate_lanes(x, cosines, sines_up, sines_down):
    width = x.shape[1]
    return x * cosines + pltpu.roll(x, width - 16, 1) * sines_up + pltpu.roll(x, 16, 1) * sines_down


def twice(table):
    return jnp.concatenate([table, table], axis=1)


def attention_kernel(
    x_ref, qn_ref, qf_ref, kn_ref, kf_ref, vn_ref, vf_ref, b_ref, c_ref, s1_ref, s2_ref,
    q_ref, k_ref, v_ref, o_ref, l_ref
):
    def project(near_ref, far_ref):
        return dot_nn(x_ref[:, :HALF], near_ref[...]) + dot_nn(x_ref[:, HALF:], far_ref[...])

    c, s1, s2 = twice(c_ref[...]), twice(s1_ref[...]), twice(s2_ref[...])
    q = project(qn_ref, qf_ref) + b_ref[2:3, :]
    q_ref[...] = (rotate_lanes(q, c, s1, s2) * (LOG2E / 8)).astype(BF16)
    k_ref[...] = rotate_lanes(project(kn_ref, kf_ref), c, s1, s2).astype(BF16)
    v_ref[...] = (project(vn_ref, vf_ref) + b_ref[3:4, :]).astype(BF16)
    lane = lax.broadcasted_iota(jnp.int32, (1, 128), 1)
    low_half = lane < 64

    stats = jnp.zeros((ROWS, 128), F32)
    for pair in range(2):
        cols = slice(pair * 128, pair * 128 + 128)
        q_pair = q_ref[:, cols]
        k_pair, v_pair = k_ref[0:KEYS, cols], v_ref[0:KEYS, cols]
        k_class = k_ref[KEYS : KEYS + 16, cols].astype(F32)[0:1]
        v_class = v_ref[KEYS : KEYS + 16, cols].astype(F32)[0:1]
        product = q_pair.astype(F32) * k_class
        outs = []
        for h in range(2):
            own = low_half if h == 0 else ~low_half
            scores = dot_nt(jnp.where(own, q_pair, jnp.zeros_like(q_pair)), k_pair)
            class_score = jnp.sum(jnp.where(own, product, 0.0), axis=1, keepdims=True)
            peak = jnp.maximum(jnp.max(scores, axis=1, keepdims=True), class_score)
            p = jnp.exp2(scores - peak)
            class_p = jnp.exp2(class_score - peak)
            total = jnp.sum(p, axis=1, keepdims=True) + class_p
            out = dot_nn(p.astype(BF16), v_pair) + class_p * v_class
            outs.append(out * (1.0 / total))
            stats = jnp.where(lane == pair * 2 + h, peak + jnp.log2(total), stats)
        o_ref[:, cols] = jnp.where(low_half, outs[0], outs[1]).astype(BF16)
    l_ref[...] = stats.T[0:8, :]


def attention_forward(x, near, far, biases, head_block, at, tables):
    def block(index):
        return pl.BlockSpec((HALF, HEAD_COLS), lambda j: (0, index))

    def whole(a):
        return pl.BlockSpec(a.shape, lambda j: (0, 0))

    out = pl.BlockSpec((ROWS, HEAD_COLS), lambda j: (0, 0))
    return pl.pallas_call(
        attention_kernel,
        grid=(1,),
        in_specs=[whole(x)]
        + [block(at + first) for first in (0, 0, 2, 2, 4, 4)]
        + [pl.BlockSpec((8, HEAD_COLS), lambda j: (0, head_block))]
        + [whole(t) for t in tables],
        out_specs=[out] * 4 + [pl.BlockSpec((8, ROWS), lambda j: (0, 0))],
        out_shape=[jax.ShapeDtypeStruct((ROWS, HEAD_COLS), BF16)] * 4 + [jax.ShapeDtypeStruct((8, ROWS), F32)],
        compiler_params=pltpu.CompilerParams(vmem_limit_bytes=56 << 20),
        cost_estimate=cost_of(flops=7_500_000_000, bytes_accessed=7_000_000, transcendentals=4_300_000),
        name="attention_forward",
    )(x, near, far, near, far, near, far, biases, *tables)


def attention_back_kernel(
    q_ref, k_ref, v_ref, g_ref, o_ref, l_ref, c_ref, s1_ref, s2_ref,
    dq_ref, dk_ref, dv_ref, sum_ref, dq_turned, dk_sum, dv_sum, delta_ref, k_turned, *, step
):
    lane = lax.broadcasted_iota(jnp.int32, (1, 128), 1)
    low_half = lane < 64
    deltas = jnp.zeros((ROWS, 128), F32)
    for pair in range(2):
        cols = slice(pair * 128, pair * 128 + 128)
        product = g_ref[:, cols].astype(F32) * o_ref[:, cols].astype(F32)
        for h in range(2):
            own = low_half if h == 0 else ~low_half
            delta = jnp.sum(jnp.where(own, product, 0.0), axis=1, keepdims=True)
            deltas = jnp.where(lane == pair * 2 + h, delta, deltas)
    delta_ref[...] = deltas.T[0:8, :]
    real_key = lax.broadcasted_iota(jnp.int32, (ROWS, 1), 0) <= KEYS
    class_key = lax.broadcasted_iota(jnp.int32, (ROWS - KEYS, 1), 0) == 0
    k_turned[...] = k_ref[...].T
    for t in range(KEYS // step):
        rows = pl.ds(t * step, step)
        for pair in range(2):
            cols = slice(pair * 128, pair * 128 + 128)
            q_pair, g_pair = q_ref[rows, cols], g_ref[rows, cols]
            k_pair, v_pair = k_ref[:, cols], v_ref[:, cols]
            dk, dv = None, None
            for h in range(2):
                own = low_half if h == 0 else ~low_half
                head = pair * 2 + h
                q_head = jnp.where(own, q_pair, jnp.zeros_like(q_pair))
                g_head = jnp.where(own, g_pair, jnp.zeros_like(g_pair))
                scores = dot_nt(k_pair, q_head)
                log_sums = l_ref[head : head + 1, rows]
                p = jnp.concatenate(
                    [
                        jnp.exp2(scores[:KEYS] - log_sums),
                        jnp.where(class_key, jnp.exp2(scores[KEYS:] - log_sums), 0.0),
                    ],
                    axis=0,
                )
                gp = dot_nt(v_pair, g_head)
                ds = (p * (gp - delta_ref[head : head + 1, rows])).astype(BF16)
                dv_part, dk_part = dot_nn(p.astype(BF16), g_head), dot_nn(ds, q_head)
                dv = dv_part if dv is None else dv + dv_part
                dk = dk_part if dk is None else dk + dk_part
                own_rows = slice(head * 64, head * 64 + 64)
                dq_turned[own_rows, rows] = dot_nn(k_turned[own_rows, :], ds)
            if t == 0:
                dk_sum[:, cols], dv_sum[:, cols] = dk, dv
            else:
                dk_sum[:, cols] += dk
                dv_sum[:, cols] += dv
    q_class = q_ref[KEYS : KEYS + 16, :][0:1].astype(F32)
    g_class = g_ref[KEYS : KEYS + 16, :][0:1].astype(F32)
    shape = (128, HEAD_COLS)
    own = lax.broadcasted_iota(jnp.int32, shape, 0) == lax.broadcasted_iota(jnp.int32, shape, 1) // 64
    q_diag = jnp.where(own, q_class, 0.0).astype(BF16)
    g_diag = jnp.where(own, g_class, 0.0).astype(BF16)
    scores, gp = dot_nt(k_ref[...], q_diag), dot_nt(v_ref[...], g_diag)
    log_class, delta_class = jnp.zeros((1, 128), F32), jnp.zeros((1, 128), F32)
    for head in range(4):
        log_class = jnp.where(lane == head, l_ref[head : head + 1, KEYS : KEYS + 1], log_class)
        delta_class = jnp.where(lane == head, delta_ref[head : head + 1, KEYS : KEYS + 1], delta_class)
    p = jnp.where(real_key & (lane < 4), jnp.exp2(scores - log_class), 0.0)
    ds = (p * (gp - delta_class)).astype(BF16)
    dv = dv_sum[...] + dot_nn(p.astype(BF16), g_diag)
    dk = dk_sum[...] + dot_nn(ds, q_diag)
    dq_class = jnp.sum(jnp.where(own, dot_tn(ds, k_ref[...]), 0.0), axis=0, keepdims=True)
    first = lax.broadcasted_iota(jnp.int32, (16, 1), 0) == 0
    dq = jnp.concatenate([dq_turned[...].T, jnp.where(first, dq_class, 0.0)], axis=0)
    c, s1, s2 = twice(c_ref[...]), twice(s1_ref[...]), twice(s2_ref[...])
    dq = (rotate_lanes(dq, c, -s1, -s2) * 0.125).astype(BF16)
    dv = dv.astype(BF16)
    dq_ref[...] = dq
    dk_ref[...] = (rotate_lanes(dk, c, -s1, -s2) * (1.0 / LOG2E)).astype(BF16)
    dv_ref[...] = dv
    sum_ref[0:1, :] = jnp.sum(dq.astype(F32), axis=0, keepdims=True)
    sum_ref[1:2, :] = jnp.sum(dv.astype(F32), axis=0, keepdims=True)
    sum_ref[2:8, :] = jnp.zeros((6, HEAD_COLS), F32)


def attention_backward(q, k, v, o, log_sums, g, tables, step=256):
    def whole(a):
        return pl.BlockSpec(a.shape, lambda j: (0, 0))

    block = pl.BlockSpec((ROWS, HEAD_COLS), lambda j: (0, 0))
    return pl.pallas_call(
        functools.partial(attention_back_kernel, step=step),
        grid=(1,),
        in_specs=[block] * 5 + [pl.BlockSpec((8, ROWS), lambda j: (0, 0))] + [whole(t) for t in tables],
        out_specs=[block] * 3 + [pl.BlockSpec((8, HEAD_COLS), lambda j: (0, 0))],
        out_shape=[jax.ShapeDtypeStruct((ROWS, HEAD_COLS), BF16)] * 3
        + [jax.ShapeDtypeStruct((8, HEAD_COLS), F32)],
        scratch_shapes=[pltpu.VMEM((HEAD_COLS, KEYS), F32)]
        + [pltpu.VMEM((ROWS, HEAD_COLS), F32)] * 2
        + [pltpu.VMEM((8, ROWS), F32), pltpu.VMEM((HEAD_COLS, ROWS), BF16)],
        compiler_params=pltpu.CompilerParams(vmem_limit_bytes=48 << 20),
        cost_estimate=cost_of(
            flops=13_000_000_000, bytes_accessed=5_000_000, transcendentals=4_300_000
        ),
        name="attention_backward",
    )(q, k, v, g, o, log_sums, *tables)


def over_rows(kernel, name, tiled, held, outs, sums=(), flops=0, step=STEP, only=None):
    rows = ROWS if only is None else step
    if only is None:
        in_specs = [pl.BlockSpec((step, a.shape[1]), lambda i: (i, 0)) for a in tiled]
    else:
        in_specs = [
            pl.BlockSpec((pl.Element(step), pl.Element(a.shape[1])), lambda i: (only, 0)) for a in tiled
        ]
    held = [h if isinstance(h, tuple) else (h, h.shape, 0) for h in held]
    in_specs += [
        pl.BlockSpec(shape, lambda i, column=column: (0, column), pipeline_mode=pl.Buffered(1))
        for _, shape, column in held
    ]
    held = [h[0] for h in held]
    out_specs = [pl.BlockSpec((step, n), lambda i: (i, 0)) for n, _ in outs]
    out_specs += [pl.BlockSpec((8, n), lambda i: (0, 0)) for n in sums]
    out_shape = [jax.ShapeDtypeStruct((rows, n), t) for n, t in outs]
    out_shape += [jax.ShapeDtypeStruct((8, n), F32) for n in sums]
    moved = sum(a.size * a.dtype.itemsize for a in list(tiled) + list(held))
    moved += sum(s.size * s.dtype.itemsize for s in out_shape)
    return pl.pallas_call(
        kernel,
        grid=(rows // step,),
        in_specs=in_specs,
        out_specs=out_specs,
        out_shape=out_shape,
        compiler_params=pltpu.CompilerParams(vmem_limit_bytes=56 << 20),
        cost_estimate=cost_of(flops=flops, bytes_accessed=moved, transcendentals=0),
        name=name,
    )(*tiled, *held)


def add_sums(ref, *rows):
    @pl.when(pl.program_id(0) == 0)
    def _():
        ref[...] = jnp.zeros_like(ref)

    for i, value in enumerate(rows):
        ref[i : i + 1, :] += jnp.sum(value, axis=0, keepdims=True)


def unit_norm(values):
    centred = values - jnp.mean(values, axis=-1, keepdims=True)
    inv_std = lax.rsqrt(jnp.mean(centred * centred, axis=-1, keepdims=True) + epsilon)
    return centred * inv_std, inv_std


def unit_norm_back(scaled, unit, inv_std):
    return inv_std * (
        scaled
        - jnp.mean(scaled, axis=-1, keepdims=True)
        - unit * jnp.mean(scaled * unit, axis=-1, keepdims=True)
    )


def vectors_kernel(near_ref, far_ref, order_ref, vec_ref, head_ref):
    rows = jnp.concatenate([near_ref[...].astype(F32).T, far_ref[...].astype(F32).T], axis=1)[0:8]
    vec_ref[...] = rows
    head_ref[...] = dot_nt(rows.astype(BF16), order_ref[...])


def gathered_vectors(near, far, order):
    block = pl.BlockSpec((HALF, 128), lambda j: (0, 3 * HALF // 128))
    out = pl.BlockSpec((8, WIDTH), lambda j: (0, 0))
    return pl.pallas_call(
        vectors_kernel,
        grid=(1,),
        in_specs=[block, block, pl.BlockSpec(order.shape, lambda j: (0, 0))],
        out_specs=[out, out],
        out_shape=[jax.ShapeDtypeStruct((8, WIDTH), F32)] * 2,
        cost_estimate=cost_of(flops=40_000_000, bytes_accessed=2_400_000, transcendentals=0),
        name="vectors",
    )(near, far, order)


def sigmoid_of(x):
    return 0.5 * jnp.tanh(0.5 * x) + 0.5


def start_kernel(rows_ref, order_ref, vec_ref, tokens_ref, normed_ref):
    tokens = dot_nn(rows_ref[...], order_ref[...])
    tokens_ref[...] = tokens.astype(BF16)
    unit, _ = unit_norm(tokens)
    normed_ref[...] = (unit * vec_ref[0:1, :] + vec_ref[1:2, :]).astype(BF16)


def middle_kernel(a0_ref, a1_ref, a2_ref, a3_ref, tokens_ref, na_ref, nb_ref, fa_ref, fb_ref, vec_ref, middle_ref, normed_ref):
    low = jnp.concatenate([a0_ref[...], a1_ref[...]], axis=1)
    high = jnp.concatenate([a2_ref[...], a3_ref[...]], axis=1)
    branch = jnp.concatenate(
        [
            dot_nt(low, na_ref[...]) + dot_nt(high, nb_ref[...]),
            dot_nt(low, fa_ref[...]) + dot_nt(high, fb_ref[...]),
        ],
        axis=1,
    )
    middle = tokens_ref[...].astype(F32) + (branch + vec_ref[4:5, :])
    middle_ref[...] = middle.astype(BF16)
    unit, _ = unit_norm(middle)
    normed_ref[...] = (unit * vec_ref[5:6, :] + vec_ref[6:7, :]).astype(BF16)


def hidden_kernel(x_ref, gn_ref, gf_ref, un_ref, uf_ref, ffn_ref, gate_ref, up_ref, inner_ref, stat_ref, *, hidden):
    near, far = x_ref[:, :HALF], x_ref[:, HALF:]
    gate = dot_nn(near, gn_ref[...]) + dot_nn(far, gf_ref[...]) + ffn_ref[0:1, :]
    up = dot_nn(near, un_ref[...]) + dot_nn(far, uf_ref[...]) + ffn_ref[1:2, :]
    gate_ref[...] = gate.astype(gate_ref.dtype)
    up_ref[...] = up.astype(up_ref.dtype)
    mix = gate * sigmoid_of(gate) * up
    mean = jnp.sum(mix, axis=1, keepdims=True) * (1.0 / hidden)
    real = lax.broadcasted_iota(jnp.int32, (1, mix.shape[1]), 1) < hidden
    centred = jnp.where(real, mix - mean, 0.0)
    inv_std = lax.rsqrt(jnp.sum(centred * centred, axis=1, keepdims=True) * (1.0 / hidden) + epsilon)
    inner_ref[...] = (centred * inv_std * ffn_ref[2:3, :] + ffn_ref[3:4, :]).astype(BF16)
    lane = lax.broadcasted_iota(jnp.int32, (1, 128), 1)
    stat_ref[...] = jnp.where(lane == 0, mean, inv_std)


def result_kernel(inner_ref, middle_ref, near_ref, far_ref, vec_ref, order_ref, keep_ref, out_ref):
    inner = inner_ref[...]
    branch = jnp.concatenate([dot_nt(inner, near_ref[...]), dot_nt(inner, far_ref[...])], axis=1)
    result = middle_ref[...].astype(F32) + (branch + vec_ref[7:8, :])
    rounded = (result * keep_ref[0:1, 0:1]).astype(BF16)
    out_ref[...] = dot_nt(rounded, order_ref[...]).astype(BF16)


def hidden_back_kernel(
    d_ref, gate_ref, up_ref, stat_ref, order_ref, keep_ref, near_ref, far_ref, ffn_ref,
    branch_ref, dgate_ref, dup_ref, wide_ref, sum_ref, *, hidden
):
    branch = (dot_nn(d_ref[...], order_ref[...]) * keep_ref[0:1, 0:1]).astype(BF16)
    branch_ref[...] = branch
    g_inner = dot_nn(branch[:, :HALF], near_ref[...]) + dot_nn(branch[:, HALF:], far_ref[...])
    gate, up = gate_ref[...].astype(F32), up_ref[...].astype(F32)
    sigmoid = sigmoid_of(gate)
    silu = gate * sigmoid
    mean, inv_std = stat_ref[:, 0:1], stat_ref[:, 1:2]
    unit = (silu * up - mean) * inv_std
    g_unit = g_inner * ffn_ref[2:3, :]
    share = 1.0 / hidden
    g_mix = inv_std * (
        g_unit
        - jnp.sum(g_unit, axis=1, keepdims=True) * share
        - unit * (jnp.sum(g_unit * unit, axis=1, keepdims=True) * share)
    )
    d_gate = (g_mix * up * (sigmoid * (1.0 + gate * (1.0 - sigmoid)))).astype(BF16)
    d_up = (g_mix * silu).astype(BF16)
    dgate_ref[...] = d_gate
    dup_ref[...] = d_up
    add_sums(wide_ref, d_gate.astype(F32), d_up.astype(F32), g_inner * unit, g_inner)
    add_sums(sum_ref, branch.astype(F32))


def middle_back_kernel(
    dgate_ref, dup_ref, branch_ref, middle_ref, gn_ref, gf_ref, un_ref, uf_ref, na_ref, nb_ref, fa_ref, fb_ref, vec_ref,
    low_ref, d0_ref, d1_ref, d2_ref, d3_ref, sum_ref
):
    d_gate, d_up = dgate_ref[...], dup_ref[...]
    g_two = jnp.concatenate(
        [
            dot_nt(d_gate, gn_ref[...]) + dot_nt(d_up, un_ref[...]),
            dot_nt(d_gate, gf_ref[...]) + dot_nt(d_up, uf_ref[...]),
        ],
        axis=1,
    )
    unit, inv_std = unit_norm(middle_ref[...].astype(F32))
    g_middle = branch_ref[...].astype(F32) + unit_norm_back(g_two * vec_ref[5:6, :], unit, inv_std)
    low = g_middle.astype(BF16)
    low_ref[...] = low
    near, far = low[:, :HALF], low[:, HALF:]
    d_low = (dot_nn(near, na_ref[...]) + dot_nn(far, fa_ref[...])).astype(BF16)
    d_high = (dot_nn(near, nb_ref[...]) + dot_nn(far, fb_ref[...])).astype(BF16)
    d0_ref[...], d1_ref[...] = d_low[:, :HEAD_COLS], d_low[:, HEAD_COLS:]
    d2_ref[...], d3_ref[...] = d_high[:, :HEAD_COLS], d_high[:, HEAD_COLS:]
    add_sums(sum_ref, low.astype(F32), g_two * unit, g_two)


def last_kernel(*refs):
    grads = refs[:12]
    gmid_ref, tokens_ref, an_ref, af_ref, bn_ref, bf_ref, vec_ref, order_ref, grad_ref, sum_ref = refs[12:]

    def back(low_w, high_w):
        total = 0.0
        for first, w_ref in ((0, low_w), (6, high_w)):
            for i in range(3):
                g = jnp.concatenate([grads[first + i][...], grads[first + 3 + i][...]], axis=1)
                total = total + dot_nt(g, w_ref[:, i * HALF : i * HALF + HALF])
        return total

    g_one = jnp.concatenate([back(an_ref, bn_ref), back(af_ref, bf_ref)], axis=1)
    unit, inv_std = unit_norm(tokens_ref[...].astype(F32))
    grad = gmid_ref[...].astype(F32) + unit_norm_back(g_one * vec_ref[0:1, :], unit, inv_std)
    grad_ref[...] = dot_nt(grad.astype(BF16), order_ref[...]).astype(BF16)
    add_sums(sum_ref, g_one * unit, g_one)


def weight_grads(half, steps, received=None):
    sources, arrays = [], []
    for x, gs in steps:
        if not any(x is s for s in sources):
            sources.append(x)
        for g, _, _ in gs:
            if not any(g is a for a in arrays):
                arrays.append(g)
    tile = sum(width for _, width, _ in steps[0][1])
    refs_of, specs, operands = [], [], []
    for j, (x, gs) in enumerate(steps):
        mine = []
        for g, width, at in gs:
            found = next((i for i, o in enumerate(operands) if o[0] is g and o[1] == width), None)
            if found is None:
                operands.append((g, width, {}))
                found = len(operands) - 1
            operands[found][2][j] = at
            mine.append(found)
        refs_of.append(mine)
    for g, width, places in operands:
        known = sorted(places.items())

        def index(j, known=known):
            at = known[0][1]
            for step, place in known[1:]:
                at = jnp.where(j >= step, place, at)
            return 0, at

        specs.append(pl.BlockSpec((ROWS, width), index))
    plus = [] if received is None else [received]

    def kernel(*refs):
        xs, gs = refs[: len(sources)], refs[len(sources) : len(sources) + len(operands)]
        out_ref, turned, last = refs[-3:]
        step = pl.program_id(0)
        for j, (x, _) in enumerate(steps):
            source = next(i for i, s in enumerate(sources) if s is x)
            fresh = j == 0 or steps[j - 1][0] is not x

            @pl.when(step == j)
            def _(j=j, source=source, fresh=fresh):
                if fresh:
                    turned[...] = xs[source][0:KEYS, :].T
                    last[...] = xs[source][KEYS:ROWS, :].astype(F32).T
                parts = [gs[r] for r in refs_of[j]]
                main = jnp.concatenate([p[0:KEYS, :] for p in parts], axis=1)
                row = jnp.concatenate([p[KEYS:ROWS, :].astype(F32)[0:1] for p in parts], axis=1)
                out = dot_nn(turned[...], main) + last[:, 0:1] * row
                if plus:
                    out = out + refs[len(sources) + len(operands)][...].astype(F32)
                out_ref[...] = out.astype(BF16)

    block = pl.BlockSpec((HALF, tile), lambda j: (0, j))
    columns = len(steps) * tile
    return pl.pallas_call(
        kernel,
        grid=(len(steps),),
        in_specs=[pl.BlockSpec((ROWS, HALF), lambda j: (0, half), pipeline_mode=pl.Buffered(1)) for _ in sources]
        + specs
        + [block] * len(plus),
        out_specs=block,
        out_shape=jax.ShapeDtypeStruct((HALF, columns), BF16),
        scratch_shapes=[pltpu.VMEM((HALF, KEYS), BF16), pltpu.VMEM((HALF, ROWS - KEYS), F32)],
        compiler_params=pltpu.CompilerParams(vmem_limit_bytes=48 << 20),
        cost_estimate=cost_of(
            flops=ROWS * WIDTH * columns, bytes_accessed=3 * ROWS * columns, transcendentals=0
        ),
        name="weight_grads",
    )(*sources, *[g for g, _, _ in operands], *plus)


def pair_tables(coords):
    lane = jnp.arange(128)
    freqs = 10000.0 ** (-(lane % 16).astype(F32) / 16.0)
    along_rows = (lane % 64 < 32)[None, :]
    places = jnp.where(along_rows, coords[:, 0:1], coords[:, 1:2]).astype(F32)
    angles = jnp.pad(places * freqs[None, :], ((0, ROWS - KEYS), (0, 0)))
    cosines, sines = jnp.cos(angles), jnp.sin(angles)
    even = (lane % 32 < 16)[None, :]
    return cosines, jnp.where(even, -sines, 0.0), jnp.where(even, 0.0, sines)


def feature_order(me):
    natural = lax.broadcasted_iota(jnp.int32, (WIDTH, WIDTH), 0)
    place = lax.broadcasted_iota(jnp.int32, (WIDTH, WIDTH), 1)
    block = place // 32
    owner = (
        (block // 16) * BIT_CORE
        + (block // 8 % 2) * BIT_X
        + (block // 4 % 2) * BIT_Y
        + (block // 2 % 2) * BIT_Z1
        + (block % 2) * BIT_Z0
    ) ^ me
    return (natural == owner * 32 + place % 32).astype(BF16)


def paired_device(
    patch_in, cls_in, d_patch, d_cls, image_valid, patch_coords,
    w_query, w_key, w_value, w_gate, w_up, w_out, w_down, layer_vectors, ffn_vectors,
):
    SENT.clear()
    me, pos = lax.axis_index(BOTH), lax.axis_index("ctx")
    hidden = w_gate.shape[1]
    wide = (hidden + 255) // 256 * 256
    extra = ((0, 0), (0, wide - hidden))

    def own_image(patches, classes, *deps):
        near = lax.dynamic_index_in_dim(patches, pos, 0, keepdims=False)
        sent = after(lax.dynamic_index_in_dim(patches, 1 - pos, 0, keepdims=False), *deps)
        far = swap_over(sent, BIT_X)
        class_row = lax.dynamic_index_in_dim(classes, pos, 0)
        return joined(near, far, jnp.pad(class_row, ((0, ROWS - KEYS - 1), (0, 0)))), far

    def to_pair(rows, far):
        near = rows[:512]
        is_first = pos == 0
        near_class, far_class = rows[KEYS], far[512]
        patches = jnp.where(is_first, jnp.stack([near, far[:512]]), jnp.stack([far[:512], near]))
        classes = jnp.where(is_first, jnp.stack([near_class, far_class]), jnp.stack([far_class, near_class]))
        return patches, classes

    vectors_local = jnp.pad(layer_vectors.T, ((0, 0), (0, 120)))
    low_heads = [w[:, :HALF] for w in (w_query, w_key, w_value)]
    high_heads = [w[:, HALF:] for w in (w_query, w_key, w_value)]
    g_low = Gather(joined(*low_heads, vectors_local, axis=1))
    g_high = Gather(joined(*high_heads, w_out.T, axis=1))
    g_gate = Gather(jnp.pad(w_gate, extra))
    g_up = Gather(jnp.pad(w_up, extra))
    g_down = Gather(jnp.pad(w_down.T, extra))

    image_rows, image_far = own_image(patch_in, cls_in)
    coords = joined(patch_coords, swap_over(patch_coords, BIT_X))
    order = feature_order(me)
    tables = pair_tables(coords)
    keep = lax.dynamic_index_in_dim(image_valid, pos, 0, keepdims=False).astype(F32)
    keep = jnp.full((8, 128), keep, F32)
    ffn = jnp.pad(ffn_vectors.astype(F32), ((0, 4), (0, wide - hidden)))

    z_one = g_low.along_z0()
    z_low = g_low.along_z1()
    g_high.along_z0(z_one)
    xy_low = g_low.along_xy()
    z_high = g_high.along_z1(z_low)
    corner_low = g_low.corners(image_far)
    z_one = g_gate.along_z0(z_high)
    xy_high = g_high.along_xy(xy_low)
    near_low = g_low.whole(z_high)

    gate = near_low, g_low.far, image_rows, z_one
    z_gate = g_gate.along_z1(gate)
    vectors, head_biases = gathered_vectors(near_low, g_low.far, order)
    tokens, normed = over_rows(
        start_kernel, "start", [ready(image_rows, gate)], [order, vectors], [(WIDTH, BF16), (WIDTH, BF16)],
        flops=2_200_000_000,
    )

    def attend(block, gate):
        group = g_low if block < 2 else g_high
        return attention_forward(
            ready(normed, gate), group.near, group.far, head_biases, block, block % 2, tables
        )

    gate = normed, xy_high, z_gate
    z_up = g_up.along_z0(gate)
    corner_high = g_high.corners(gate)
    xy_gate = g_gate.along_xy(gate)
    heads = [attend(0, gate)]

    gate = heads[0][3], corner_high, xy_gate, z_up
    near_high = g_high.whole(gate)
    corner_gate = g_gate.corners(gate)
    z_up = g_up.along_z1(gate)
    heads.append(attend(1, gate))

    gate = heads[1][3], g_high.far, corner_gate, z_up
    near_gate = g_gate.whole(gate)
    xy_up = g_up.along_xy(gate)
    z_down = g_down.along_z0(gate)
    heads.append(attend(2, gate))

    gate = heads[2][3], xy_up, g_gate.far, z_down
    corner_up = g_up.corners(gate)
    z_down = g_down.along_z1(gate)
    heads.append(attend(3, gate))

    gate = heads[3][3], corner_up, z_down
    near_up = g_up.whole(gate)
    xy_down = g_down.along_xy(gate)
    out_w = [((w, (HALF, HALF), 3 + i)) for w in (near_high, g_high.far) for i in range(2)]
    attended = [h[3] for h in heads]
    middle, normed_two = over_rows(
        middle_kernel, "middle", attended + [ready(tokens, gate)], out_w + [vectors],
        [(WIDTH, BF16), (WIDTH, BF16)], flops=2_200_000_000, step=520,
    )

    gate = normed_two, g_up.far, xy_down
    corner_down = g_down.corners(gate)
    grad_image_rows, grad_far = own_image(d_patch, d_cls, gate)
    gate_up = [near_gate, g_gate.far, near_up, g_up.far]
    gate_act, up_act, inner, stats = over_rows(
        functools.partial(hidden_kernel, hidden=hidden), "hidden", [ready(normed_two, gate)],
        gate_up + [ffn], [(wide, BF16), (wide, BF16), (wide, BF16), (128, F32)], flops=12_000_000_000,
    )

    gate = inner, corner_down, grad_far
    near_down = g_down.whole(gate)
    down_w = [near_down, g_down.far]
    (out_rows,) = over_rows(
        result_kernel, "result", [inner, ready(middle, gate)], down_w + [vectors, order, keep],
        [(WIDTH, BF16)], flops=8_000_000_000, step=520,
    )

    gate = out_rows
    far_rows = swap_over(after(out_rows, gate)[HALF:], BIT_X)
    branch, d_gate, d_up, wide_sums, branch_sums = over_rows(
        functools.partial(hidden_back_kernel, hidden=hidden), "hidden_back",
        [ready(grad_image_rows, gate), gate_act, up_act, stats], [order, keep] + down_w + [ffn],
        [(WIDTH, BF16), (wide, BF16), (wide, BF16)], [wide, WIDTH], flops=8_000_000_000,
    )

    gate = wide_sums, far_rows
    outs = to_pair(after(out_rows, far_rows), far_rows)
    all_sums = lax.all_gather(wide_sums, BOTH)
    part_width = wide // 2
    down, second, low, high = Scatter(), Scatter(), Scatter(), Scatter()
    late = ready(normed_two, gate)
    second_steps = [(late, [(g, part_width, i)]) for g in (d_gate, d_up) for i in range(2)]
    second_far = weight_grads(1, second_steps)

    gate = second_far
    second_stage = second.over_core(second_far, gate)
    late = ready(branch, gate)
    down_steps = [(late, [(inner, part_width, i)]) for i in range(2)]
    down_far = weight_grads(1, down_steps)

    gate = down_far, second_stage
    down_stage = down.over_core(down_far, gate)
    late = ready(normed_two, gate)
    second_total = weight_grads(0, [(late, gs) for _, gs in second_steps], second_stage)

    gate = second_total, down_stage
    second_stage = second.corners(second_total, gate)
    late = ready(branch, gate)
    down_total = weight_grads(0, [(late, gs) for _, gs in down_steps], down_stage)

    gate = down_total, second_stage
    second_stage = second.sides(gate)
    att_low, *att_grads, middle_sums = over_rows(
        middle_back_kernel, "middle_back", [d_gate, d_up, branch, ready(middle, gate)],
        gate_up + out_w + [vectors], [(WIDTH, BF16)] + [(HEAD_COLS, BF16)] * 4, [WIDTH],
        flops=14_000_000_000, step=520,
    )

    def attend_back(block, gate):
        return attention_backward(*heads[block], ready(att_grads[block], gate), tables)

    gate = att_low, second_stage
    second_stage, down_stage = second.along_z1(gate), down.corners(down_total, gate)
    parts = [attend_back(0, gate)]

    gate = parts[0][0], second_stage, down_stage
    gate_up_grad, down_stage = second.along_z0(gate), down.sides(gate)
    parts.append(attend_back(1, gate))

    def pieces(*arrays):
        return [(a, HEAD_COLS, 0) for a in arrays]

    gate = parts[1][0], gate_up_grad, down_stage
    down_stage = down.along_z1(gate)
    late, late_two = ready((att_low, normed), gate)
    grads = [g for part in parts for g in part[:3]]
    low_steps = [(late, pieces(*attended[2 * i : 2 * i + 2])) for i in range(2)]
    low_steps += [(late_two, pieces(*grads[2 * i : 2 * i + 2])) for i in range(3)]
    low_far = weight_grads(1, low_steps)

    gate = low_far, down_stage
    low_stage, down_grad = low.over_core(low_far, gate), down.along_z0(gate)
    parts.append(attend_back(2, gate))

    gate = parts[2][0], low_stage, down_grad
    late, late_two = ready((att_low, normed), gate)
    low_total = weight_grads(
        0, [(late if i < 2 else late_two, gs) for i, (_, gs) in enumerate(low_steps)], low_stage
    )

    gate = low_total
    low_stage = low.corner(low_total, gate)
    parts.append(attend_back(3, gate))

    gate = parts[3][0], low_stage
    low_stage = low.sides(gate)
    late = ready(normed, gate)
    grads = [g for part in parts[2:] for g in part[:3]]
    high_steps = [(late, pieces(*grads[2 * i : 2 * i + 2])) for i in range(3)]
    high_far = weight_grads(1, high_steps)
    high_stage = high.over_core(high_far)

    def last_rows(gate, first, count):
        return over_rows(
            last_kernel, "last",
            [g for part in parts for g in part[:3]] + [ready(att_low, gate), tokens],
            [(near_low, (HALF, 3 * HALF), 0), (g_low.far, (HALF, 3 * HALF), 0)]
            + [(near_high, (HALF, 3 * HALF), 0), (g_high.far, (HALF, 3 * HALF), 0), vectors, order],
            [(WIDTH, BF16)], [WIDTH], flops=4_500_000_000, step=count, only=first,
        )

    far_part, far_sums = last_rows(high_far, HALF, ROWS - HALF)

    gate = far_part, high_stage, low_stage
    low_stage = low.along_z1(gate)
    late = ready(normed, gate)
    high_total = weight_grads(0, [(late, gs) for _, gs in high_steps], high_stage)

    gate = high_total
    high.total = high_total
    far_rows = swap_over(after(far_part, gate), BIT_X)
    high_stage = high.over_y(gate)
    near_part, near_sums = last_rows(gate, 0, HALF)

    gate = near_part, low_stage, high_stage
    low_grad = low.along_z0(gate)
    high.over_x(gate, far_rows)
    high.along_z1()
    high_grad = high.along_z0()
    sums = [far_sums, near_sums, middle_sums, branch_sums] + [part[3] for part in parts]
    far_sums, near_sums, middle_sums, branch_sums, *head_sums = after(sums, far_rows)
    patch_grad, cls_grad = to_pair(after(joined(near_part, far_part), far_rows), far_rows)
    ffn_grads = jnp.sum(after(all_sums, far_rows), axis=0)[:4, :hidden]
    head_sums = jnp.dot(
        joined(*[part[:2] for part in head_sums], axis=1), order.astype(F32), precision=lax.Precision.HIGHEST
    )
    vector_grads = scatter_small(
        joined((far_sums + near_sums)[:2], head_sums, middle_sums[:3], branch_sums[:1]).T
    )
    blocks = [low_grad[:, WIDTH + i * HEAD_COLS :][:, :HEAD_COLS] for i in range(6)]
    blocks += [high_grad[:, i * HEAD_COLS :][:, :HEAD_COLS] for i in range(6)]
    query_grad, key_grad, value_grad = (joined(*blocks[i::3], axis=1) for i in range(3))
    return (
        outs[0],
        outs[1],
        patch_grad,
        cls_grad,
        query_grad,
        key_grad,
        value_grad,
        gate_up_grad[:, :hidden],
        gate_up_grad[:, wide : wide + hidden],
        low_grad[:, :WIDTH].T,
        down_grad[:, :hidden].T,
        vector_grads.T,
        ffn_grads,
    )


def solution(mesh):
    in_specs = (
        P("dp", "ctx", None),
        P("dp", None),
        P("dp", "ctx", None),
        P("dp", None),
        P("dp"),
        P("ctx", None),
        P(("dp", "ctx"), None),
        P(("dp", "ctx"), None),
        P(("dp", "ctx"), None),
        P(("dp", "ctx"), None),
        P(("dp", "ctx"), None),
        P(None, ("dp", "ctx")),
        P(None, ("dp", "ctx")),
        P(None, ("dp", "ctx")),
        P(),
    )
    out_specs = (
        P("dp", "ctx", None),
        P("dp", None),
        P("dp", "ctx", None),
        P("dp", None),
        P(("dp", "ctx"), None),
        P(("dp", "ctx"), None),
        P(("dp", "ctx"), None),
        P(("dp", "ctx"), None),
        P(("dp", "ctx"), None),
        P(None, ("dp", "ctx")),
        P(None, ("dp", "ctx")),
        P(None, ("dp", "ctx")),
        P(),
    )
    sizes = dict(mesh.shape)
    pairs = sizes["dp"] == 16 and sizes["ctx"] == 2
    body = paired_device if pairs else on_device
    return jax.shard_map(
        body, mesh=mesh, in_specs=in_specs, out_specs=out_specs, check_vma=False
    )
```

```python
import functools
import math

import jax
import jax.numpy as jnp
from jax import lax
from jax.experimental import pallas as pl
from jax.experimental.pallas import tpu as pltpu
from jax.sharding import PartitionSpec as P

HD = 64
MICRO = 2


epsilon = 1e-06


def layer_norm(values, gain, shift):
    centred = values - jnp.mean(values, axis=-1, keepdims=True)
    inv_std = lax.rsqrt(jnp.mean(centred * centred, axis=-1, keepdims=True) + epsilon)
    unit_rows = centred * inv_std
    return (unit_rows * gain + shift, unit_rows, inv_std)


def norm_back(grad_out, gain, unit_rows, inv_std, row_mask):
    scaled = grad_out * gain
    grad_in = inv_std * (
        scaled
        - jnp.mean(scaled, axis=-1, keepdims=True)
        - unit_rows * jnp.mean(scaled * unit_rows, axis=-1, keepdims=True)
    )
    weighted = grad_out * row_mask
    return (grad_in, jnp.sum(weighted * unit_rows, axis=(0, 1)), jnp.sum(weighted, axis=(0, 1)))


def rotary_tables(coords):
    freqs = 10000.0 ** (-jnp.arange(16).astype(jnp.float32) / 16.0)
    along_rows = coords[:, 0:1].astype(jnp.float32) * freqs[None, :]
    along_cols = coords[:, 1:2].astype(jnp.float32) * freqs[None, :]
    angles = jnp.concatenate([along_rows, along_rows, along_cols, along_cols], axis=1)
    cosines = jnp.concatenate([jnp.ones((1, 64), jnp.float32), jnp.cos(angles)], axis=0)
    sines = jnp.concatenate([jnp.zeros((1, 64), jnp.float32), jnp.sin(angles)], axis=0)
    return (cosines, sines)


def rotate(values, cosines, sines):
    swapped = jnp.concatenate(
        [-values[..., 16:32], values[..., 0:16], -values[..., 48:64], values[..., 32:48]], axis=-1
    )
    return values * cosines[:, None, :] + swapped * sines[:, None, :]


def unrotate(grads, cosines, sines):
    with_sin = grads * sines[:, None, :]
    moved = jnp.concatenate(
        [with_sin[..., 16:32], -with_sin[..., 0:16], with_sin[..., 48:64], -with_sin[..., 32:48]],
        axis=-1,
    )
    return grads * cosines[:, None, :] + moved


def project(rows_in, weight):
    return jnp.einsum("brd,de->bre", rows_in, weight, preferred_element_type=jnp.float32)


def project_back(grads, weight):
    return jnp.einsum("bre,de->brd", grads, weight, preferred_element_type=jnp.float32)


def weight_grad(rows_in, grads):
    return jnp.einsum("brd,bre->de", rows_in, grads, preferred_element_type=jnp.float32)


def fetch_forward(w_query, w_key, w_value, w_gate, w_up, w_out, w_down, layer_vectors):
    first_group = (
        lax.all_gather(w_query, ("dp", "ctx"), axis=0, tiled=True),
        lax.all_gather(w_key, ("dp", "ctx"), axis=0, tiled=True),
        lax.all_gather(w_value, ("dp", "ctx"), axis=0, tiled=True),
        lax.all_gather(w_gate, ("dp", "ctx"), axis=0, tiled=True),
        lax.all_gather(w_up, ("dp", "ctx"), axis=0, tiled=True),
    )
    second_group = (
        lax.all_gather(w_out, ("dp", "ctx"), axis=1, tiled=True),
        lax.all_gather(w_down, ("dp", "ctx"), axis=1, tiled=True),
        lax.all_gather(layer_vectors, ("dp", "ctx"), axis=1, tiled=True),
    )
    return tuple(first_group) + tuple(second_group)


def fetch_backward(w_query, w_key, w_value, w_gate, w_up, w_out, w_down, layer_vectors):
    first_group = (
        lax.all_gather(w_query, ("dp", "ctx"), axis=0, tiled=True),
        lax.all_gather(w_key, ("dp", "ctx"), axis=0, tiled=True),
        lax.all_gather(w_value, ("dp", "ctx"), axis=0, tiled=True),
        lax.all_gather(w_gate, ("dp", "ctx"), axis=0, tiled=True),
        lax.all_gather(w_up, ("dp", "ctx"), axis=0, tiled=True),
    )
    second_group = (
        lax.all_gather(w_out, ("dp", "ctx"), axis=1, tiled=True),
        lax.all_gather(w_down, ("dp", "ctx"), axis=1, tiled=True),
        lax.all_gather(layer_vectors, ("dp", "ctx"), axis=1, tiled=True),
    )
    return tuple(first_group) + tuple(second_group)


def head_forward(item):
    block_of_queries, block_of_keys, block_of_values = item
    logit_scores = jnp.einsum(
        "wey,wmy->wem", block_of_queries, block_of_keys, preferred_element_type=jnp.float32
    )
    row_peak = jnp.max(logit_scores, axis=-1, keepdims=True)
    shifted = jnp.exp(logit_scores - row_peak)
    denominator = jnp.sum(shifted, axis=-1, keepdims=True)
    reduced_probabilities = (shifted / denominator).astype(jnp.bfloat16)
    blended_values = jnp.einsum(
        "sce,sem->scm", reduced_probabilities, block_of_values, preferred_element_type=jnp.float32
    )
    return (blended_values, (row_peak + jnp.log(denominator))[..., 0])


def forward_pass(tokens, weights, ffn_vec, cosines, sines):
    w_query, w_key, w_value, w_gate, w_up, w_out, w_down, vectors_low = weights
    vectors = vectors_low.astype(jnp.float32)
    batch, row_count, model_width = tokens.shape
    heads = model_width // HD
    normed, unit_one, std_one = layer_norm(tokens, vectors[0], vectors[1])
    normed_low = normed.astype(jnp.bfloat16)
    queries = project(normed_low, w_query) + vectors[2]
    keys_raw = project(normed_low, w_key)
    values_low = (project(normed_low, w_value) + vectors[3]).astype(jnp.bfloat16)
    q_rot = (
        rotate(queries.reshape(batch, row_count, heads, HD), cosines, sines) * HD ** (-0.5)
    ).astype(jnp.bfloat16)
    k_flat = (
        rotate(keys_raw.reshape(batch, row_count, heads, HD), cosines, sines)
        .astype(jnp.bfloat16)
        .reshape(batch, row_count, model_width)
    )
    far_keys, far_values = (
        lax.all_gather(k_flat[:, 1:], "ctx", axis=1, tiled=True),
        lax.all_gather(values_low[:, 1:], "ctx", axis=1, tiled=True),
    )
    all_keys = jnp.concatenate([k_flat[:, :1], far_keys], axis=1)
    all_values = jnp.concatenate([values_low[:, :1], far_values], axis=1)
    length = all_keys.shape[1]
    head_queries = q_rot.transpose(2, 0, 1, 3)
    head_keys = all_keys.reshape(batch, length, heads, HD).transpose(2, 0, 1, 3)
    head_values = all_values.reshape(batch, length, heads, HD).transpose(2, 0, 1, 3)
    head_out, log_sums = lax.map(head_forward, (head_queries, head_keys, head_values))
    attended = (
        head_out.transpose(1, 2, 0, 3).reshape(batch, row_count, model_width).astype(jnp.bfloat16)
    )
    middle = tokens + (project(attended, w_out) + vectors[4])
    normed_two, unit_two, std_two = layer_norm(middle, vectors[5], vectors[6])
    normed_two_low = normed_two.astype(jnp.bfloat16)
    gate_proj = project(normed_two_low, w_gate) + ffn_vec[0]
    up_proj = project(normed_two_low, w_up) + ffn_vec[1]
    activated = jax.nn.silu(gate_proj)
    inner_act, unit_three, std_three = layer_norm(activated * up_proj, ffn_vec[2], ffn_vec[3])
    inner_low = inner_act.astype(jnp.bfloat16)
    result = middle + (project(inner_low, w_down) + vectors[7])
    saved = (
        normed_low,
        unit_one,
        std_one,
        head_queries,
        head_keys,
        head_values,
        log_sums,
        attended,
        unit_two,
        std_two,
        normed_two_low,
        gate_proj,
        up_proj,
        activated,
        unit_three,
        std_three,
        inner_low,
    )
    return (result, saved)


def backward_pass(grad_rows, weights, ffn_vec, cosines, sines, saved, row_mask):
    w_query, w_key, w_value, w_gate, w_up, w_out, w_down, vectors_low = weights
    vectors = vectors_low.astype(jnp.float32)
    (
        normed_low,
        unit_one,
        std_one,
        head_queries,
        head_keys,
        head_values,
        log_sums,
        attended,
        unit_two,
        std_two,
        normed_two_low,
        gate_proj,
        up_proj,
        activated,
        unit_three,
        std_three,
        inner_low,
    ) = saved
    batch, row_count, model_width = grad_rows.shape
    heads = model_width // HD
    reduced_mask = row_mask.astype(jnp.bfloat16)
    branch_low = grad_rows.astype(jnp.bfloat16)
    grad_down = weight_grad(inner_low, branch_low * reduced_mask)
    grad_inner = project_back(branch_low, w_down)
    grad_mix, gain_three, shift_three = norm_back(
        grad_inner, ffn_vec[2], unit_three, std_three, row_mask
    )
    sigmoid_gate = jax.nn.sigmoid(gate_proj)
    gate_low = (
        grad_mix * up_proj * sigmoid_gate * (1.0 + gate_proj * (1.0 - sigmoid_gate))
    ).astype(jnp.bfloat16)
    up_low = (grad_mix * activated).astype(jnp.bfloat16)
    grad_gate_w = weight_grad(normed_two_low * reduced_mask, gate_low)
    grad_up_w = weight_grad(normed_two_low * reduced_mask, up_low)
    grad_normed_two = project_back(gate_low, w_gate) + project_back(up_low, w_up)
    grad_mid_norm, gain_two, shift_two = norm_back(
        grad_normed_two, vectors[5], unit_two, std_two, row_mask
    )
    grad_middle = grad_rows + grad_mid_norm
    out_low = grad_middle.astype(jnp.bfloat16)
    grad_out_w = weight_grad(attended * reduced_mask, out_low)
    attended_grad = project_back(out_low, w_out).astype(jnp.bfloat16)
    head_grads = attended_grad.reshape(batch, row_count, heads, HD).transpose(2, 0, 1, 3)

    def head_backward(item):
        block_of_queries, block_of_keys, block_of_values, block_gradient, log_block = item
        logit_scores = jnp.einsum(
            "wey,wmy->wem", block_of_queries, block_of_keys, preferred_element_type=jnp.float32
        )
        attn_probs = jnp.exp(logit_scores - log_block[..., None])
        grad_probs = jnp.einsum(
            "wey,wmy->wem", block_gradient, block_of_values, preferred_element_type=jnp.float32
        )
        inner_sum = jnp.sum(attn_probs * grad_probs, axis=-1, keepdims=True)
        score_gradients = (attn_probs * (grad_probs - inner_sum)).astype(jnp.bfloat16)
        grad_query = jnp.einsum(
            "sce,sem->scm", score_gradients, block_of_keys, preferred_element_type=jnp.float32
        )
        grad_key = jnp.einsum(
            "ipz,iph->izh",
            score_gradients * reduced_mask,
            block_of_queries,
            preferred_element_type=jnp.float32,
        )
        grad_value = jnp.einsum(
            "ipz,iph->izh",
            attn_probs.astype(jnp.bfloat16) * reduced_mask,
            block_gradient,
            preferred_element_type=jnp.float32,
        )
        return (grad_query, grad_key, grad_value)

    grad_q_heads, grad_k_heads, grad_v_heads = lax.map(
        head_backward, (head_queries, head_keys, head_values, head_grads, log_sums)
    )
    length = head_keys.shape[2]
    grad_keys = grad_k_heads.transpose(1, 2, 0, 3).reshape(batch, length, model_width)
    grad_values = grad_v_heads.transpose(1, 2, 0, 3).reshape(batch, length, model_width)
    own_keys, own_values = (
        lax.psum_scatter(
            grad_keys[:, 1:].astype(jnp.bfloat16), "ctx", scatter_dimension=1, tiled=True
        ).astype(jnp.float32),
        lax.psum_scatter(
            grad_values[:, 1:].astype(jnp.bfloat16), "ctx", scatter_dimension=1, tiled=True
        ).astype(jnp.float32),
    )
    class_keys, class_values = lax.psum((grad_keys[:, :1], grad_values[:, :1]), "ctx")
    key_rows = jnp.concatenate([class_keys, own_keys], axis=1).reshape(batch, row_count, heads, HD)
    value_rows = jnp.concatenate([class_values, own_values], axis=1)
    key_low = (
        unrotate(key_rows, cosines, sines)
        .reshape(batch, row_count, model_width)
        .astype(jnp.bfloat16)
    )
    value_low = value_rows.astype(jnp.bfloat16)
    query_rows = grad_q_heads.transpose(1, 2, 0, 3)
    query_low = (
        (unrotate(query_rows, cosines, sines) * HD ** (-0.5))
        .reshape(batch, row_count, model_width)
        .astype(jnp.bfloat16)
    )
    grad_query_w = weight_grad(normed_low * reduced_mask, query_low)
    grad_key_w = weight_grad(normed_low * reduced_mask, key_low)
    grad_value_w = weight_grad(normed_low * reduced_mask, value_low)
    grad_normed = (
        project_back(query_low, w_query)
        + project_back(key_low, w_key)
        + project_back(value_low, w_value)
    )
    grad_in_norm, gain_one, shift_one = norm_back(
        grad_normed, vectors[0], unit_one, std_one, row_mask
    )
    grad_tokens = grad_middle + grad_in_norm

    def column_sum(rounded):
        return jnp.sum(rounded.astype(jnp.float32) * row_mask, axis=(0, 1))

    vector_grads = jnp.stack(
        [
            gain_one,
            shift_one,
            column_sum(query_low),
            column_sum(value_low),
            column_sum(out_low),
            gain_two,
            shift_two,
            column_sum(branch_low),
        ]
    )
    ffn_grads = jnp.stack([column_sum(gate_low), column_sum(up_low), gain_three, shift_three])
    return (
        grad_tokens,
        (
            (grad_query_w, grad_key_w, grad_value_w, grad_gate_w, grad_up_w),
            (grad_out_w, grad_down, vector_grads),
            ffn_grads,
        ),
    )


def on_device(
    patch_in,
    cls_in,
    d_patch,
    d_cls,
    image_valid,
    patch_coords,
    w_query,
    w_key,
    w_value,
    w_gate,
    w_up,
    w_out,
    w_down,
    layer_vectors,
    ffn_vectors,
):
    images, patch_rows, model_width = patch_in.shape
    group_size = images // MICRO
    cosines, sines = rotary_tables(patch_coords)
    first_flag = (lax.axis_index("ctx") == 0).astype(jnp.float32)
    row_weight = jnp.concatenate([first_flag[None], jnp.ones((patch_rows,), jnp.float32)])
    row_mask = row_weight[None, :, None]
    ffn_vec = ffn_vectors.astype(jnp.float32)
    keep_mask = image_valid.astype(jnp.float32)
    results = []
    totals = None
    for micro_step in range(MICRO):
        first_image = micro_step * group_size
        last_image = first_image + group_size
        tokens = jnp.concatenate(
            [cls_in[first_image:last_image, None, :], patch_in[first_image:last_image]], axis=1
        ).astype(jnp.float32)
        weights = fetch_forward(w_query, w_key, w_value, w_gate, w_up, w_out, w_down, layer_vectors)
        result, saved = forward_pass(tokens, weights, ffn_vec, cosines, sines)
        keep_rows = keep_mask[first_image:last_image][:, None, None]
        grad_rows = (
            jnp.concatenate(
                [d_cls[first_image:last_image, None, :], d_patch[first_image:last_image]], axis=1
            ).astype(jnp.float32)
            * keep_rows
        )
        back_weights = fetch_backward(
            w_query, w_key, w_value, w_gate, w_up, w_out, w_down, layer_vectors
        )
        grad_tokens, weight_grads = backward_pass(
            grad_rows, back_weights, ffn_vec, cosines, sines, saved, row_mask
        )
        if totals is None:
            totals = weight_grads
        else:
            totals = jax.tree.map(lambda first, second: first + second, totals, weight_grads)
        results.append(
            ((result * keep_rows).astype(jnp.bfloat16), grad_tokens.astype(jnp.bfloat16))
        )
    out_rows = jnp.concatenate([entry[0] for entry in results], axis=0)
    grad_out_rows = jnp.concatenate([entry[1] for entry in results], axis=0)
    in_grads, out_grads, ffn_total = totals
    owned_in = (
        lax.psum_scatter(in_grads[0], ("dp", "ctx"), scatter_dimension=0, tiled=True),
        lax.psum_scatter(in_grads[1], ("dp", "ctx"), scatter_dimension=0, tiled=True),
        lax.psum_scatter(in_grads[2], ("dp", "ctx"), scatter_dimension=0, tiled=True),
        lax.psum_scatter(in_grads[3], ("dp", "ctx"), scatter_dimension=0, tiled=True),
        lax.psum_scatter(in_grads[4], ("dp", "ctx"), scatter_dimension=0, tiled=True),
    )
    owned_out = (
        lax.psum_scatter(out_grads[0], ("dp", "ctx"), scatter_dimension=1, tiled=True),
        lax.psum_scatter(out_grads[1], ("dp", "ctx"), scatter_dimension=1, tiled=True),
        lax.psum_scatter(out_grads[2], ("dp", "ctx"), scatter_dimension=1, tiled=True),
    )
    ffn_summed = lax.psum(ffn_total, ("dp", "ctx"))
    return (
        out_rows[:, 1:],
        out_rows[:, 0],
        grad_out_rows[:, 1:],
        grad_out_rows[:, 0],
        owned_in[0],
        owned_in[1],
        owned_in[2],
        owned_in[3],
        owned_in[4],
        owned_out[0],
        owned_out[1],
        owned_out[2],
        ffn_summed,
    )


BOTH = ("dp", "ctx")
BIT_X, BIT_CORE, BIT_Y, BIT_Z0, BIT_Z1 = 1, 2, 4, 16, 8
ROWS = 1040
KEYS = 1024
WIDTH = 1024
HALF = 512
HEAD_COLS = 256
STEP = 208
LOG2E = math.log2(math.e)
COST = 4
F32 = jnp.float32
BF16 = jnp.bfloat16


SENT = []


def swap_over(value, bit):
    value = lax.optimization_barrier(value)
    SENT.append(value)
    count = lax.axis_size(BOTH)
    return lax.ppermute(value, BOTH, [(i, i ^ bit) for i in range(count)])


def joined(*parts, axis=0):
    return jnp.concatenate(parts, axis=axis)


def after(value, *deps):
    return lax.optimization_barrier((value,) + deps)[0]


def ready(value, *deps):
    corners = [sum(v[0:1, 0:1].astype(F32) for v in SENT)] if SENT else []
    SENT.clear()
    return after(value, *deps, *corners)


def dot_nn(a, b):
    return lax.dot_general(a, b, (((1,), (0,)), ((), ())), preferred_element_type=F32)


def dot_nt(a, b):
    return lax.dot_general(a, b, (((1,), (1,)), ((), ())), preferred_element_type=F32)


def dot_tn(a, b):
    return lax.dot_general(a, b, (((0,), (0,)), ((), ())), preferred_element_type=F32)


def cost_of(flops, bytes_accessed, transcendentals):
    return pl.CostEstimate(
        flops=int(COST * flops), bytes_accessed=int(COST * bytes_accessed), transcendentals=int(COST * transcendentals)
    )


def pack_rows(*parts):
    total, columns = sum(p.shape[0] for p in parts), parts[0].shape[1]
    blocks = columns // 128
    steps = next(n for n in (4, 5, 3, 2, 1) if blocks % n == 0)
    tile = columns // steps

    def kernel(*refs):
        out, start = refs[len(parts)], 0
        for ref in refs[: len(parts)]:
            out[start : start + ref.shape[0], :] = ref[...]
            start += ref.shape[0]

    return pl.pallas_call(
        kernel,
        grid=(steps,),
        in_specs=[pl.BlockSpec((p.shape[0], tile), lambda j: (0, j)) for p in parts],
        out_specs=pl.BlockSpec((total, tile), lambda j: (0, j)),
        out_shape=jax.ShapeDtypeStruct((total, columns), parts[0].dtype),
        compiler_params=pltpu.CompilerParams(vmem_limit_bytes=32 << 20),
        cost_estimate=cost_of(flops=0, bytes_accessed=4 * total * columns, transcendentals=0),
        name="pack_rows",
    )(*parts)


class Gather:
    def __init__(self, local):
        self.part = local

    def along_z0(self, *deps):
        part = after(self.part, *deps)
        far = swap_over(part, BIT_Z0)
        self.part = joined(part, far)
        return far

    def along_z1(self, *deps):
        part = after(self.part, *deps)
        far = swap_over(part, BIT_Z1)
        self.part = joined(part, far)
        return far

    def along_xy(self, *deps):
        part = after(self.part, *deps)
        self.over = swap_over(part, BIT_X), swap_over(part, BIT_Y)
        return self.over

    def corners(self, *deps):
        over_x, over_y = after(self.over, *deps)
        self.corner = swap_over(over_y[:64], BIT_X), swap_over(over_x[64:], BIT_Y)
        return self.corner

    def whole(self, *deps):
        parts = after((self.part, self.over, self.corner), *deps)
        self.near = pack_rows(parts[0], parts[1][1], parts[1][0], *parts[2])
        self.far = swap_over(self.near, BIT_CORE)
        return self.near


def rounded_sum(*terms):
    total = terms[0].astype(F32)
    for term in terms[1:]:
        total = total + term.astype(F32)
    return total.astype(BF16)


class Scatter:
    def over_core(self, far, *deps):
        return swap_over(after(far, *deps), BIT_CORE)

    def corner(self, total, *deps):
        self.total = after(total, *deps)
        self.to_x = rounded_sum(self.total[256:384], swap_over(self.total[384:], BIT_Y))
        self.to_y = self.total[128:256]
        return self.to_x

    def corners(self, total, *deps):
        self.total = total = after(total, *deps)
        from_x, from_y = swap_over(total[384:448], BIT_X), swap_over(total[448:512], BIT_Y)
        self.to_y = joined(rounded_sum(total[128:192], from_x), total[192:256])
        self.to_x = joined(total[256:320], rounded_sum(total[320:384], from_y))
        return self.to_x, self.to_y

    def sides(self, *deps):
        to_x, to_y = after((self.to_x, self.to_y), *deps)
        self.total = rounded_sum(self.total[:128], swap_over(to_y, BIT_Y), swap_over(to_x, BIT_X))
        return self.total

    def over_y(self, *deps):
        total = after(self.total, *deps)
        kept, sent = joined(total[:128], total[256:384]), joined(total[128:256], total[384:])
        self.total = rounded_sum(kept, swap_over(sent, BIT_Y))
        return self.total

    def over_x(self, *deps):
        total = after(self.total, *deps)
        self.total = rounded_sum(total[:128], swap_over(total[128:], BIT_X))
        return self.total

    def along_z1(self, *deps):
        total = after(self.total, *deps)
        self.total = rounded_sum(total[:64], swap_over(total[64:], BIT_Z1))
        return self.total

    def along_z0(self, *deps):
        total = after(self.total, *deps)
        return total[:32].astype(F32) + swap_over(total[32:], BIT_Z0).astype(F32)


def scatter_small(value):
    for rows, bit in ((512, BIT_CORE), (256, BIT_X), (128, BIT_Y), (64, BIT_Z1), (32, BIT_Z0)):
        value = value[:rows] + swap_over(value[rows:], bit)
    return value


def rotate_lanes(x, cosines, sines_up, sines_down):
    width = x.shape[1]
    return x * cosines + pltpu.roll(x, width - 16, 1) * sines_up + pltpu.roll(x, 16, 1) * sines_down


def twice(table):
    return jnp.concatenate([table, table], axis=1)


def attention_kernel(
    x_ref, qn_ref, qf_ref, kn_ref, kf_ref, vn_ref, vf_ref, b_ref, c_ref, s1_ref, s2_ref,
    q_ref, k_ref, v_ref, o_ref, l_ref
):
    def project(near_ref, far_ref):
        return dot_nn(x_ref[:, :HALF], near_ref[...]) + dot_nn(x_ref[:, HALF:], far_ref[...])

    c, s1, s2 = twice(c_ref[...]), twice(s1_ref[...]), twice(s2_ref[...])
    q = project(qn_ref, qf_ref) + b_ref[2:3, :]
    q_ref[...] = (rotate_lanes(q, c, s1, s2) * (LOG2E / 8)).astype(BF16)
    k_ref[...] = rotate_lanes(project(kn_ref, kf_ref), c, s1, s2).astype(BF16)
    v_ref[...] = (project(vn_ref, vf_ref) + b_ref[3:4, :]).astype(BF16)
    lane = lax.broadcasted_iota(jnp.int32, (1, 128), 1)
    low_half = lane < 64

    stats = jnp.zeros((ROWS, 128), F32)
    for pair in range(2):
        cols = slice(pair * 128, pair * 128 + 128)
        q_pair = q_ref[:, cols]
        k_pair, v_pair = k_ref[0:KEYS, cols], v_ref[0:KEYS, cols]
        k_class = k_ref[KEYS : KEYS + 16, cols].astype(F32)[0:1]
        v_class = v_ref[KEYS : KEYS + 16, cols].astype(F32)[0:1]
        product = q_pair.astype(F32) * k_class
        outs = []
        for h in range(2):
            own = low_half if h == 0 else ~low_half
            scores = dot_nt(jnp.where(own, q_pair, jnp.zeros_like(q_pair)), k_pair)
            class_score = jnp.sum(jnp.where(own, product, 0.0), axis=1, keepdims=True)
            peak = jnp.maximum(jnp.max(scores, axis=1, keepdims=True), class_score)
            p = jnp.exp2(scores - peak)
            class_p = jnp.exp2(class_score - peak)
            total = jnp.sum(p, axis=1, keepdims=True) + class_p
            out = dot_nn(p.astype(BF16), v_pair) + class_p * v_class
            outs.append(out * (1.0 / total))
            stats = jnp.where(lane == pair * 2 + h, peak + jnp.log2(total), stats)
        o_ref[:, cols] = jnp.where(low_half, outs[0], outs[1]).astype(BF16)
    l_ref[...] = stats.T[0:8, :]


def attention_forward(x, near, far, biases, head_block, at, tables):
    def block(index):
        return pl.BlockSpec((HALF, HEAD_COLS), lambda j: (0, index))

    def whole(a):
        return pl.BlockSpec(a.shape, lambda j: (0, 0))

    out = pl.BlockSpec((ROWS, HEAD_COLS), lambda j: (0, 0))
    return pl.pallas_call(
        attention_kernel,
        grid=(1,),
        in_specs=[whole(x)]
        + [block(at + first) for first in (0, 0, 2, 2, 4, 4)]
        + [pl.BlockSpec((8, HEAD_COLS), lambda j: (0, head_block))]
        + [whole(t) for t in tables],
        out_specs=[out] * 4 + [pl.BlockSpec((8, ROWS), lambda j: (0, 0))],
        out_shape=[jax.ShapeDtypeStruct((ROWS, HEAD_COLS), BF16)] * 4 + [jax.ShapeDtypeStruct((8, ROWS), F32)],
        compiler_params=pltpu.CompilerParams(vmem_limit_bytes=56 << 20),
        cost_estimate=cost_of(flops=7_500_000_000, bytes_accessed=7_000_000, transcendentals=4_300_000),
        name="attention_forward",
    )(x, near, far, near, far, near, far, biases, *tables)


def attention_back_kernel(
    q_ref, k_ref, v_ref, g_ref, o_ref, l_ref, c_ref, s1_ref, s2_ref,
    dq_ref, dk_ref, dv_ref, sum_ref, dq_turned, dk_sum, dv_sum, delta_ref, k_turned, *, step
):
    lane = lax.broadcasted_iota(jnp.int32, (1, 128), 1)
    low_half = lane < 64
    deltas = jnp.zeros((ROWS, 128), F32)
    for pair in range(2):
        cols = slice(pair * 128, pair * 128 + 128)
        product = g_ref[:, cols].astype(F32) * o_ref[:, cols].astype(F32)
        for h in range(2):
            own = low_half if h == 0 else ~low_half
            delta = jnp.sum(jnp.where(own, product, 0.0), axis=1, keepdims=True)
            deltas = jnp.where(lane == pair * 2 + h, delta, deltas)
    delta_ref[...] = deltas.T[0:8, :]
    real_key = lax.broadcasted_iota(jnp.int32, (ROWS, 1), 0) <= KEYS
    class_key = lax.broadcasted_iota(jnp.int32, (ROWS - KEYS, 1), 0) == 0
    k_turned[...] = k_ref[...].T
    for t in range(KEYS // step):
        rows = pl.ds(t * step, step)
        for pair in range(2):
            cols = slice(pair * 128, pair * 128 + 128)
            q_pair, g_pair = q_ref[rows, cols], g_ref[rows, cols]
            k_pair, v_pair = k_ref[:, cols], v_ref[:, cols]
            dk, dv = None, None
            for h in range(2):
                own = low_half if h == 0 else ~low_half
                head = pair * 2 + h
                q_head = jnp.where(own, q_pair, jnp.zeros_like(q_pair))
                g_head = jnp.where(own, g_pair, jnp.zeros_like(g_pair))
                scores = dot_nt(k_pair, q_head)
                log_sums = l_ref[head : head + 1, rows]
                p = jnp.concatenate(
                    [
                        jnp.exp2(scores[:KEYS] - log_sums),
                        jnp.where(class_key, jnp.exp2(scores[KEYS:] - log_sums), 0.0),
                    ],
                    axis=0,
                )
                gp = dot_nt(v_pair, g_head)
                ds = (p * (gp - delta_ref[head : head + 1, rows])).astype(BF16)
                dv_part, dk_part = dot_nn(p.astype(BF16), g_head), dot_nn(ds, q_head)
                dv = dv_part if dv is None else dv + dv_part
                dk = dk_part if dk is None else dk + dk_part
                own_rows = slice(head * 64, head * 64 + 64)
                dq_turned[own_rows, rows] = dot_nn(k_turned[own_rows, :], ds)
            if t == 0:
                dk_sum[:, cols], dv_sum[:, cols] = dk, dv
            else:
                dk_sum[:, cols] += dk
                dv_sum[:, cols] += dv
    q_class = q_ref[KEYS : KEYS + 16, :][0:1].astype(F32)
    g_class = g_ref[KEYS : KEYS + 16, :][0:1].astype(F32)
    shape = (128, HEAD_COLS)
    own = lax.broadcasted_iota(jnp.int32, shape, 0) == lax.broadcasted_iota(jnp.int32, shape, 1) // 64
    q_diag = jnp.where(own, q_class, 0.0).astype(BF16)
    g_diag = jnp.where(own, g_class, 0.0).astype(BF16)
    scores, gp = dot_nt(k_ref[...], q_diag), dot_nt(v_ref[...], g_diag)
    log_class, delta_class = jnp.zeros((1, 128), F32), jnp.zeros((1, 128), F32)
    for head in range(4):
        log_class = jnp.where(lane == head, l_ref[head : head + 1, KEYS : KEYS + 1], log_class)
        delta_class = jnp.where(lane == head, delta_ref[head : head + 1, KEYS : KEYS + 1], delta_class)
    p = jnp.where(real_key & (lane < 4), jnp.exp2(scores - log_class), 0.0)
    ds = (p * (gp - delta_class)).astype(BF16)
    dv = dv_sum[...] + dot_nn(p.astype(BF16), g_diag)
    dk = dk_sum[...] + dot_nn(ds, q_diag)
    dq_class = jnp.sum(jnp.where(own, dot_tn(ds, k_ref[...]), 0.0), axis=0, keepdims=True)
    first = lax.broadcasted_iota(jnp.int32, (16, 1), 0) == 0
    dq = jnp.concatenate([dq_turned[...].T, jnp.where(first, dq_class, 0.0)], axis=0)
    c, s1, s2 = twice(c_ref[...]), twice(s1_ref[...]), twice(s2_ref[...])
    dq = (rotate_lanes(dq, c, -s1, -s2) * 0.125).astype(BF16)
    dv = dv.astype(BF16)
    dq_ref[...] = dq
    dk_ref[...] = (rotate_lanes(dk, c, -s1, -s2) * (1.0 / LOG2E)).astype(BF16)
    dv_ref[...] = dv
    sum_ref[0:1, :] = jnp.sum(dq.astype(F32), axis=0, keepdims=True)
    sum_ref[1:2, :] = jnp.sum(dv.astype(F32), axis=0, keepdims=True)
    sum_ref[2:8, :] = jnp.zeros((6, HEAD_COLS), F32)


def attention_backward(q, k, v, o, log_sums, g, tables, step=256):
    def whole(a):
        return pl.BlockSpec(a.shape, lambda j: (0, 0))

    block = pl.BlockSpec((ROWS, HEAD_COLS), lambda j: (0, 0))
    return pl.pallas_call(
        functools.partial(attention_back_kernel, step=step),
        grid=(1,),
        in_specs=[block] * 5 + [pl.BlockSpec((8, ROWS), lambda j: (0, 0))] + [whole(t) for t in tables],
        out_specs=[block] * 3 + [pl.BlockSpec((8, HEAD_COLS), lambda j: (0, 0))],
        out_shape=[jax.ShapeDtypeStruct((ROWS, HEAD_COLS), BF16)] * 3
        + [jax.ShapeDtypeStruct((8, HEAD_COLS), F32)],
        scratch_shapes=[pltpu.VMEM((HEAD_COLS, KEYS), F32)]
        + [pltpu.VMEM((ROWS, HEAD_COLS), F32)] * 2
        + [pltpu.VMEM((8, ROWS), F32), pltpu.VMEM((HEAD_COLS, ROWS), BF16)],
        compiler_params=pltpu.CompilerParams(vmem_limit_bytes=48 << 20),
        cost_estimate=cost_of(
            flops=13_000_000_000, bytes_accessed=5_000_000, transcendentals=4_300_000
        ),
        name="attention_backward",
    )(q, k, v, g, o, log_sums, *tables)


def over_rows(kernel, name, tiled, held, outs, sums=(), flops=0, step=STEP, only=None):
    rows = ROWS if only is None else step
    if only is None:
        in_specs = [pl.BlockSpec((step, a.shape[1]), lambda i: (i, 0)) for a in tiled]
    else:
        in_specs = [
            pl.BlockSpec((pl.Element(step), pl.Element(a.shape[1])), lambda i: (only, 0)) for a in tiled
        ]
    held = [h if isinstance(h, tuple) else (h, h.shape, 0) for h in held]
    in_specs += [
        pl.BlockSpec(shape, lambda i, column=column: (0, column), pipeline_mode=pl.Buffered(1))
        for _, shape, column in held
    ]
    held = [h[0] for h in held]
    out_specs = [pl.BlockSpec((step, n), lambda i: (i, 0)) for n, _ in outs]
    out_specs += [pl.BlockSpec((8, n), lambda i: (0, 0)) for n in sums]
    out_shape = [jax.ShapeDtypeStruct((rows, n), t) for n, t in outs]
    out_shape += [jax.ShapeDtypeStruct((8, n), F32) for n in sums]
    moved = sum(a.size * a.dtype.itemsize for a in list(tiled) + list(held))
    moved += sum(s.size * s.dtype.itemsize for s in out_shape)
    return pl.pallas_call(
        kernel,
        grid=(rows // step,),
        in_specs=in_specs,
        out_specs=out_specs,
        out_shape=out_shape,
        compiler_params=pltpu.CompilerParams(vmem_limit_bytes=56 << 20),
        cost_estimate=cost_of(flops=flops, bytes_accessed=moved, transcendentals=0),
        name=name,
    )(*tiled, *held)


def add_sums(ref, *rows):
    @pl.when(pl.program_id(0) == 0)
    def _():
        ref[...] = jnp.zeros_like(ref)

    for i, value in enumerate(rows):
        ref[i : i + 1, :] += jnp.sum(value, axis=0, keepdims=True)


def unit_norm(values):
    centred = values - jnp.mean(values, axis=-1, keepdims=True)
    inv_std = lax.rsqrt(jnp.mean(centred * centred, axis=-1, keepdims=True) + epsilon)
    return centred * inv_std, inv_std


def unit_norm_back(scaled, unit, inv_std):
    return inv_std * (
        scaled
        - jnp.mean(scaled, axis=-1, keepdims=True)
        - unit * jnp.mean(scaled * unit, axis=-1, keepdims=True)
    )


def vectors_kernel(near_ref, far_ref, order_ref, vec_ref, head_ref):
    rows = jnp.concatenate([near_ref[...].astype(F32).T, far_ref[...].astype(F32).T], axis=1)[0:8]
    vec_ref[...] = rows
    head_ref[...] = dot_nt(rows.astype(BF16), order_ref[...])


def gathered_vectors(near, far, order):
    block = pl.BlockSpec((HALF, 128), lambda j: (0, 3 * HALF // 128))
    out = pl.BlockSpec((8, WIDTH), lambda j: (0, 0))
    return pl.pallas_call(
        vectors_kernel,
        grid=(1,),
        in_specs=[block, block, pl.BlockSpec(order.shape, lambda j: (0, 0))],
        out_specs=[out, out],
        out_shape=[jax.ShapeDtypeStruct((8, WIDTH), F32)] * 2,
        cost_estimate=cost_of(flops=40_000_000, bytes_accessed=2_400_000, transcendentals=0),
        name="vectors",
    )(near, far, order)


def sigmoid_of(x):
    return 0.5 * jnp.tanh(0.5 * x) + 0.5


def start_kernel(rows_ref, order_ref, vec_ref, tokens_ref, normed_ref):
    tokens = dot_nn(rows_ref[...], order_ref[...])
    tokens_ref[...] = tokens.astype(BF16)
    unit, _ = unit_norm(tokens)
    normed_ref[...] = (unit * vec_ref[0:1, :] + vec_ref[1:2, :]).astype(BF16)


def middle_kernel(a0_ref, a1_ref, a2_ref, a3_ref, tokens_ref, na_ref, nb_ref, fa_ref, fb_ref, vec_ref, middle_ref, normed_ref):
    low = jnp.concatenate([a0_ref[...], a1_ref[...]], axis=1)
    high = jnp.concatenate([a2_ref[...], a3_ref[...]], axis=1)
    branch = jnp.concatenate(
        [
            dot_nt(low, na_ref[...]) + dot_nt(high, nb_ref[...]),
            dot_nt(low, fa_ref[...]) + dot_nt(high, fb_ref[...]),
        ],
        axis=1,
    )
    middle = tokens_ref[...].astype(F32) + (branch + vec_ref[4:5, :])
    middle_ref[...] = middle.astype(BF16)
    unit, _ = unit_norm(middle)
    normed_ref[...] = (unit * vec_ref[5:6, :] + vec_ref[6:7, :]).astype(BF16)


def hidden_kernel(x_ref, gn_ref, gf_ref, un_ref, uf_ref, ffn_ref, gate_ref, up_ref, inner_ref, stat_ref, *, hidden):
    near, far = x_ref[:, :HALF], x_ref[:, HALF:]
    gate = dot_nn(near, gn_ref[...]) + dot_nn(far, gf_ref[...]) + ffn_ref[0:1, :]
    up = dot_nn(near, un_ref[...]) + dot_nn(far, uf_ref[...]) + ffn_ref[1:2, :]
    gate_ref[...] = gate.astype(gate_ref.dtype)
    up_ref[...] = up.astype(up_ref.dtype)
    mix = gate * sigmoid_of(gate) * up
    mean = jnp.sum(mix, axis=1, keepdims=True) * (1.0 / hidden)
    real = lax.broadcasted_iota(jnp.int32, (1, mix.shape[1]), 1) < hidden
    centred = jnp.where(real, mix - mean, 0.0)
    inv_std = lax.rsqrt(jnp.sum(centred * centred, axis=1, keepdims=True) * (1.0 / hidden) + epsilon)
    inner_ref[...] = (centred * inv_std * ffn_ref[2:3, :] + ffn_ref[3:4, :]).astype(BF16)
    lane = lax.broadcasted_iota(jnp.int32, (1, 128), 1)
    stat_ref[...] = jnp.where(lane == 0, mean, inv_std)


def result_kernel(inner_ref, middle_ref, near_ref, far_ref, vec_ref, order_ref, keep_ref, out_ref):
    inner = inner_ref[...]
    branch = jnp.concatenate([dot_nt(inner, near_ref[...]), dot_nt(inner, far_ref[...])], axis=1)
    result = middle_ref[...].astype(F32) + (branch + vec_ref[7:8, :])
    rounded = (result * keep_ref[0:1, 0:1]).astype(BF16)
    out_ref[...] = dot_nt(rounded, order_ref[...]).astype(BF16)


def hidden_back_kernel(
    d_ref, gate_ref, up_ref, stat_ref, order_ref, keep_ref, near_ref, far_ref, ffn_ref,
    branch_ref, dgate_ref, dup_ref, wide_ref, sum_ref, *, hidden
):
    branch = (dot_nn(d_ref[...], order_ref[...]) * keep_ref[0:1, 0:1]).astype(BF16)
    branch_ref[...] = branch
    g_inner = dot_nn(branch[:, :HALF], near_ref[...]) + dot_nn(branch[:, HALF:], far_ref[...])
    gate, up = gate_ref[...].astype(F32), up_ref[...].astype(F32)
    sigmoid = sigmoid_of(gate)
    silu = gate * sigmoid
    mean, inv_std = stat_ref[:, 0:1], stat_ref[:, 1:2]
    unit = (silu * up - mean) * inv_std
    g_unit = g_inner * ffn_ref[2:3, :]
    share = 1.0 / hidden
    g_mix = inv_std * (
        g_unit
        - jnp.sum(g_unit, axis=1, keepdims=True) * share
        - unit * (jnp.sum(g_unit * unit, axis=1, keepdims=True) * share)
    )
    d_gate = (g_mix * up * (sigmoid * (1.0 + gate * (1.0 - sigmoid)))).astype(BF16)
    d_up = (g_mix * silu).astype(BF16)
    dgate_ref[...] = d_gate
    dup_ref[...] = d_up
    add_sums(wide_ref, d_gate.astype(F32), d_up.astype(F32), g_inner * unit, g_inner)
    add_sums(sum_ref, branch.astype(F32))


def middle_back_kernel(
    dgate_ref, dup_ref, branch_ref, middle_ref, gn_ref, gf_ref, un_ref, uf_ref, na_ref, nb_ref, fa_ref, fb_ref, vec_ref,
    low_ref, d0_ref, d1_ref, d2_ref, d3_ref, sum_ref
):
    d_gate, d_up = dgate_ref[...], dup_ref[...]
    g_two = jnp.concatenate(
        [
            dot_nt(d_gate, gn_ref[...]) + dot_nt(d_up, un_ref[...]),
            dot_nt(d_gate, gf_ref[...]) + dot_nt(d_up, uf_ref[...]),
        ],
        axis=1,
    )
    unit, inv_std = unit_norm(middle_ref[...].astype(F32))
    g_middle = branch_ref[...].astype(F32) + unit_norm_back(g_two * vec_ref[5:6, :], unit, inv_std)
    low = g_middle.astype(BF16)
    low_ref[...] = low
    near, far = low[:, :HALF], low[:, HALF:]
    d_low = (dot_nn(near, na_ref[...]) + dot_nn(far, fa_ref[...])).astype(BF16)
    d_high = (dot_nn(near, nb_ref[...]) + dot_nn(far, fb_ref[...])).astype(BF16)
    d0_ref[...], d1_ref[...] = d_low[:, :HEAD_COLS], d_low[:, HEAD_COLS:]
    d2_ref[...], d3_ref[...] = d_high[:, :HEAD_COLS], d_high[:, HEAD_COLS:]
    add_sums(sum_ref, low.astype(F32), g_two * unit, g_two)


def last_kernel(*refs):
    grads = refs[:12]
    gmid_ref, tokens_ref, an_ref, af_ref, bn_ref, bf_ref, vec_ref, order_ref, grad_ref, sum_ref = refs[12:]

    def back(low_w, high_w):
        total = 0.0
        for first, w_ref in ((0, low_w), (6, high_w)):
            for i in range(3):
                g = jnp.concatenate([grads[first + i][...], grads[first + 3 + i][...]], axis=1)
                total = total + dot_nt(g, w_ref[:, i * HALF : i * HALF + HALF])
        return total

    g_one = jnp.concatenate([back(an_ref, bn_ref), back(af_ref, bf_ref)], axis=1)
    unit, inv_std = unit_norm(tokens_ref[...].astype(F32))
    grad = gmid_ref[...].astype(F32) + unit_norm_back(g_one * vec_ref[0:1, :], unit, inv_std)
    grad_ref[...] = dot_nt(grad.astype(BF16), order_ref[...]).astype(BF16)
    add_sums(sum_ref, g_one * unit, g_one)


def weight_grads(half, steps, received=None):
    sources, arrays = [], []
    for x, gs in steps:
        if not any(x is s for s in sources):
            sources.append(x)
        for g, _, _ in gs:
            if not any(g is a for a in arrays):
                arrays.append(g)
    tile = sum(width for _, width, _ in steps[0][1])
    refs_of, specs, operands = [], [], []
    for j, (x, gs) in enumerate(steps):
        mine = []
        for g, width, at in gs:
            found = next((i for i, o in enumerate(operands) if o[0] is g and o[1] == width), None)
            if found is None:
                operands.append((g, width, {}))
                found = len(operands) - 1
            operands[found][2][j] = at
            mine.append(found)
        refs_of.append(mine)
    for g, width, places in operands:
        known = sorted(places.items())

        def index(j, known=known):
            at = known[0][1]
            for step, place in known[1:]:
                at = jnp.where(j >= step, place, at)
            return 0, at

        specs.append(pl.BlockSpec((ROWS, width), index))
    plus = [] if received is None else [received]

    def kernel(*refs):
        xs, gs = refs[: len(sources)], refs[len(sources) : len(sources) + len(operands)]
        out_ref, turned, last = refs[-3:]
        step = pl.program_id(0)
        for j, (x, _) in enumerate(steps):
            source = next(i for i, s in enumerate(sources) if s is x)
            fresh = j == 0 or steps[j - 1][0] is not x

            @pl.when(step == j)
            def _(j=j, source=source, fresh=fresh):
                if fresh:
                    turned[...] = xs[source][0:KEYS, :].T
                    last[...] = xs[source][KEYS:ROWS, :].astype(F32).T
                parts = [gs[r] for r in refs_of[j]]
                main = jnp.concatenate([p[0:KEYS, :] for p in parts], axis=1)
                row = jnp.concatenate([p[KEYS:ROWS, :].astype(F32)[0:1] for p in parts], axis=1)
                out = dot_nn(turned[...], main) + last[:, 0:1] * row
                if plus:
                    out = out + refs[len(sources) + len(operands)][...].astype(F32)
                out_ref[...] = out.astype(BF16)

    block = pl.BlockSpec((HALF, tile), lambda j: (0, j))
    columns = len(steps) * tile
    return pl.pallas_call(
        kernel,
        grid=(len(steps),),
        in_specs=[pl.BlockSpec((ROWS, HALF), lambda j: (0, half), pipeline_mode=pl.Buffered(1)) for _ in sources]
        + specs
        + [block] * len(plus),
        out_specs=block,
        out_shape=jax.ShapeDtypeStruct((HALF, columns), BF16),
        scratch_shapes=[pltpu.VMEM((HALF, KEYS), BF16), pltpu.VMEM((HALF, ROWS - KEYS), F32)],
        compiler_params=pltpu.CompilerParams(vmem_limit_bytes=48 << 20),
        cost_estimate=cost_of(
            flops=ROWS * WIDTH * columns, bytes_accessed=3 * ROWS * columns, transcendentals=0
        ),
        name="weight_grads",
    )(*sources, *[g for g, _, _ in operands], *plus)


def pair_tables(coords):
    lane = jnp.arange(128)
    freqs = 10000.0 ** (-(lane % 16).astype(F32) / 16.0)
    along_rows = (lane % 64 < 32)[None, :]
    places = jnp.where(along_rows, coords[:, 0:1], coords[:, 1:2]).astype(F32)
    angles = jnp.pad(places * freqs[None, :], ((0, ROWS - KEYS), (0, 0)))
    cosines, sines = jnp.cos(angles), jnp.sin(angles)
    even = (lane % 32 < 16)[None, :]
    return cosines, jnp.where(even, -sines, 0.0), jnp.where(even, 0.0, sines)


def feature_order(me):
    natural = lax.broadcasted_iota(jnp.int32, (WIDTH, WIDTH), 0)
    place = lax.broadcasted_iota(jnp.int32, (WIDTH, WIDTH), 1)
    block = place // 32
    owner = (
        (block // 16) * BIT_CORE
        + (block // 8 % 2) * BIT_X
        + (block // 4 % 2) * BIT_Y
        + (block // 2 % 2) * BIT_Z1
        + (block % 2) * BIT_Z0
    ) ^ me
    return (natural == owner * 32 + place % 32).astype(BF16)


def paired_device(
    patch_in, cls_in, d_patch, d_cls, image_valid, patch_coords,
    w_query, w_key, w_value, w_gate, w_up, w_out, w_down, layer_vectors, ffn_vectors,
):
    SENT.clear()
    me, pos = lax.axis_index(BOTH), lax.axis_index("ctx")
    hidden = w_gate.shape[1]
    wide = (hidden + 255) // 256 * 256
    extra = ((0, 0), (0, wide - hidden))

    def own_image(patches, classes, *deps):
        near = lax.dynamic_index_in_dim(patches, pos, 0, keepdims=False)
        sent = after(lax.dynamic_index_in_dim(patches, 1 - pos, 0, keepdims=False), *deps)
        far = swap_over(sent, BIT_X)
        class_row = lax.dynamic_index_in_dim(classes, pos, 0)
        return joined(near, far, jnp.pad(class_row, ((0, ROWS - KEYS - 1), (0, 0)))), far

    def to_pair(rows, far):
        near = rows[:512]
        is_first = pos == 0
        near_class, far_class = rows[KEYS], far[512]
        patches = jnp.where(is_first, jnp.stack([near, far[:512]]), jnp.stack([far[:512], near]))
        classes = jnp.where(is_first, jnp.stack([near_class, far_class]), jnp.stack([far_class, near_class]))
        return patches, classes

    vectors_local = jnp.pad(layer_vectors.T, ((0, 0), (0, 120)))
    low_heads = [w[:, :HALF] for w in (w_query, w_key, w_value)]
    high_heads = [w[:, HALF:] for w in (w_query, w_key, w_value)]
    g_low = Gather(joined(*low_heads, vectors_local, axis=1))
    g_high = Gather(joined(*high_heads, w_out.T, axis=1))
    g_gate = Gather(jnp.pad(w_gate, extra))
    g_up = Gather(jnp.pad(w_up, extra))
    g_down = Gather(jnp.pad(w_down.T, extra))

    image_rows, image_far = own_image(patch_in, cls_in)
    coords = joined(patch_coords, swap_over(patch_coords, BIT_X))
    order = feature_order(me)
    tables = pair_tables(coords)
    keep = lax.dynamic_index_in_dim(image_valid, pos, 0, keepdims=False).astype(F32)
    keep = jnp.full((8, 128), keep, F32)
    ffn = jnp.pad(ffn_vectors.astype(F32), ((0, 4), (0, wide - hidden)))

    z_one = g_low.along_z0()
    z_low = g_low.along_z1()
    z_one = g_high.along_z0(z_one)
    z_one = g_gate.along_z0(z_one)
    xy_low = g_low.along_xy()
    z_high = g_high.along_z1(z_low)
    corner_low = g_low.corners(image_far)
    xy_high = g_high.along_xy(xy_low)
    near_low = g_low.whole(z_high)

    gate = near_low, g_low.far, image_rows, z_one, xy_high
    z_gate = g_gate.along_z1(gate)
    corner_high = g_high.corners(gate)
    vectors, head_biases = gathered_vectors(near_low, g_low.far, order)
    tokens, normed = over_rows(
        start_kernel, "start", [ready(image_rows, gate)], [order, vectors], [(WIDTH, BF16), (WIDTH, BF16)],
        flops=2_200_000_000,
    )

    def attend(block, gate):
        group = g_low if block < 2 else g_high
        return attention_forward(
            ready(normed, gate), group.near, group.far, head_biases, block, block % 2, tables
        )

    gate = normed, z_gate, corner_high
    z_up = g_up.along_z0(gate)
    near_high = g_high.whole(gate)
    xy_gate = g_gate.along_xy(gate)
    heads = [attend(0, gate)]

    gate = heads[0][3], xy_gate, z_up
    corner_gate = g_gate.corners(gate)
    z_up = g_up.along_z1(gate)
    heads.append(attend(1, gate))

    gate = heads[1][3], g_high.far, corner_gate, z_up
    near_gate = g_gate.whole(gate)
    xy_up = g_up.along_xy(gate)
    z_down = g_down.along_z0(gate)
    heads.append(attend(2, gate))

    gate = heads[2][3], xy_up, g_gate.far, z_down
    corner_up = g_up.corners(gate)
    z_down = g_down.along_z1(gate)
    heads.append(attend(3, gate))

    gate = heads[3][3], corner_up, z_down
    near_up = g_up.whole(gate)
    xy_down = g_down.along_xy(gate)
    out_w = [((w, (HALF, HALF), 3 + i)) for w in (near_high, g_high.far) for i in range(2)]
    attended = [h[3] for h in heads]
    middle, normed_two = over_rows(
        middle_kernel, "middle", attended + [ready(tokens, gate)], out_w + [vectors],
        [(WIDTH, BF16), (WIDTH, BF16)], flops=2_200_000_000, step=520,
    )

    gate = normed_two, g_up.far, xy_down
    corner_down = g_down.corners(gate)
    grad_image_rows, grad_far = own_image(d_patch, d_cls, gate)
    gate_up = [near_gate, g_gate.far, near_up, g_up.far]
    gate_act, up_act, inner, stats = over_rows(
        functools.partial(hidden_kernel, hidden=hidden), "hidden", [ready(normed_two, gate)],
        gate_up + [ffn], [(wide, BF16), (wide, BF16), (wide, BF16), (128, F32)], flops=12_000_000_000,
    )

    gate = inner, corner_down, grad_far
    near_down = g_down.whole(gate)
    down_w = [near_down, g_down.far]
    (out_rows,) = over_rows(
        result_kernel, "result", [inner, ready(middle, gate)], down_w + [vectors, order, keep],
        [(WIDTH, BF16)], flops=8_000_000_000, step=520,
    )

    gate = out_rows
    far_rows = swap_over(after(out_rows, gate)[HALF:], BIT_X)
    branch, d_gate, d_up, wide_sums, branch_sums = over_rows(
        functools.partial(hidden_back_kernel, hidden=hidden), "hidden_back",
        [ready(grad_image_rows, gate), gate_act, up_act, stats], [order, keep] + down_w + [ffn],
        [(WIDTH, BF16), (wide, BF16), (wide, BF16)], [wide, WIDTH], flops=8_000_000_000,
    )

    gate = wide_sums, far_rows
    outs = to_pair(after(out_rows, far_rows), far_rows)
    all_sums = lax.all_gather(wide_sums, BOTH)
    part_width = wide // 2
    down, second, low, high = Scatter(), Scatter(), Scatter(), Scatter()
    late = ready(normed_two, gate)
    second_steps = [(late, [(g, part_width, i)]) for g in (d_gate, d_up) for i in range(2)]
    second_far = weight_grads(1, second_steps)

    gate = second_far
    second_stage = second.over_core(second_far, gate)
    late = ready(branch, gate)
    down_steps = [(late, [(inner, part_width, i)]) for i in range(2)]
    down_far = weight_grads(1, down_steps)

    gate = down_far, second_stage
    down_stage = down.over_core(down_far, gate)
    late = ready(normed_two, gate)
    second_total = weight_grads(0, [(late, gs) for _, gs in second_steps], second_stage)

    gate = second_total, down_stage
    second_stage = second.corners(second_total, gate)
    late = ready(branch, gate)
    down_total = weight_grads(0, [(late, gs) for _, gs in down_steps], down_stage)

    gate = down_total, second_stage
    second_stage = second.sides(gate)
    att_low, *att_grads, middle_sums = over_rows(
        middle_back_kernel, "middle_back", [d_gate, d_up, branch, ready(middle, gate)],
        gate_up + out_w + [vectors], [(WIDTH, BF16)] + [(HEAD_COLS, BF16)] * 4, [WIDTH],
        flops=14_000_000_000, step=520,
    )

    def attend_back(block, gate):
        return attention_backward(*heads[block], ready(att_grads[block], gate), tables)

    gate = att_low, second_stage
    second_stage, down_stage = second.along_z1(gate), down.corners(down_total, gate)
    parts = [attend_back(0, gate)]

    gate = parts[0][0], second_stage, down_stage
    gate_up_grad, down_stage = second.along_z0(gate), down.sides(gate)
    parts.append(attend_back(1, gate))

    def pieces(*arrays):
        return [(a, HEAD_COLS, 0) for a in arrays]

    gate = parts[1][0], gate_up_grad, down_stage
    down_stage = down.along_z1(gate)
    late, late_two = ready((att_low, normed), gate)
    grads = [g for part in parts for g in part[:3]]
    low_steps = [(late, pieces(*attended[2 * i : 2 * i + 2])) for i in range(2)]
    low_steps += [(late_two, pieces(*grads[2 * i : 2 * i + 2])) for i in range(3)]
    low_far = weight_grads(1, low_steps)

    gate = low_far, down_stage
    low_stage, down_grad = low.over_core(low_far, gate), down.along_z0(gate)
    parts.append(attend_back(2, gate))

    gate = parts[2][0], low_stage, down_grad
    late, late_two = ready((att_low, normed), gate)
    low_total = weight_grads(
        0, [(late if i < 2 else late_two, gs) for i, (_, gs) in enumerate(low_steps)], low_stage
    )

    gate = low_total
    low_stage = low.corner(low_total, gate)
    parts.append(attend_back(3, gate))

    gate = parts[3][0], low_stage
    low_stage = low.sides(gate)
    late = ready(normed, gate)
    grads = [g for part in parts[2:] for g in part[:3]]
    high_steps = [(late, pieces(*grads[2 * i : 2 * i + 2])) for i in range(3)]
    high_far = weight_grads(1, high_steps)
    high_stage = high.over_core(high_far)

    def last_rows(gate, first, count):
        return over_rows(
            last_kernel, "last",
            [g for part in parts for g in part[:3]] + [ready(att_low, gate), tokens],
            [(near_low, (HALF, 3 * HALF), 0), (g_low.far, (HALF, 3 * HALF), 0)]
            + [(near_high, (HALF, 3 * HALF), 0), (g_high.far, (HALF, 3 * HALF), 0), vectors, order],
            [(WIDTH, BF16)], [WIDTH], flops=4_500_000_000, step=count, only=first,
        )

    far_part, far_sums = last_rows(high_far, HALF, ROWS - HALF)

    gate = far_part, high_stage, low_stage
    low_stage = low.along_z1(gate)
    late = ready(normed, gate)
    high_total = weight_grads(0, [(late, gs) for _, gs in high_steps], high_stage)

    gate = high_total
    high.total = high_total
    far_rows = swap_over(after(far_part, gate), BIT_X)
    high_stage = high.over_y(gate)
    near_part, near_sums = last_rows(gate, 0, HALF)

    gate = near_part, low_stage, high_stage, far_rows
    low_grad = low.along_z0(gate)
    high.over_x(gate)
    high.along_z1()
    high_grad = high.along_z0()
    sums = [far_sums, near_sums, middle_sums, branch_sums] + [part[3] for part in parts]
    far_sums, near_sums, middle_sums, branch_sums, *head_sums = after(sums, far_rows)
    patch_grad, cls_grad = to_pair(after(joined(near_part, far_part), far_rows), far_rows)
    ffn_grads = jnp.sum(after(all_sums, far_rows), axis=0)[:4, :hidden]
    head_sums = jnp.dot(
        joined(*[part[:2] for part in head_sums], axis=1), order.astype(F32), precision=lax.Precision.HIGHEST
    )
    vector_grads = scatter_small(
        joined((far_sums + near_sums)[:2], head_sums, middle_sums[:3], branch_sums[:1]).T
    )
    blocks = [low_grad[:, WIDTH + i * HEAD_COLS :][:, :HEAD_COLS] for i in range(6)]
    blocks += [high_grad[:, i * HEAD_COLS :][:, :HEAD_COLS] for i in range(6)]
    query_grad, key_grad, value_grad = (joined(*blocks[i::3], axis=1) for i in range(3))
    return (
        outs[0],
        outs[1],
        patch_grad,
        cls_grad,
        query_grad,
        key_grad,
        value_grad,
        gate_up_grad[:, :hidden],
        gate_up_grad[:, wide : wide + hidden],
        low_grad[:, :WIDTH].T,
        down_grad[:, :hidden].T,
        vector_grads.T,
        ffn_grads,
    )


def solution(mesh):
    in_specs = (
        P("dp", "ctx", None),
        P("dp", None),
        P("dp", "ctx", None),
        P("dp", None),
        P("dp"),
        P("ctx", None),
        P(("dp", "ctx"), None),
        P(("dp", "ctx"), None),
        P(("dp", "ctx"), None),
        P(("dp", "ctx"), None),
        P(("dp", "ctx"), None),
        P(None, ("dp", "ctx")),
        P(None, ("dp", "ctx")),
        P(None, ("dp", "ctx")),
        P(),
    )
    out_specs = (
        P("dp", "ctx", None),
        P("dp", None),
        P("dp", "ctx", None),
        P("dp", None),
        P(("dp", "ctx"), None),
        P(("dp", "ctx"), None),
        P(("dp", "ctx"), None),
        P(("dp", "ctx"), None),
        P(("dp", "ctx"), None),
        P(None, ("dp", "ctx")),
        P(None, ("dp", "ctx")),
        P(None, ("dp", "ctx")),
        P(),
    )
    sizes = dict(mesh.shape)
    pairs = sizes["dp"] == 16 and sizes["ctx"] == 2
    body = paired_device if pairs else on_device
    return jax.shard_map(
        body, mesh=mesh, in_specs=in_specs, out_specs=out_specs, check_vma=False
    )
```

```python
import functools
import math

import jax
import jax.numpy as jnp
from jax import lax
from jax.experimental import pallas as pl
from jax.experimental.pallas import tpu as pltpu
from jax.sharding import PartitionSpec as P

HD = 64
MICRO = 2


epsilon = 1e-06


def layer_norm(values, gain, shift):
    centred = values - jnp.mean(values, axis=-1, keepdims=True)
    inv_std = lax.rsqrt(jnp.mean(centred * centred, axis=-1, keepdims=True) + epsilon)
    unit_rows = centred * inv_std
    return (unit_rows * gain + shift, unit_rows, inv_std)


def norm_back(grad_out, gain, unit_rows, inv_std, row_mask):
    scaled = grad_out * gain
    grad_in = inv_std * (
        scaled
        - jnp.mean(scaled, axis=-1, keepdims=True)
        - unit_rows * jnp.mean(scaled * unit_rows, axis=-1, keepdims=True)
    )
    weighted = grad_out * row_mask
    return (grad_in, jnp.sum(weighted * unit_rows, axis=(0, 1)), jnp.sum(weighted, axis=(0, 1)))


def rotary_tables(coords):
    freqs = 10000.0 ** (-jnp.arange(16).astype(jnp.float32) / 16.0)
    along_rows = coords[:, 0:1].astype(jnp.float32) * freqs[None, :]
    along_cols = coords[:, 1:2].astype(jnp.float32) * freqs[None, :]
    angles = jnp.concatenate([along_rows, along_rows, along_cols, along_cols], axis=1)
    cosines = jnp.concatenate([jnp.ones((1, 64), jnp.float32), jnp.cos(angles)], axis=0)
    sines = jnp.concatenate([jnp.zeros((1, 64), jnp.float32), jnp.sin(angles)], axis=0)
    return (cosines, sines)


def rotate(values, cosines, sines):
    swapped = jnp.concatenate(
        [-values[..., 16:32], values[..., 0:16], -values[..., 48:64], values[..., 32:48]], axis=-1
    )
    return values * cosines[:, None, :] + swapped * sines[:, None, :]


def unrotate(grads, cosines, sines):
    with_sin = grads * sines[:, None, :]
    moved = jnp.concatenate(
        [with_sin[..., 16:32], -with_sin[..., 0:16], with_sin[..., 48:64], -with_sin[..., 32:48]],
        axis=-1,
    )
    return grads * cosines[:, None, :] + moved


def project(rows_in, weight):
    return jnp.einsum("brd,de->bre", rows_in, weight, preferred_element_type=jnp.float32)


def project_back(grads, weight):
    return jnp.einsum("bre,de->brd", grads, weight, preferred_element_type=jnp.float32)


def weight_grad(rows_in, grads):
    return jnp.einsum("brd,bre->de", rows_in, grads, preferred_element_type=jnp.float32)


def fetch_forward(w_query, w_key, w_value, w_gate, w_up, w_out, w_down, layer_vectors):
    first_group = (
        lax.all_gather(w_query, ("dp", "ctx"), axis=0, tiled=True),
        lax.all_gather(w_key, ("dp", "ctx"), axis=0, tiled=True),
        lax.all_gather(w_value, ("dp", "ctx"), axis=0, tiled=True),
        lax.all_gather(w_gate, ("dp", "ctx"), axis=0, tiled=True),
        lax.all_gather(w_up, ("dp", "ctx"), axis=0, tiled=True),
    )
    second_group = (
        lax.all_gather(w_out, ("dp", "ctx"), axis=1, tiled=True),
        lax.all_gather(w_down, ("dp", "ctx"), axis=1, tiled=True),
        lax.all_gather(layer_vectors, ("dp", "ctx"), axis=1, tiled=True),
    )
    return tuple(first_group) + tuple(second_group)


def fetch_backward(w_query, w_key, w_value, w_gate, w_up, w_out, w_down, layer_vectors):
    first_group = (
        lax.all_gather(w_query, ("dp", "ctx"), axis=0, tiled=True),
        lax.all_gather(w_key, ("dp", "ctx"), axis=0, tiled=True),
        lax.all_gather(w_value, ("dp", "ctx"), axis=0, tiled=True),
        lax.all_gather(w_gate, ("dp", "ctx"), axis=0, tiled=True),
        lax.all_gather(w_up, ("dp", "ctx"), axis=0, tiled=True),
    )
    second_group = (
        lax.all_gather(w_out, ("dp", "ctx"), axis=1, tiled=True),
        lax.all_gather(w_down, ("dp", "ctx"), axis=1, tiled=True),
        lax.all_gather(layer_vectors, ("dp", "ctx"), axis=1, tiled=True),
    )
    return tuple(first_group) + tuple(second_group)


def head_forward(item):
    block_of_queries, block_of_keys, block_of_values = item
    logit_scores = jnp.einsum(
        "wey,wmy->wem", block_of_queries, block_of_keys, preferred_element_type=jnp.float32
    )
    row_peak = jnp.max(logit_scores, axis=-1, keepdims=True)
    shifted = jnp.exp(logit_scores - row_peak)
    denominator = jnp.sum(shifted, axis=-1, keepdims=True)
    reduced_probabilities = (shifted / denominator).astype(jnp.bfloat16)
    blended_values = jnp.einsum(
        "sce,sem->scm", reduced_probabilities, block_of_values, preferred_element_type=jnp.float32
    )
    return (blended_values, (row_peak + jnp.log(denominator))[..., 0])


def forward_pass(tokens, weights, ffn_vec, cosines, sines):
    w_query, w_key, w_value, w_gate, w_up, w_out, w_down, vectors_low = weights
    vectors = vectors_low.astype(jnp.float32)
    batch, row_count, model_width = tokens.shape
    heads = model_width // HD
    normed, unit_one, std_one = layer_norm(tokens, vectors[0], vectors[1])
    normed_low = normed.astype(jnp.bfloat16)
    queries = project(normed_low, w_query) + vectors[2]
    keys_raw = project(normed_low, w_key)
    values_low = (project(normed_low, w_value) + vectors[3]).astype(jnp.bfloat16)
    q_rot = (
        rotate(queries.reshape(batch, row_count, heads, HD), cosines, sines) * HD ** (-0.5)
    ).astype(jnp.bfloat16)
    k_flat = (
        rotate(keys_raw.reshape(batch, row_count, heads, HD), cosines, sines)
        .astype(jnp.bfloat16)
        .reshape(batch, row_count, model_width)
    )
    far_keys, far_values = (
        lax.all_gather(k_flat[:, 1:], "ctx", axis=1, tiled=True),
        lax.all_gather(values_low[:, 1:], "ctx", axis=1, tiled=True),
    )
    all_keys = jnp.concatenate([k_flat[:, :1], far_keys], axis=1)
    all_values = jnp.concatenate([values_low[:, :1], far_values], axis=1)
    length = all_keys.shape[1]
    head_queries = q_rot.transpose(2, 0, 1, 3)
    head_keys = all_keys.reshape(batch, length, heads, HD).transpose(2, 0, 1, 3)
    head_values = all_values.reshape(batch, length, heads, HD).transpose(2, 0, 1, 3)
    head_out, log_sums = lax.map(head_forward, (head_queries, head_keys, head_values))
    attended = (
        head_out.transpose(1, 2, 0, 3).reshape(batch, row_count, model_width).astype(jnp.bfloat16)
    )
    middle = tokens + (project(attended, w_out) + vectors[4])
    normed_two, unit_two, std_two = layer_norm(middle, vectors[5], vectors[6])
    normed_two_low = normed_two.astype(jnp.bfloat16)
    gate_proj = project(normed_two_low, w_gate) + ffn_vec[0]
    up_proj = project(normed_two_low, w_up) + ffn_vec[1]
    activated = jax.nn.silu(gate_proj)
    inner_act, unit_three, std_three = layer_norm(activated * up_proj, ffn_vec[2], ffn_vec[3])
    inner_low = inner_act.astype(jnp.bfloat16)
    result = middle + (project(inner_low, w_down) + vectors[7])
    saved = (
        normed_low,
        unit_one,
        std_one,
        head_queries,
        head_keys,
        head_values,
        log_sums,
        attended,
        unit_two,
        std_two,
        normed_two_low,
        gate_proj,
        up_proj,
        activated,
        unit_three,
        std_three,
        inner_low,
    )
    return (result, saved)


def backward_pass(grad_rows, weights, ffn_vec, cosines, sines, saved, row_mask):
    w_query, w_key, w_value, w_gate, w_up, w_out, w_down, vectors_low = weights
    vectors = vectors_low.astype(jnp.float32)
    (
        normed_low,
        unit_one,
        std_one,
        head_queries,
        head_keys,
        head_values,
        log_sums,
        attended,
        unit_two,
        std_two,
        normed_two_low,
        gate_proj,
        up_proj,
        activated,
        unit_three,
        std_three,
        inner_low,
    ) = saved
    batch, row_count, model_width = grad_rows.shape
    heads = model_width // HD
    reduced_mask = row_mask.astype(jnp.bfloat16)
    branch_low = grad_rows.astype(jnp.bfloat16)
    grad_down = weight_grad(inner_low, branch_low * reduced_mask)
    grad_inner = project_back(branch_low, w_down)
    grad_mix, gain_three, shift_three = norm_back(
        grad_inner, ffn_vec[2], unit_three, std_three, row_mask
    )
    sigmoid_gate = jax.nn.sigmoid(gate_proj)
    gate_low = (
        grad_mix * up_proj * sigmoid_gate * (1.0 + gate_proj * (1.0 - sigmoid_gate))
    ).astype(jnp.bfloat16)
    up_low = (grad_mix * activated).astype(jnp.bfloat16)
    grad_gate_w = weight_grad(normed_two_low * reduced_mask, gate_low)
    grad_up_w = weight_grad(normed_two_low * reduced_mask, up_low)
    grad_normed_two = project_back(gate_low, w_gate) + project_back(up_low, w_up)
    grad_mid_norm, gain_two, shift_two = norm_back(
        grad_normed_two, vectors[5], unit_two, std_two, row_mask
    )
    grad_middle = grad_rows + grad_mid_norm
    out_low = grad_middle.astype(jnp.bfloat16)
    grad_out_w = weight_grad(attended * reduced_mask, out_low)
    attended_grad = project_back(out_low, w_out).astype(jnp.bfloat16)
    head_grads = attended_grad.reshape(batch, row_count, heads, HD).transpose(2, 0, 1, 3)

    def head_backward(item):
        block_of_queries, block_of_keys, block_of_values, block_gradient, log_block = item
        logit_scores = jnp.einsum(
            "wey,wmy->wem", block_of_queries, block_of_keys, preferred_element_type=jnp.float32
        )
        attn_probs = jnp.exp(logit_scores - log_block[..., None])
        grad_probs = jnp.einsum(
            "wey,wmy->wem", block_gradient, block_of_values, preferred_element_type=jnp.float32
        )
        inner_sum = jnp.sum(attn_probs * grad_probs, axis=-1, keepdims=True)
        score_gradients = (attn_probs * (grad_probs - inner_sum)).astype(jnp.bfloat16)
        grad_query = jnp.einsum(
            "sce,sem->scm", score_gradients, block_of_keys, preferred_element_type=jnp.float32
        )
        grad_key = jnp.einsum(
            "ipz,iph->izh",
            score_gradients * reduced_mask,
            block_of_queries,
            preferred_element_type=jnp.float32,
        )
        grad_value = jnp.einsum(
            "ipz,iph->izh",
            attn_probs.astype(jnp.bfloat16) * reduced_mask,
            block_gradient,
            preferred_element_type=jnp.float32,
        )
        return (grad_query, grad_key, grad_value)

    grad_q_heads, grad_k_heads, grad_v_heads = lax.map(
        head_backward, (head_queries, head_keys, head_values, head_grads, log_sums)
    )
    length = head_keys.shape[2]
    grad_keys = grad_k_heads.transpose(1, 2, 0, 3).reshape(batch, length, model_width)
    grad_values = grad_v_heads.transpose(1, 2, 0, 3).reshape(batch, length, model_width)
    own_keys, own_values = (
        lax.psum_scatter(
            grad_keys[:, 1:].astype(jnp.bfloat16), "ctx", scatter_dimension=1, tiled=True
        ).astype(jnp.float32),
        lax.psum_scatter(
            grad_values[:, 1:].astype(jnp.bfloat16), "ctx", scatter_dimension=1, tiled=True
        ).astype(jnp.float32),
    )
    class_keys, class_values = lax.psum((grad_keys[:, :1], grad_values[:, :1]), "ctx")
    key_rows = jnp.concatenate([class_keys, own_keys], axis=1).reshape(batch, row_count, heads, HD)
    value_rows = jnp.concatenate([class_values, own_values], axis=1)
    key_low = (
        unrotate(key_rows, cosines, sines)
        .reshape(batch, row_count, model_width)
        .astype(jnp.bfloat16)
    )
    value_low = value_rows.astype(jnp.bfloat16)
    query_rows = grad_q_heads.transpose(1, 2, 0, 3)
    query_low = (
        (unrotate(query_rows, cosines, sines) * HD ** (-0.5))
        .reshape(batch, row_count, model_width)
        .astype(jnp.bfloat16)
    )
    grad_query_w = weight_grad(normed_low * reduced_mask, query_low)
    grad_key_w = weight_grad(normed_low * reduced_mask, key_low)
    grad_value_w = weight_grad(normed_low * reduced_mask, value_low)
    grad_normed = (
        project_back(query_low, w_query)
        + project_back(key_low, w_key)
        + project_back(value_low, w_value)
    )
    grad_in_norm, gain_one, shift_one = norm_back(
        grad_normed, vectors[0], unit_one, std_one, row_mask
    )
    grad_tokens = grad_middle + grad_in_norm

    def column_sum(rounded):
        return jnp.sum(rounded.astype(jnp.float32) * row_mask, axis=(0, 1))

    vector_grads = jnp.stack(
        [
            gain_one,
            shift_one,
            column_sum(query_low),
            column_sum(value_low),
            column_sum(out_low),
            gain_two,
            shift_two,
            column_sum(branch_low),
        ]
    )
    ffn_grads = jnp.stack([column_sum(gate_low), column_sum(up_low), gain_three, shift_three])
    return (
        grad_tokens,
        (
            (grad_query_w, grad_key_w, grad_value_w, grad_gate_w, grad_up_w),
            (grad_out_w, grad_down, vector_grads),
            ffn_grads,
        ),
    )


def on_device(
    patch_in,
    cls_in,
    d_patch,
    d_cls,
    image_valid,
    patch_coords,
    w_query,
    w_key,
    w_value,
    w_gate,
    w_up,
    w_out,
    w_down,
    layer_vectors,
    ffn_vectors,
):
    images, patch_rows, model_width = patch_in.shape
    group_size = images // MICRO
    cosines, sines = rotary_tables(patch_coords)
    first_flag = (lax.axis_index("ctx") == 0).astype(jnp.float32)
    row_weight = jnp.concatenate([first_flag[None], jnp.ones((patch_rows,), jnp.float32)])
    row_mask = row_weight[None, :, None]
    ffn_vec = ffn_vectors.astype(jnp.float32)
    keep_mask = image_valid.astype(jnp.float32)
    results = []
    totals = None
    for micro_step in range(MICRO):
        first_image = micro_step * group_size
        last_image = first_image + group_size
        tokens = jnp.concatenate(
            [cls_in[first_image:last_image, None, :], patch_in[first_image:last_image]], axis=1
        ).astype(jnp.float32)
        weights = fetch_forward(w_query, w_key, w_value, w_gate, w_up, w_out, w_down, layer_vectors)
        result, saved = forward_pass(tokens, weights, ffn_vec, cosines, sines)
        keep_rows = keep_mask[first_image:last_image][:, None, None]
        grad_rows = (
            jnp.concatenate(
                [d_cls[first_image:last_image, None, :], d_patch[first_image:last_image]], axis=1
            ).astype(jnp.float32)
            * keep_rows
        )
        back_weights = fetch_backward(
            w_query, w_key, w_value, w_gate, w_up, w_out, w_down, layer_vectors
        )
        grad_tokens, weight_grads = backward_pass(
            grad_rows, back_weights, ffn_vec, cosines, sines, saved, row_mask
        )
        if totals is None:
            totals = weight_grads
        else:
            totals = jax.tree.map(lambda first, second: first + second, totals, weight_grads)
        results.append(
            ((result * keep_rows).astype(jnp.bfloat16), grad_tokens.astype(jnp.bfloat16))
        )
    out_rows = jnp.concatenate([entry[0] for entry in results], axis=0)
    grad_out_rows = jnp.concatenate([entry[1] for entry in results], axis=0)
    in_grads, out_grads, ffn_total = totals
    owned_in = (
        lax.psum_scatter(in_grads[0], ("dp", "ctx"), scatter_dimension=0, tiled=True),
        lax.psum_scatter(in_grads[1], ("dp", "ctx"), scatter_dimension=0, tiled=True),
        lax.psum_scatter(in_grads[2], ("dp", "ctx"), scatter_dimension=0, tiled=True),
        lax.psum_scatter(in_grads[3], ("dp", "ctx"), scatter_dimension=0, tiled=True),
        lax.psum_scatter(in_grads[4], ("dp", "ctx"), scatter_dimension=0, tiled=True),
    )
    owned_out = (
        lax.psum_scatter(out_grads[0], ("dp", "ctx"), scatter_dimension=1, tiled=True),
        lax.psum_scatter(out_grads[1], ("dp", "ctx"), scatter_dimension=1, tiled=True),
        lax.psum_scatter(out_grads[2], ("dp", "ctx"), scatter_dimension=1, tiled=True),
    )
    ffn_summed = lax.psum(ffn_total, ("dp", "ctx"))
    return (
        out_rows[:, 1:],
        out_rows[:, 0],
        grad_out_rows[:, 1:],
        grad_out_rows[:, 0],
        owned_in[0],
        owned_in[1],
        owned_in[2],
        owned_in[3],
        owned_in[4],
        owned_out[0],
        owned_out[1],
        owned_out[2],
        ffn_summed,
    )


BOTH = ("dp", "ctx")
BIT_X, BIT_CORE, BIT_Y, BIT_Z0, BIT_Z1 = 1, 2, 4, 16, 8
ROWS = 1040
KEYS = 1024
WIDTH = 1024
HALF = 512
HEAD_COLS = 256
STEP = 208
LOG2E = math.log2(math.e)
COST = 4
F32 = jnp.float32
BF16 = jnp.bfloat16


SENT = []


def swap_over(value, bit):
    value = lax.optimization_barrier(value)
    SENT.append(value)
    count = lax.axis_size(BOTH)
    return lax.ppermute(value, BOTH, [(i, i ^ bit) for i in range(count)])


def joined(*parts, axis=0):
    return jnp.concatenate(parts, axis=axis)


def after(value, *deps):
    return lax.optimization_barrier((value,) + deps)[0]


def ready(value, *deps):
    corners = [sum(v[0:1, 0:1].astype(F32) for v in SENT)] if SENT else []
    SENT.clear()
    return after(value, *deps, *corners)


def dot_nn(a, b):
    return lax.dot_general(a, b, (((1,), (0,)), ((), ())), preferred_element_type=F32)


def dot_nt(a, b):
    return lax.dot_general(a, b, (((1,), (1,)), ((), ())), preferred_element_type=F32)


def dot_tn(a, b):
    return lax.dot_general(a, b, (((0,), (0,)), ((), ())), preferred_element_type=F32)


def cost_of(flops, bytes_accessed, transcendentals):
    return pl.CostEstimate(
        flops=int(COST * flops), bytes_accessed=int(COST * bytes_accessed), transcendentals=int(COST * transcendentals)
    )


def pack_rows(*parts):
    total, columns = sum(p.shape[0] for p in parts), parts[0].shape[1]
    blocks = columns // 128
    steps = next(n for n in (4, 5, 3, 2, 1) if blocks % n == 0)
    tile = columns // steps

    def kernel(*refs):
        out, start = refs[len(parts)], 0
        for ref in refs[: len(parts)]:
            out[start : start + ref.shape[0], :] = ref[...]
            start += ref.shape[0]

    return pl.pallas_call(
        kernel,
        grid=(steps,),
        in_specs=[pl.BlockSpec((p.shape[0], tile), lambda j: (0, j)) for p in parts],
        out_specs=pl.BlockSpec((total, tile), lambda j: (0, j)),
        out_shape=jax.ShapeDtypeStruct((total, columns), parts[0].dtype),
        compiler_params=pltpu.CompilerParams(vmem_limit_bytes=32 << 20),
        cost_estimate=cost_of(flops=0, bytes_accessed=4 * total * columns, transcendentals=0),
        name="pack_rows",
    )(*parts)


class Gather:
    def __init__(self, local):
        self.part = local

    def along_z0(self, *deps):
        part = after(self.part, *deps)
        far = swap_over(part, BIT_Z0)
        self.part = joined(part, far)
        return far

    def along_z1(self, *deps):
        part = after(self.part, *deps)
        far = swap_over(part, BIT_Z1)
        self.part = joined(part, far)
        return far

    def along_xy(self, *deps):
        part = after(self.part, *deps)
        self.over = swap_over(part, BIT_X), swap_over(part, BIT_Y)
        return self.over

    def corners(self, *deps):
        over_x, over_y = after(self.over, *deps)
        self.corner = swap_over(over_y[:64], BIT_X), swap_over(over_x[64:], BIT_Y)
        return self.corner

    def whole(self, *deps):
        parts = after((self.part, self.over, self.corner), *deps)
        self.near = pack_rows(parts[0], parts[1][1], parts[1][0], *parts[2])
        self.far = swap_over(self.near, BIT_CORE)
        return self.near


def rounded_sum(*terms):
    total = terms[0].astype(F32)
    for term in terms[1:]:
        total = total + term.astype(F32)
    return total.astype(BF16)


class Scatter:
    def over_core(self, far, *deps):
        return swap_over(after(far, *deps), BIT_CORE)

    def corner(self, total, *deps):
        self.total = after(total, *deps)
        self.to_x = rounded_sum(self.total[256:384], swap_over(self.total[384:], BIT_Y))
        self.to_y = self.total[128:256]
        return self.to_x

    def corners(self, total, *deps):
        self.total = total = after(total, *deps)
        from_x, from_y = swap_over(total[384:448], BIT_X), swap_over(total[448:512], BIT_Y)
        self.to_y = joined(rounded_sum(total[128:192], from_x), total[192:256])
        self.to_x = joined(total[256:320], rounded_sum(total[320:384], from_y))
        return self.to_x, self.to_y

    def sides(self, *deps):
        to_x, to_y = after((self.to_x, self.to_y), *deps)
        self.total = rounded_sum(self.total[:128], swap_over(to_y, BIT_Y), swap_over(to_x, BIT_X))
        return self.total

    def over_y(self, *deps):
        total = after(self.total, *deps)
        kept, sent = joined(total[:128], total[256:384]), joined(total[128:256], total[384:])
        self.total = rounded_sum(kept, swap_over(sent, BIT_Y))
        return self.total

    def over_x(self, *deps):
        total = after(self.total, *deps)
        self.total = rounded_sum(total[:128], swap_over(total[128:], BIT_X))
        return self.total

    def along_z1(self, *deps):
        total = after(self.total, *deps)
        self.total = rounded_sum(total[:64], swap_over(total[64:], BIT_Z1))
        return self.total

    def along_z0(self, *deps):
        total = after(self.total, *deps)
        return total[:32].astype(F32) + swap_over(total[32:], BIT_Z0).astype(F32)


def scatter_small(value):
    for rows, bit in ((512, BIT_CORE), (256, BIT_X), (128, BIT_Y), (64, BIT_Z1), (32, BIT_Z0)):
        value = value[:rows] + swap_over(value[rows:], bit)
    return value


def rotate_lanes(x, cosines, sines_up, sines_down):
    width = x.shape[1]
    return x * cosines + pltpu.roll(x, width - 16, 1) * sines_up + pltpu.roll(x, 16, 1) * sines_down


def twice(table):
    return jnp.concatenate([table, table], axis=1)


def attention_kernel(
    x_ref, qn_ref, qf_ref, kn_ref, kf_ref, vn_ref, vf_ref, b_ref, c_ref, s1_ref, s2_ref,
    q_ref, k_ref, v_ref, o_ref, l_ref
):
    def project(near_ref, far_ref):
        return dot_nn(x_ref[:, :HALF], near_ref[...]) + dot_nn(x_ref[:, HALF:], far_ref[...])

    c, s1, s2 = twice(c_ref[...]), twice(s1_ref[...]), twice(s2_ref[...])
    q = project(qn_ref, qf_ref) + b_ref[2:3, :]
    q_ref[...] = (rotate_lanes(q, c, s1, s2) * (LOG2E / 8)).astype(BF16)
    k_ref[...] = rotate_lanes(project(kn_ref, kf_ref), c, s1, s2).astype(BF16)
    v_ref[...] = (project(vn_ref, vf_ref) + b_ref[3:4, :]).astype(BF16)
    lane = lax.broadcasted_iota(jnp.int32, (1, 128), 1)
    low_half = lane < 64

    stats = jnp.zeros((ROWS, 128), F32)
    for pair in range(2):
        cols = slice(pair * 128, pair * 128 + 128)
        q_pair = q_ref[:, cols]
        k_pair, v_pair = k_ref[0:KEYS, cols], v_ref[0:KEYS, cols]
        k_class = k_ref[KEYS : KEYS + 16, cols].astype(F32)[0:1]
        v_class = v_ref[KEYS : KEYS + 16, cols].astype(F32)[0:1]
        product = q_pair.astype(F32) * k_class
        outs = []
        for h in range(2):
            own = low_half if h == 0 else ~low_half
            scores = dot_nt(jnp.where(own, q_pair, jnp.zeros_like(q_pair)), k_pair)
            class_score = jnp.sum(jnp.where(own, product, 0.0), axis=1, keepdims=True)
            peak = jnp.maximum(jnp.max(scores, axis=1, keepdims=True), class_score)
            p = jnp.exp2(scores - peak)
            class_p = jnp.exp2(class_score - peak)
            total = jnp.sum(p, axis=1, keepdims=True) + class_p
            out = dot_nn(p.astype(BF16), v_pair) + class_p * v_class
            outs.append(out * (1.0 / total))
            stats = jnp.where(lane == pair * 2 + h, peak + jnp.log2(total), stats)
        o_ref[:, cols] = jnp.where(low_half, outs[0], outs[1]).astype(BF16)
    l_ref[...] = stats.T[0:8, :]


def attention_forward(x, near, far, biases, head_block, at, tables):
    def block(index):
        return pl.BlockSpec((HALF, HEAD_COLS), lambda j: (0, index))

    def whole(a):
        return pl.BlockSpec(a.shape, lambda j: (0, 0))

    out = pl.BlockSpec((ROWS, HEAD_COLS), lambda j: (0, 0))
    return pl.pallas_call(
        attention_kernel,
        grid=(1,),
        in_specs=[whole(x)]
        + [block(at + first) for first in (0, 0, 2, 2, 4, 4)]
        + [pl.BlockSpec((8, HEAD_COLS), lambda j: (0, head_block))]
        + [whole(t) for t in tables],
        out_specs=[out] * 4 + [pl.BlockSpec((8, ROWS), lambda j: (0, 0))],
        out_shape=[jax.ShapeDtypeStruct((ROWS, HEAD_COLS), BF16)] * 4 + [jax.ShapeDtypeStruct((8, ROWS), F32)],
        compiler_params=pltpu.CompilerParams(vmem_limit_bytes=56 << 20),
        cost_estimate=cost_of(flops=7_500_000_000, bytes_accessed=7_000_000, transcendentals=4_300_000),
        name="attention_forward",
    )(x, near, far, near, far, near, far, biases, *tables)


def attention_back_kernel(
    q_ref, k_ref, v_ref, g_ref, o_ref, l_ref, c_ref, s1_ref, s2_ref,
    dq_ref, dk_ref, dv_ref, sum_ref, dq_turned, dk_sum, dv_sum, delta_ref, k_turned, *, step
):
    lane = lax.broadcasted_iota(jnp.int32, (1, 128), 1)
    low_half = lane < 64
    deltas = jnp.zeros((ROWS, 128), F32)
    for pair in range(2):
        cols = slice(pair * 128, pair * 128 + 128)
        product = g_ref[:, cols].astype(F32) * o_ref[:, cols].astype(F32)
        for h in range(2):
            own = low_half if h == 0 else ~low_half
            delta = jnp.sum(jnp.where(own, product, 0.0), axis=1, keepdims=True)
            deltas = jnp.where(lane == pair * 2 + h, delta, deltas)
    delta_ref[...] = deltas.T[0:8, :]
    real_key = lax.broadcasted_iota(jnp.int32, (ROWS, 1), 0) <= KEYS
    class_key = lax.broadcasted_iota(jnp.int32, (ROWS - KEYS, 1), 0) == 0
    k_turned[...] = k_ref[...].T
    for t in range(KEYS // step):
        rows = pl.ds(t * step, step)
        for pair in range(2):
            cols = slice(pair * 128, pair * 128 + 128)
            q_pair, g_pair = q_ref[rows, cols], g_ref[rows, cols]
            k_pair, v_pair = k_ref[:, cols], v_ref[:, cols]
            dk, dv = None, None
            for h in range(2):
                own = low_half if h == 0 else ~low_half
                head = pair * 2 + h
                q_head = jnp.where(own, q_pair, jnp.zeros_like(q_pair))
                g_head = jnp.where(own, g_pair, jnp.zeros_like(g_pair))
                scores = dot_nt(k_pair, q_head)
                log_sums = l_ref[head : head + 1, rows]
                p = jnp.concatenate(
                    [
                        jnp.exp2(scores[:KEYS] - log_sums),
                        jnp.where(class_key, jnp.exp2(scores[KEYS:] - log_sums), 0.0),
                    ],
                    axis=0,
                )
                gp = dot_nt(v_pair, g_head)
                ds = (p * (gp - delta_ref[head : head + 1, rows])).astype(BF16)
                dv_part, dk_part = dot_nn(p.astype(BF16), g_head), dot_nn(ds, q_head)
                dv = dv_part if dv is None else dv + dv_part
                dk = dk_part if dk is None else dk + dk_part
                own_rows = slice(head * 64, head * 64 + 64)
                dq_turned[own_rows, rows] = dot_nn(k_turned[own_rows, :], ds)
            if t == 0:
                dk_sum[:, cols], dv_sum[:, cols] = dk, dv
            else:
                dk_sum[:, cols] += dk
                dv_sum[:, cols] += dv
    q_class = q_ref[KEYS : KEYS + 16, :][0:1].astype(F32)
    g_class = g_ref[KEYS : KEYS + 16, :][0:1].astype(F32)
    shape = (128, HEAD_COLS)
    own = lax.broadcasted_iota(jnp.int32, shape, 0) == lax.broadcasted_iota(jnp.int32, shape, 1) // 64
    q_diag = jnp.where(own, q_class, 0.0).astype(BF16)
    g_diag = jnp.where(own, g_class, 0.0).astype(BF16)
    scores, gp = dot_nt(k_ref[...], q_diag), dot_nt(v_ref[...], g_diag)
    log_class, delta_class = jnp.zeros((1, 128), F32), jnp.zeros((1, 128), F32)
    for head in range(4):
        log_class = jnp.where(lane == head, l_ref[head : head + 1, KEYS : KEYS + 1], log_class)
        delta_class = jnp.where(lane == head, delta_ref[head : head + 1, KEYS : KEYS + 1], delta_class)
    p = jnp.where(real_key & (lane < 4), jnp.exp2(scores - log_class), 0.0)
    ds = (p * (gp - delta_class)).astype(BF16)
    dv = dv_sum[...] + dot_nn(p.astype(BF16), g_diag)
    dk = dk_sum[...] + dot_nn(ds, q_diag)
    dq_class = jnp.sum(jnp.where(own, dot_tn(ds, k_ref[...]), 0.0), axis=0, keepdims=True)
    first = lax.broadcasted_iota(jnp.int32, (16, 1), 0) == 0
    dq = jnp.concatenate([dq_turned[...].T, jnp.where(first, dq_class, 0.0)], axis=0)
    c, s1, s2 = twice(c_ref[...]), twice(s1_ref[...]), twice(s2_ref[...])
    dq = (rotate_lanes(dq, c, -s1, -s2) * 0.125).astype(BF16)
    dv = dv.astype(BF16)
    dq_ref[...] = dq
    dk_ref[...] = (rotate_lanes(dk, c, -s1, -s2) * (1.0 / LOG2E)).astype(BF16)
    dv_ref[...] = dv
    sum_ref[0:1, :] = jnp.sum(dq.astype(F32), axis=0, keepdims=True)
    sum_ref[1:2, :] = jnp.sum(dv.astype(F32), axis=0, keepdims=True)
    sum_ref[2:8, :] = jnp.zeros((6, HEAD_COLS), F32)


def attention_backward(q, k, v, o, log_sums, g, tables, step=256):
    def whole(a):
        return pl.BlockSpec(a.shape, lambda j: (0, 0))

    block = pl.BlockSpec((ROWS, HEAD_COLS), lambda j: (0, 0))
    return pl.pallas_call(
        functools.partial(attention_back_kernel, step=step),
        grid=(1,),
        in_specs=[block] * 5 + [pl.BlockSpec((8, ROWS), lambda j: (0, 0))] + [whole(t) for t in tables],
        out_specs=[block] * 3 + [pl.BlockSpec((8, HEAD_COLS), lambda j: (0, 0))],
        out_shape=[jax.ShapeDtypeStruct((ROWS, HEAD_COLS), BF16)] * 3
        + [jax.ShapeDtypeStruct((8, HEAD_COLS), F32)],
        scratch_shapes=[pltpu.VMEM((HEAD_COLS, KEYS), F32)]
        + [pltpu.VMEM((ROWS, HEAD_COLS), F32)] * 2
        + [pltpu.VMEM((8, ROWS), F32), pltpu.VMEM((HEAD_COLS, ROWS), BF16)],
        compiler_params=pltpu.CompilerParams(vmem_limit_bytes=48 << 20),
        cost_estimate=cost_of(
            flops=13_000_000_000, bytes_accessed=5_000_000, transcendentals=4_300_000
        ),
        name="attention_backward",
    )(q, k, v, g, o, log_sums, *tables)


def over_rows(kernel, name, tiled, held, outs, sums=(), flops=0, step=STEP, only=None):
    rows = ROWS if only is None else step
    if only is None:
        in_specs = [pl.BlockSpec((step, a.shape[1]), lambda i: (i, 0)) for a in tiled]
    else:
        in_specs = [
            pl.BlockSpec((pl.Element(step), pl.Element(a.shape[1])), lambda i: (only, 0)) for a in tiled
        ]
    held = [h if isinstance(h, tuple) else (h, h.shape, 0) for h in held]
    in_specs += [
        pl.BlockSpec(shape, lambda i, column=column: (0, column), pipeline_mode=pl.Buffered(1))
        for _, shape, column in held
    ]
    held = [h[0] for h in held]
    out_specs = [pl.BlockSpec((step, n), lambda i: (i, 0)) for n, _ in outs]
    out_specs += [pl.BlockSpec((8, n), lambda i: (0, 0)) for n in sums]
    out_shape = [jax.ShapeDtypeStruct((rows, n), t) for n, t in outs]
    out_shape += [jax.ShapeDtypeStruct((8, n), F32) for n in sums]
    moved = sum(a.size * a.dtype.itemsize for a in list(tiled) + list(held))
    moved += sum(s.size * s.dtype.itemsize for s in out_shape)
    return pl.pallas_call(
        kernel,
        grid=(rows // step,),
        in_specs=in_specs,
        out_specs=out_specs,
        out_shape=out_shape,
        compiler_params=pltpu.CompilerParams(vmem_limit_bytes=56 << 20),
        cost_estimate=cost_of(flops=flops, bytes_accessed=moved, transcendentals=0),
        name=name,
    )(*tiled, *held)


def add_sums(ref, *rows):
    @pl.when(pl.program_id(0) == 0)
    def _():
        ref[...] = jnp.zeros_like(ref)

    for i, value in enumerate(rows):
        ref[i : i + 1, :] += jnp.sum(value, axis=0, keepdims=True)


def unit_norm(values):
    centred = values - jnp.mean(values, axis=-1, keepdims=True)
    inv_std = lax.rsqrt(jnp.mean(centred * centred, axis=-1, keepdims=True) + epsilon)
    return centred * inv_std, inv_std


def unit_norm_back(scaled, unit, inv_std):
    return inv_std * (
        scaled
        - jnp.mean(scaled, axis=-1, keepdims=True)
        - unit * jnp.mean(scaled * unit, axis=-1, keepdims=True)
    )


def vectors_kernel(near_ref, far_ref, order_ref, vec_ref, head_ref):
    rows = jnp.concatenate([near_ref[...].astype(F32).T, far_ref[...].astype(F32).T], axis=1)[0:8]
    vec_ref[...] = rows
    head_ref[...] = dot_nt(rows.astype(BF16), order_ref[...])


def gathered_vectors(near, far, order):
    block = pl.BlockSpec((HALF, 128), lambda j: (0, 3 * HALF // 128))
    out = pl.BlockSpec((8, WIDTH), lambda j: (0, 0))
    return pl.pallas_call(
        vectors_kernel,
        grid=(1,),
        in_specs=[block, block, pl.BlockSpec(order.shape, lambda j: (0, 0))],
        out_specs=[out, out],
        out_shape=[jax.ShapeDtypeStruct((8, WIDTH), F32)] * 2,
        cost_estimate=cost_of(flops=40_000_000, bytes_accessed=2_400_000, transcendentals=0),
        name="vectors",
    )(near, far, order)


def sigmoid_of(x):
    return 0.5 * jnp.tanh(0.5 * x) + 0.5


def start_kernel(rows_ref, order_ref, vec_ref, tokens_ref, normed_ref):
    tokens = dot_nn(rows_ref[...], order_ref[...])
    tokens_ref[...] = tokens.astype(BF16)
    unit, _ = unit_norm(tokens)
    normed_ref[...] = (unit * vec_ref[0:1, :] + vec_ref[1:2, :]).astype(BF16)


def middle_kernel(a0_ref, a1_ref, a2_ref, a3_ref, tokens_ref, na_ref, nb_ref, fa_ref, fb_ref, vec_ref, middle_ref, normed_ref):
    low = jnp.concatenate([a0_ref[...], a1_ref[...]], axis=1)
    high = jnp.concatenate([a2_ref[...], a3_ref[...]], axis=1)
    branch = jnp.concatenate(
        [
            dot_nt(low, na_ref[...]) + dot_nt(high, nb_ref[...]),
            dot_nt(low, fa_ref[...]) + dot_nt(high, fb_ref[...]),
        ],
        axis=1,
    )
    middle = tokens_ref[...].astype(F32) + (branch + vec_ref[4:5, :])
    middle_ref[...] = middle.astype(BF16)
    unit, _ = unit_norm(middle)
    normed_ref[...] = (unit * vec_ref[5:6, :] + vec_ref[6:7, :]).astype(BF16)


def hidden_kernel(x_ref, gn_ref, gf_ref, un_ref, uf_ref, ffn_ref, gate_ref, up_ref, inner_ref, stat_ref, *, hidden):
    near, far = x_ref[:, :HALF], x_ref[:, HALF:]
    gate = dot_nn(near, gn_ref[...]) + dot_nn(far, gf_ref[...]) + ffn_ref[0:1, :]
    up = dot_nn(near, un_ref[...]) + dot_nn(far, uf_ref[...]) + ffn_ref[1:2, :]
    gate_ref[...] = gate.astype(gate_ref.dtype)
    up_ref[...] = up.astype(up_ref.dtype)
    mix = gate * sigmoid_of(gate) * up
    mean = jnp.sum(mix, axis=1, keepdims=True) * (1.0 / hidden)
    real = lax.broadcasted_iota(jnp.int32, (1, mix.shape[1]), 1) < hidden
    centred = jnp.where(real, mix - mean, 0.0)
    inv_std = lax.rsqrt(jnp.sum(centred * centred, axis=1, keepdims=True) * (1.0 / hidden) + epsilon)
    inner_ref[...] = (centred * inv_std * ffn_ref[2:3, :] + ffn_ref[3:4, :]).astype(BF16)
    lane = lax.broadcasted_iota(jnp.int32, (1, 128), 1)
    stat_ref[...] = jnp.where(lane == 0, mean, inv_std)


def result_kernel(inner_ref, middle_ref, near_ref, far_ref, vec_ref, order_ref, keep_ref, out_ref):
    inner = inner_ref[...]
    branch = jnp.concatenate([dot_nt(inner, near_ref[...]), dot_nt(inner, far_ref[...])], axis=1)
    result = middle_ref[...].astype(F32) + (branch + vec_ref[7:8, :])
    rounded = (result * keep_ref[0:1, 0:1]).astype(BF16)
    out_ref[...] = dot_nt(rounded, order_ref[...]).astype(BF16)


def hidden_back_kernel(
    d_ref, gate_ref, up_ref, stat_ref, order_ref, keep_ref, near_ref, far_ref, ffn_ref,
    branch_ref, dgate_ref, dup_ref, wide_ref, sum_ref, *, hidden
):
    branch = (dot_nn(d_ref[...], order_ref[...]) * keep_ref[0:1, 0:1]).astype(BF16)
    branch_ref[...] = branch
    g_inner = dot_nn(branch[:, :HALF], near_ref[...]) + dot_nn(branch[:, HALF:], far_ref[...])
    gate, up = gate_ref[...].astype(F32), up_ref[...].astype(F32)
    sigmoid = sigmoid_of(gate)
    silu = gate * sigmoid
    mean, inv_std = stat_ref[:, 0:1], stat_ref[:, 1:2]
    unit = (silu * up - mean) * inv_std
    g_unit = g_inner * ffn_ref[2:3, :]
    share = 1.0 / hidden
    g_mix = inv_std * (
        g_unit
        - jnp.sum(g_unit, axis=1, keepdims=True) * share
        - unit * (jnp.sum(g_unit * unit, axis=1, keepdims=True) * share)
    )
    d_gate = (g_mix * up * (sigmoid * (1.0 + gate * (1.0 - sigmoid)))).astype(BF16)
    d_up = (g_mix * silu).astype(BF16)
    dgate_ref[...] = d_gate
    dup_ref[...] = d_up
    add_sums(wide_ref, d_gate.astype(F32), d_up.astype(F32), g_inner * unit, g_inner)
    add_sums(sum_ref, branch.astype(F32))


def middle_back_kernel(
    dgate_ref, dup_ref, branch_ref, middle_ref, gn_ref, gf_ref, un_ref, uf_ref, na_ref, nb_ref, fa_ref, fb_ref, vec_ref,
    low_ref, d0_ref, d1_ref, d2_ref, d3_ref, sum_ref
):
    d_gate, d_up = dgate_ref[...], dup_ref[...]
    g_two = jnp.concatenate(
        [
            dot_nt(d_gate, gn_ref[...]) + dot_nt(d_up, un_ref[...]),
            dot_nt(d_gate, gf_ref[...]) + dot_nt(d_up, uf_ref[...]),
        ],
        axis=1,
    )
    unit, inv_std = unit_norm(middle_ref[...].astype(F32))
    g_middle = branch_ref[...].astype(F32) + unit_norm_back(g_two * vec_ref[5:6, :], unit, inv_std)
    low = g_middle.astype(BF16)
    low_ref[...] = low
    near, far = low[:, :HALF], low[:, HALF:]
    d_low = (dot_nn(near, na_ref[...]) + dot_nn(far, fa_ref[...])).astype(BF16)
    d_high = (dot_nn(near, nb_ref[...]) + dot_nn(far, fb_ref[...])).astype(BF16)
    d0_ref[...], d1_ref[...] = d_low[:, :HEAD_COLS], d_low[:, HEAD_COLS:]
    d2_ref[...], d3_ref[...] = d_high[:, :HEAD_COLS], d_high[:, HEAD_COLS:]
    add_sums(sum_ref, low.astype(F32), g_two * unit, g_two)


def last_kernel(*refs):
    grads = refs[:12]
    gmid_ref, tokens_ref, an_ref, af_ref, bn_ref, bf_ref, vec_ref, order_ref, grad_ref, sum_ref = refs[12:]

    def back(low_w, high_w):
        total = 0.0
        for first, w_ref in ((0, low_w), (6, high_w)):
            for i in range(3):
                g = jnp.concatenate([grads[first + i][...], grads[first + 3 + i][...]], axis=1)
                total = total + dot_nt(g, w_ref[:, i * HALF : i * HALF + HALF])
        return total

    g_one = jnp.concatenate([back(an_ref, bn_ref), back(af_ref, bf_ref)], axis=1)
    unit, inv_std = unit_norm(tokens_ref[...].astype(F32))
    grad = gmid_ref[...].astype(F32) + unit_norm_back(g_one * vec_ref[0:1, :], unit, inv_std)
    grad_ref[...] = dot_nt(grad.astype(BF16), order_ref[...]).astype(BF16)
    add_sums(sum_ref, g_one * unit, g_one)


def weight_grads(half, steps, received=None):
    sources, arrays = [], []
    for x, gs in steps:
        if not any(x is s for s in sources):
            sources.append(x)
        for g, _, _ in gs:
            if not any(g is a for a in arrays):
                arrays.append(g)
    tile = sum(width for _, width, _ in steps[0][1])
    refs_of, specs, operands = [], [], []
    for j, (x, gs) in enumerate(steps):
        mine = []
        for g, width, at in gs:
            found = next((i for i, o in enumerate(operands) if o[0] is g and o[1] == width), None)
            if found is None:
                operands.append((g, width, {}))
                found = len(operands) - 1
            operands[found][2][j] = at
            mine.append(found)
        refs_of.append(mine)
    for g, width, places in operands:
        known = sorted(places.items())

        def index(j, known=known):
            at = known[0][1]
            for step, place in known[1:]:
                at = jnp.where(j >= step, place, at)
            return 0, at

        specs.append(pl.BlockSpec((ROWS, width), index))
    plus = [] if received is None else [received]

    def kernel(*refs):
        xs, gs = refs[: len(sources)], refs[len(sources) : len(sources) + len(operands)]
        out_ref, turned, last = refs[-3:]
        step = pl.program_id(0)
        for j, (x, _) in enumerate(steps):
            source = next(i for i, s in enumerate(sources) if s is x)
            fresh = j == 0 or steps[j - 1][0] is not x

            @pl.when(step == j)
            def _(j=j, source=source, fresh=fresh):
                if fresh:
                    turned[...] = xs[source][0:KEYS, :].T
                    last[...] = xs[source][KEYS:ROWS, :].astype(F32).T
                parts = [gs[r] for r in refs_of[j]]
                main = jnp.concatenate([p[0:KEYS, :] for p in parts], axis=1)
                row = jnp.concatenate([p[KEYS:ROWS, :].astype(F32)[0:1] for p in parts], axis=1)
                out = dot_nn(turned[...], main) + last[:, 0:1] * row
                if plus:
                    out = out + refs[len(sources) + len(operands)][...].astype(F32)
                out_ref[...] = out.astype(BF16)

    block = pl.BlockSpec((HALF, tile), lambda j: (0, j))
    columns = len(steps) * tile
    return pl.pallas_call(
        kernel,
        grid=(len(steps),),
        in_specs=[pl.BlockSpec((ROWS, HALF), lambda j: (0, half), pipeline_mode=pl.Buffered(1)) for _ in sources]
        + specs
        + [block] * len(plus),
        out_specs=block,
        out_shape=jax.ShapeDtypeStruct((HALF, columns), BF16),
        scratch_shapes=[pltpu.VMEM((HALF, KEYS), BF16), pltpu.VMEM((HALF, ROWS - KEYS), F32)],
        compiler_params=pltpu.CompilerParams(vmem_limit_bytes=48 << 20),
        cost_estimate=cost_of(
            flops=ROWS * WIDTH * columns, bytes_accessed=3 * ROWS * columns, transcendentals=0
        ),
        name="weight_grads",
    )(*sources, *[g for g, _, _ in operands], *plus)


def pair_tables(coords):
    lane = jnp.arange(128)
    freqs = 10000.0 ** (-(lane % 16).astype(F32) / 16.0)
    along_rows = (lane % 64 < 32)[None, :]
    places = jnp.where(along_rows, coords[:, 0:1], coords[:, 1:2]).astype(F32)
    angles = jnp.pad(places * freqs[None, :], ((0, ROWS - KEYS), (0, 0)))
    cosines, sines = jnp.cos(angles), jnp.sin(angles)
    even = (lane % 32 < 16)[None, :]
    return cosines, jnp.where(even, -sines, 0.0), jnp.where(even, 0.0, sines)


def feature_order(me):
    natural = lax.broadcasted_iota(jnp.int32, (WIDTH, WIDTH), 0)
    place = lax.broadcasted_iota(jnp.int32, (WIDTH, WIDTH), 1)
    block = place // 32
    owner = (
        (block // 16) * BIT_CORE
        + (block // 8 % 2) * BIT_X
        + (block // 4 % 2) * BIT_Y
        + (block // 2 % 2) * BIT_Z1
        + (block % 2) * BIT_Z0
    ) ^ me
    return (natural == owner * 32 + place % 32).astype(BF16)


def paired_device(
    patch_in, cls_in, d_patch, d_cls, image_valid, patch_coords,
    w_query, w_key, w_value, w_gate, w_up, w_out, w_down, layer_vectors, ffn_vectors,
):
    SENT.clear()
    me, pos = lax.axis_index(BOTH), lax.axis_index("ctx")
    hidden = w_gate.shape[1]
    wide = (hidden + 255) // 256 * 256
    extra = ((0, 0), (0, wide - hidden))

    def own_image(patches, classes, *deps):
        near = lax.dynamic_index_in_dim(patches, pos, 0, keepdims=False)
        sent = after(lax.dynamic_index_in_dim(patches, 1 - pos, 0, keepdims=False), *deps)
        far = swap_over(sent, BIT_X)
        class_row = lax.dynamic_index_in_dim(classes, pos, 0)
        return joined(near, far, jnp.pad(class_row, ((0, ROWS - KEYS - 1), (0, 0)))), far

    def to_pair(rows, far):
        near = rows[:512]
        is_first = pos == 0
        near_class, far_class = rows[KEYS], far[512]
        patches = jnp.where(is_first, jnp.stack([near, far[:512]]), jnp.stack([far[:512], near]))
        classes = jnp.where(is_first, jnp.stack([near_class, far_class]), jnp.stack([far_class, near_class]))
        return patches, classes

    vectors_local = jnp.pad(layer_vectors.T, ((0, 0), (0, 120)))
    low_heads = [w[:, :HALF] for w in (w_query, w_key, w_value)]
    high_heads = [w[:, HALF:] for w in (w_query, w_key, w_value)]
    g_low = Gather(joined(*low_heads, vectors_local, axis=1))
    g_high = Gather(joined(*high_heads, w_out.T, axis=1))
    g_gate = Gather(jnp.pad(w_gate, extra))
    g_up = Gather(jnp.pad(w_up, extra))
    g_down = Gather(jnp.pad(w_down.T, extra))

    image_rows, image_far = own_image(patch_in, cls_in)
    coords = joined(patch_coords, swap_over(patch_coords, BIT_X))
    order = feature_order(me)
    tables = pair_tables(coords)
    keep = lax.dynamic_index_in_dim(image_valid, pos, 0, keepdims=False).astype(F32)
    keep = jnp.full((8, 128), keep, F32)
    ffn = jnp.pad(ffn_vectors.astype(F32), ((0, 4), (0, wide - hidden)))

    z_one = g_low.along_z0()
    z_low = g_low.along_z1()
    z_one = g_high.along_z0(z_one)
    z_one = g_gate.along_z0(z_one)
    xy_low = g_low.along_xy()
    z_high = g_high.along_z1(z_low)
    corner_low = g_low.corners(image_far)
    xy_high = g_high.along_xy(xy_low)
    near_low = g_low.whole(z_high, z_one)

    gate = near_low, g_low.far, image_rows, z_one, xy_high
    z_gate = g_gate.along_z1(gate)
    corner_high = g_high.corners(gate)
    vectors, head_biases = gathered_vectors(near_low, g_low.far, order)
    tokens, normed = over_rows(
        start_kernel, "start", [ready(image_rows, gate)], [order, vectors], [(WIDTH, BF16), (WIDTH, BF16)],
        flops=2_200_000_000,
    )

    def attend(block, gate):
        group = g_low if block < 2 else g_high
        return attention_forward(
            ready(normed, gate), group.near, group.far, head_biases, block, block % 2, tables
        )

    gate = normed, z_gate, corner_high
    z_up = g_up.along_z0(gate)
    near_high = g_high.whole(gate)
    xy_gate = g_gate.along_xy(gate)
    heads = [attend(0, gate)]

    gate = heads[0][3], xy_gate, z_up
    corner_gate = g_gate.corners(gate)
    z_up = g_up.along_z1(gate)
    heads.append(attend(1, gate))

    gate = heads[1][3], g_high.far, corner_gate, z_up
    near_gate = g_gate.whole(gate)
    xy_up = g_up.along_xy(gate)
    z_down = g_down.along_z0(gate)
    heads.append(attend(2, gate))

    gate = heads[2][3], xy_up, g_gate.far, z_down
    corner_up = g_up.corners(gate)
    z_down = g_down.along_z1(gate)
    heads.append(attend(3, gate))

    gate = heads[3][3], corner_up, z_down
    near_up = g_up.whole(gate)
    xy_down = g_down.along_xy(gate)
    out_w = [((w, (HALF, HALF), 3 + i)) for w in (near_high, g_high.far) for i in range(2)]
    attended = [h[3] for h in heads]
    middle, normed_two = over_rows(
        middle_kernel, "middle", attended + [ready(tokens, gate)], out_w + [vectors],
        [(WIDTH, BF16), (WIDTH, BF16)], flops=2_200_000_000, step=520,
    )

    gate = normed_two, g_up.far, xy_down
    corner_down = g_down.corners(gate)
    grad_image_rows, grad_far = own_image(d_patch, d_cls, gate)
    gate_up = [near_gate, g_gate.far, near_up, g_up.far]
    gate_act, up_act, inner, stats = over_rows(
        functools.partial(hidden_kernel, hidden=hidden), "hidden", [ready(normed_two, gate)],
        gate_up + [ffn], [(wide, BF16), (wide, BF16), (wide, BF16), (128, F32)], flops=12_000_000_000,
    )

    gate = inner, corner_down, grad_far
    near_down = g_down.whole(gate)
    down_w = [near_down, g_down.far]
    (out_rows,) = over_rows(
        result_kernel, "result", [inner, ready(middle, gate)], down_w + [vectors, order, keep],
        [(WIDTH, BF16)], flops=8_000_000_000, step=520,
    )

    gate = out_rows
    far_rows = swap_over(after(out_rows, gate)[HALF:], BIT_X)
    branch, d_gate, d_up, wide_sums, branch_sums = over_rows(
        functools.partial(hidden_back_kernel, hidden=hidden), "hidden_back",
        [ready(grad_image_rows, gate), gate_act, up_act, stats], [order, keep] + down_w + [ffn],
        [(WIDTH, BF16), (wide, BF16), (wide, BF16)], [wide, WIDTH], flops=8_000_000_000,
    )

    gate = wide_sums, far_rows
    outs = to_pair(after(out_rows, far_rows), far_rows)
    all_sums = lax.all_gather(wide_sums, BOTH)
    part_width = wide // 2
    down, second, low, high = Scatter(), Scatter(), Scatter(), Scatter()
    late = ready(normed_two, gate)
    second_steps = [(late, [(g, part_width, i)]) for g in (d_gate, d_up) for i in range(2)]
    second_far = weight_grads(1, second_steps)

    gate = second_far
    second_stage = second.over_core(second_far, gate)
    late = ready(branch, gate)
    down_steps = [(late, [(inner, part_width, i)]) for i in range(2)]
    down_far = weight_grads(1, down_steps)

    gate = down_far, second_stage
    down_stage = down.over_core(down_far, gate)
    late = ready(normed_two, gate)
    second_total = weight_grads(0, [(late, gs) for _, gs in second_steps], second_stage)

    gate = second_total, down_stage
    second_stage = second.corners(second_total, gate)
    late = ready(branch, gate)
    down_total = weight_grads(0, [(late, gs) for _, gs in down_steps], down_stage)

    gate = down_total, second_stage
    second_stage = second.sides(gate)
    att_low, *att_grads, middle_sums = over_rows(
        middle_back_kernel, "middle_back", [d_gate, d_up, branch, ready(middle, gate)],
        gate_up + out_w + [vectors], [(WIDTH, BF16)] + [(HEAD_COLS, BF16)] * 4, [WIDTH],
        flops=14_000_000_000, step=520,
    )

    def attend_back(block, gate):
        return attention_backward(*heads[block], ready(att_grads[block], gate), tables)

    gate = att_low, second_stage
    second_stage, down_stage = second.along_z1(gate), down.corners(down_total, gate)
    parts = [attend_back(0, gate)]

    gate = parts[0][0], second_stage, down_stage
    gate_up_grad, down_stage = second.along_z0(gate), down.sides(gate)
    parts.append(attend_back(1, gate))

    def pieces(*arrays):
        return [(a, HEAD_COLS, 0) for a in arrays]

    gate = parts[1][0], gate_up_grad, down_stage
    down_stage = down.along_z1(gate)
    late, late_two = ready((att_low, normed), gate)
    grads = [g for part in parts for g in part[:3]]
    low_steps = [(late, pieces(*attended[2 * i : 2 * i + 2])) for i in range(2)]
    low_steps += [(late_two, pieces(*grads[2 * i : 2 * i + 2])) for i in range(3)]
    low_far = weight_grads(1, low_steps)

    gate = low_far, down_stage
    low_stage, down_grad = low.over_core(low_far, gate), down.along_z0(gate)
    parts.append(attend_back(2, gate))

    gate = parts[2][0], low_stage, down_grad
    late, late_two = ready((att_low, normed), gate)
    low_total = weight_grads(
        0, [(late if i < 2 else late_two, gs) for i, (_, gs) in enumerate(low_steps)], low_stage
    )

    gate = low_total
    low_stage = low.corner(low_total, gate)
    parts.append(attend_back(3, gate))

    gate = parts[3][0], low_stage
    low_stage = low.sides(gate)
    late = ready(normed, gate)
    grads = [g for part in parts[2:] for g in part[:3]]
    high_steps = [(late, pieces(*grads[2 * i : 2 * i + 2])) for i in range(3)]
    high_far = weight_grads(1, high_steps)
    high_stage = high.over_core(high_far)

    def last_rows(gate, first, count):
        return over_rows(
            last_kernel, "last",
            [g for part in parts for g in part[:3]] + [ready(att_low, gate), tokens],
            [(near_low, (HALF, 3 * HALF), 0), (g_low.far, (HALF, 3 * HALF), 0)]
            + [(near_high, (HALF, 3 * HALF), 0), (g_high.far, (HALF, 3 * HALF), 0), vectors, order],
            [(WIDTH, BF16)], [WIDTH], flops=4_500_000_000, step=count, only=first,
        )

    far_part, far_sums = last_rows(high_far, HALF, ROWS - HALF)

    gate = far_part, high_stage, low_stage
    low_stage = low.along_z1(gate)
    late = ready(normed, gate)
    high_total = weight_grads(0, [(late, gs) for _, gs in high_steps], high_stage)

    gate = high_total
    high.total = high_total
    far_rows = swap_over(after(far_part, gate), BIT_X)
    high_stage = high.over_y(gate)
    near_part, near_sums = last_rows(gate, 0, HALF)

    gate = near_part, low_stage, high_stage, far_rows
    low_grad = low.along_z0(gate)
    high.over_x(gate)
    high.along_z1()
    high_grad = high.along_z0()
    sums = [far_sums, near_sums, middle_sums, branch_sums] + [part[3] for part in parts]
    far_sums, near_sums, middle_sums, branch_sums, *head_sums = after(sums, far_rows)
    patch_grad, cls_grad = to_pair(after(joined(near_part, far_part), far_rows), far_rows)
    ffn_grads = jnp.sum(after(all_sums, far_rows), axis=0)[:4, :hidden]
    head_sums = jnp.dot(
        joined(*[part[:2] for part in head_sums], axis=1), order.astype(F32), precision=lax.Precision.HIGHEST
    )
    vector_grads = scatter_small(
        joined((far_sums + near_sums)[:2], head_sums, middle_sums[:3], branch_sums[:1]).T
    )
    blocks = [low_grad[:, WIDTH + i * HEAD_COLS :][:, :HEAD_COLS] for i in range(6)]
    blocks += [high_grad[:, i * HEAD_COLS :][:, :HEAD_COLS] for i in range(6)]
    query_grad, key_grad, value_grad = (joined(*blocks[i::3], axis=1) for i in range(3))
    return (
        outs[0],
        outs[1],
        patch_grad,
        cls_grad,
        query_grad,
        key_grad,
        value_grad,
        gate_up_grad[:, :hidden],
        gate_up_grad[:, wide : wide + hidden],
        low_grad[:, :WIDTH].T,
        down_grad[:, :hidden].T,
        vector_grads.T,
        ffn_grads,
    )


def solution(mesh):
    in_specs = (
        P("dp", "ctx", None),
        P("dp", None),
        P("dp", "ctx", None),
        P("dp", None),
        P("dp"),
        P("ctx", None),
        P(("dp", "ctx"), None),
        P(("dp", "ctx"), None),
        P(("dp", "ctx"), None),
        P(("dp", "ctx"), None),
        P(("dp", "ctx"), None),
        P(None, ("dp", "ctx")),
        P(None, ("dp", "ctx")),
        P(None, ("dp", "ctx")),
        P(),
    )
    out_specs = (
        P("dp", "ctx", None),
        P("dp", None),
        P("dp", "ctx", None),
        P("dp", None),
        P(("dp", "ctx"), None),
        P(("dp", "ctx"), None),
        P(("dp", "ctx"), None),
        P(("dp", "ctx"), None),
        P(("dp", "ctx"), None),
        P(None, ("dp", "ctx")),
        P(None, ("dp", "ctx")),
        P(None, ("dp", "ctx")),
        P(),
    )
    sizes = dict(mesh.shape)
    pairs = sizes["dp"] == 16 and sizes["ctx"] == 2
    body = paired_device if pairs else on_device
    return jax.shard_map(
        body, mesh=mesh, in_specs=in_specs, out_specs=out_specs, check_vma=False
    )
```
